256 devices in a mesh: row: 8 (over y_lo, x), col: 32 (over z, y_hi, core).
Axes of the slice: x: 4, y: 4 (y_hi: 2, y_lo: 2; y = y_hi * 2 + y_lo), z: 8, core: 2. Of those that a mesh axis runs over, the one named last changes fastest.
Arguments:
- volume: bfloat16 [16, 32, 32, 4096], P(None, None, 'row', 'col'), may hold values from -6 to 6
- cotangent: bfloat16 [16, 32, 32, 4096], P(None, None, 'row', 'col'), may hold values from -6 to 6
- w_half: bfloat16 [32, 16, 3, 3, 3], replicated, may hold values from -0.3125 to 0.3125
- w_quarter: bfloat16 [64, 32, 3, 3, 3], replicated, may hold values from -0.21875 to 0.21875
- w_back_half: bfloat16 [32, 64, 3, 3, 3], replicated, may hold values from -0.4375 to 0.4375
- w_back_full: bfloat16 [16, 32, 3, 3, 3], replicated, may hold values from -0.625 to 0.625
Outputs:
- grad_volume: bfloat16 [16, 32, 32, 4096], P(None, None, 'row', 'col')
- grad_w_half: float32 [32, 16, 3, 3, 3], replicated
- grad_w_quarter: float32 [64, 32, 3, 3, 3], replicated
- grad_w_back_half: float32 [32, 64, 3, 3, 3], replicated
- grad_w_back_full: float32 [16, 32, 3, 3, 3], replicated
The draws below stay inside these ranges and needn't reach their ends.
All inputs are finite; a program needn't handle non-finite values.
Results may differ from the reference program's by a relative error of at most 0.013.
Values may be sent and summed in bfloat16 or wider, within the bound.
No kernel may reach another device: no remote copies, remote signals or barrier semaphores. Data moves between devices by JAX's collectives and lax.ppermute only.
A program may use at most 128 MiB of HBM per device.

```python
import math
import jax
import jax.numpy as jnp
from jax import lax

CF = 16
CH = 32
CQ = 64
DISP = 32
NROWS = 32
NCOLS = 4096
VOXELS = 4194304


def steps_of(rng, extent, split, least, top_value):
    loudness = 1.0
    for dim, blocks in split:
        heights = jax.random.uniform(jax.random.fold_in(jax.random.fold_in(rng, 6), dim), (blocks,), jnp.float32, least / len(split), top_value / len(split))
        loudness = loudness * jnp.repeat(jnp.exp(heights), extent[dim] // blocks).reshape((-1,) + (1,) * (len(extent) - 1 - dim))
    return loudness


def scatter_about(own_key, dims, deviation, bound, pieces=(), held_as=jnp.bfloat16):
    drawn = deviation * jax.random.normal(own_key, dims, jnp.float32)
    if pieces:
        drawn = drawn * steps_of(own_key, dims, pieces, -0.22, 0.18)
    return jnp.clip(drawn, -bound, bound).astype(held_as)


def setup_inputs(seed: int = 0) -> dict:
    key_of = jax.random.split(jax.random.key(seed), 7)
    volume = scatter_about(key_of[0], (CF, DISP, NROWS, NCOLS), 1.0, 6.0, ((2, 8), (3, 32)))
    cotangent = scatter_about(key_of[1], (CF, DISP, NROWS, NCOLS), 1.0, 6.0, ((2, 8), (3, 32)))
    w_half = scatter_about(key_of[2], (CH, CF, 3, 3, 3), (CF * 27) ** -0.5, 0.3125)
    w_quarter = scatter_about(key_of[3], (CQ, CH, 3, 3, 3), (CH * 27) ** -0.5, 0.21875)
    w_back_half = scatter_about(key_of[4], (CH, CQ, 3, 3, 3), (CQ * 27 // 8) ** -0.5, 0.4375)
    w_back_full = scatter_about(key_of[5], (CF, CH, 3, 3, 3), (CH * 27 // 8) ** -0.5, 0.625)
    return {"volume": volume, "cotangent": cotangent, "w_half": w_half, "w_quarter": w_quarter, "w_back_half": w_back_half, "w_back_full": w_back_full}


NUMBERS = ('NCDHW', 'OIDHW', 'NCDHW')

def down(extended, weight):
    result = lax.conv_general_dilated(extended[None], weight, (2, 2, 2), ((1, 1), (0, 0), (0, 0)), dimension_numbers=NUMBERS, preferred_element_type=jnp.float32)
    return result[0]

def upsample(extended, weight):
    result = lax.conv_general_dilated(extended[None], weight, (1, 1, 1), ((1, 2), (1, 0), (1, 0)), lhs_dilation=(2, 2, 2), dimension_numbers=NUMBERS, preferred_element_type=jnp.float32)
    return result[0]

def flipped(weight):
    return jnp.flip(weight, axis=(2, 3, 4)).transpose(1, 0, 2, 3, 4)

def silu_slope(pre):
    sigma = jax.nn.sigmoid(pre)
    return sigma * (1.0 + pre * (1.0 - sigma))

def down_wgrad(extended, grad_out):
    depth, height, width = (grad_out.shape[1], grad_out.shape[2], grad_out.shape[3])
    padded = jnp.pad(extended, ((0, 0), (1, 0), (0, 0), (0, 0)))
    terms = []
    for depth_tap in range(3):
        for row_tap in range(3):
            for col_tap in range(3):
                piece = lax.slice(padded, (0, depth_tap, row_tap, col_tap), (padded.shape[0], depth_tap + 2 * depth - 1, row_tap + 2 * height - 1, col_tap + 2 * width - 1), (1, 2, 2, 2))
                terms.append(jnp.einsum('odhw,idhw->oi', grad_out, piece, preferred_element_type=jnp.float32))
    stacked = jnp.stack(terms, axis=-1)
    return stacked.reshape(stacked.shape[0], stacked.shape[1], 3, 3, 3)

def up_wgrad(source, grad_ext):
    depth, height, width = (source.shape[1], source.shape[2], source.shape[3])
    padded = jnp.pad(grad_ext, ((0, 0), (1, 0), (0, 0), (0, 0)))
    terms = []
    for depth_tap in range(3):
        for row_tap in range(3):
            for col_tap in range(3):
                start = (0, 2 - depth_tap, 2 - row_tap, 2 - col_tap)
                limit = (padded.shape[0], start[1] + 2 * depth - 1, start[2] + 2 * height - 1, start[3] + 2 * width - 1)
                piece = lax.slice(padded, start, limit, (1, 2, 2, 2))
                terms.append(jnp.einsum('idhw,odhw->oi', source, piece, preferred_element_type=jnp.float32))
    stacked = jnp.stack(terms, axis=-1)
    return stacked.reshape(stacked.shape[0], stacked.shape[1], 3, 3, 3)

def lower_pad(field):
    return jnp.pad(field, ((0, 0), (0, 0), (1, 0), (1, 0)))

def upper_pad(field):
    return jnp.pad(field, ((0, 0), (0, 0), (0, 1), (0, 1)))

def reference(volume, cotangent, w_half, w_quarter, w_back_half, w_back_full):
    scale = 1.0 / math.sqrt(VOXELS)
    volume_ext = lower_pad(volume)
    pre_h = down(volume_ext, w_half)
    half_act = jax.nn.silu(pre_h).astype(jnp.bfloat16)
    half_ext = lower_pad(half_act)
    pre_q = down(half_ext, w_quarter)
    quarter_act = jax.nn.silu(pre_q).astype(jnp.bfloat16)
    pre_m = upsample(upper_pad(quarter_act), w_back_half) + half_act.astype(jnp.float32)
    mixed_act = jax.nn.silu(pre_m).astype(jnp.bfloat16)
    cot_ext = lower_pad(cotangent)
    grad_mixed = (down(cot_ext, flipped(w_back_full)) * silu_slope(pre_m)).astype(jnp.bfloat16)
    grad_w4 = up_wgrad(mixed_act, cot_ext) * scale
    mixed_ext = lower_pad(grad_mixed)
    grad_quarter = (down(mixed_ext, flipped(w_back_half)) * silu_slope(pre_q)).astype(jnp.bfloat16)
    grad_w3 = up_wgrad(quarter_act, mixed_ext) * scale
    summed = upsample(upper_pad(grad_quarter), flipped(w_quarter)) + grad_mixed.astype(jnp.float32)
    grad_half = (summed * silu_slope(pre_h)).astype(jnp.bfloat16)
    grad_w2 = down_wgrad(half_ext, grad_quarter) * scale
    grad_volume = (upsample(upper_pad(grad_half), flipped(w_half)) + cotangent.astype(jnp.float32)).astype(jnp.bfloat16)
    grad_w1 = down_wgrad(volume_ext, grad_half) * scale
    return (grad_volume, grad_w1, grad_w2, grad_w3, grad_w4)
```

```python
import functools
import math

import jax
import jax.numpy as jnp
import numpy as np
from jax import lax
from jax.experimental import pallas as pl
from jax.experimental.pallas import tpu as pltpu
from jax.sharding import PartitionSpec as P

BF = jnp.bfloat16
F32 = jnp.float32

QD, QC, HALO = 8, 32, 2
SPAN = QC + 2 * HALO
LANES = 384
PACK = 1152
LIMIT = 24 * 1024 * 1024


def lane_of(d, c):
    return SPAN * d + c + HALO


def constants():
    spread = np.zeros((QD * 128, 4 * 256), np.float32)
    rims = np.zeros((4 * LANES, 128), np.float32)
    place = np.zeros((2, 256, 4 * LANES), np.float32)
    for d in range(QD):
        for phase in range(4):
            for c in range(QC):
                spread[d * 128 + 4 * c + phase, phase * 256 + lane_of(d, c) - (0 if d < 6 else 128)] = 1
            for e in range(2):
                for side in range(2):
                    slot = phase * 16 + d * 2 + e
                    column = e if side == 0 else QC - 2 + e
                    rims[phase * LANES + lane_of(d, column), side * 64 + slot] = 1
                    outside = e - 2 if side == 0 else QC + e
                    for half in range(2):
                        place[half, side * 128 + half * 64 + slot, phase * LANES + lane_of(d, outside)] = 1
    order = np.zeros((256, 256), np.float32)
    for ch in range(16):
        for pd in range(4):
            for r in range(4):
                order[r * 64 + pd * 16 + ch, ch * 16 + pd * 4 + r] = 1
    return [np.asarray(a, BF) for a in (spread, rims, place, order)]


def dot(a, b):
    return lax.dot_general(a, b, (((1,), (0,)), ((), ())), preferred_element_type=F32)


def dot_nt(a, b):
    return lax.dot_general(a, b, (((1,), (1,)), ((), ())), preferred_element_type=F32)


def sigmoid(t):
    return 1.0 / (1.0 + jnp.exp(-t))


def slope(t):
    s = sigmoid(t)
    return s * (1.0 + t * (1.0 - s))


def relayout(x_ref, spread_ref, order_ref):
    wide = jnp.concatenate([x_ref[:, d].reshape(256, 128) for d in range(QD)], axis=1)
    rows = dot(order_ref[...], wide).astype(BF)
    early = dot(rows[:, :768], spread_ref[0:768])
    late = dot(rows[:, 768:], spread_ref[768:1024])
    pieces = []
    for pc in range(4):
        low, high = pc * 256, pc * 256 + 128
        pieces += [early[:, low:high], early[:, high : low + 256] + late[:, low:high], late[:, high : low + 256]]
    return jnp.concatenate(pieces, axis=1).astype(BF)


def own_kernel(vol_ref, cot_ref, spread_ref, order_ref, yv_ref, yc_ref, last_ref):
    yv_ref[...] = relayout(vol_ref, spread_ref, order_ref)
    yc_ref[...] = relayout(cot_ref, spread_ref, order_ref)
    last_ref[...] = yc_ref[192:256]


def parity(axis):
    return lax.axis_index(axis) & 1


def flag(condition):
    return jnp.where(condition, 1.0, 0.0).astype(F32)


def rows_kernel(xa_ref, xb_ref, yv_ref, yc_ref, ycrow_ref, spread_ref, order_ref, rims_ref, near_ref, yclo_ref, senda_ref, sendb_ref, edge_ref):
    odd = parity("row")
    near_ref[1 - odd] = relayout(xa_ref, spread_ref, order_ref)
    near_ref[odd] = relayout(xb_ref, spread_ref, order_ref)
    inner = flag(lax.axis_index("row") > 0)
    near_ref[0] = (near_ref[0].astype(F32) * inner).astype(BF)
    yclo_ref[...] = (ycrow_ref[...].astype(F32) * inner).astype(BF)
    rims = rims_ref[...]
    top = jnp.concatenate([dot(near_ref[0, 64:256], rims), dot(yv_ref[...], rims), dot(near_ref[1, 0:64], rims)], axis=0)
    bottom = jnp.concatenate([dot(near_ref[1, 64:256], rims), dot(yclo_ref[...], rims), dot(yc_ref[...], rims)], axis=0)
    edge_ref[0] = jnp.concatenate([top[:, :64], bottom[:, :64]], axis=1).astype(BF)
    edge_ref[1] = jnp.concatenate([top[:, 64:], bottom[:, 64:]], axis=1).astype(BF)
    odd = parity("col")
    senda_ref[...] = edge_ref[1 - odd]
    sendb_ref[...] = edge_ref[odd]


UP_TAP = {(0, 0): 1, (1, 0): 0, (1, 1): 2}
PAIRS = [(a, b, c) for a in range(2) for b in range(2) for c in range(2)]


def write_masks(mask_ref):
    lane = lax.broadcasted_iota(jnp.int32, (1, LANES), 1)
    c = lane
    for d in range(1, QD):
        c = jnp.where(lane >= d * SPAN, lane - d * SPAN, c)
    c = c - HALO
    inside = lane < QD * SPAN
    last_col = lax.axis_index("col") == lax.axis_size("col") - 1
    last_row = lax.axis_index("row") == lax.axis_size("row") - 1
    bound = jnp.where(last_col, QC, LANES)
    seen = jnp.where(inside & (c < bound), 1.0, 0.0).astype(F32)
    mask_ref[...] = jnp.zeros(mask_ref.shape, F32)
    mask_ref[0:1] = seen
    mask_ref[1:2] = seen * jnp.where(last_row, 0.0, 1.0)
    mask_ref[2:3] = jnp.where(inside & (c >= 0) & (c < QC), 1.0, 0.0).astype(F32)


def prepare_kernel(wh_ref, wq_ref, wbh_ref, wbf_ref, w1_ref, w2_ref, w3_ref, w4_ref, up1_ref, up2_ref, up3_ref, mask_ref):
    write_masks(mask_ref)
    for ref, out, eye, back in ((wh_ref, w1_ref, 32, False), (wq_ref, w2_ref, 64, False), (wbh_ref, w3_ref, 64, True), (wbf_ref, w4_ref, 32, True)):
        small, large = ref.shape[1], ref.shape[2]
        if back:
            flat = jnp.concatenate([ref[26 - k] for k in range(27)], axis=0)
        else:
            flat = ref[...].reshape(27 * small, large)
        rows = lax.broadcasted_iota(jnp.int32, (eye, eye), 0)
        cols = lax.broadcasted_iota(jnp.int32, (eye, eye), 1)
        unit = jnp.where(rows == cols, 1.0, 0.0).astype(BF)
        out[...] = dot_nt(unit, flat).astype(BF)
    for ref, out, back in ((wh_ref, up1_ref, True), (wq_ref, up2_ref, True), (wbh_ref, up3_ref, False)):
        small, large = ref.shape[1], ref.shape[2]
        out[...] = jnp.zeros(out.shape, BF)
        for p, (pr, pd, pc) in enumerate(PAIRS):
            for n, (nr, nd, nc) in enumerate(PAIRS):
                taps = [UP_TAP.get(key) for key in ((pd, nd), (pr, nr), (pc, nc))]
                if None in taps:
                    continue
                j = taps[0] * 9 + taps[1] * 3 + taps[2]
                out[p * small : (p + 1) * small, n * large : (n + 1) * large] = ref[26 - j if back else j]


def roll_up(x, steps):
    return pltpu.roll(x, steps % LANES, x.ndim - 1)


def fill_full(win_ref, y, base, count):
    pieces = [y[:, pc * LANES : (pc + 1) * LANES] for pc in range(4)]
    pieces = [roll_up(pieces[3], 1)] + pieces
    for c in range(5):
        piece = pieces[c].reshape(count, 4, 16, LANES)
        for pd in range(4):
            win_ref[1 + pd, base : base + count, c] = piece[:, pd].astype(BF)
        last = piece[:, 3].reshape(count * 16, LANES)
        win_ref[0, base : base + count, c] = roll_up(last, SPAN).reshape(count, 16, LANES).astype(BF)


def put_half(win_ref, row, pd, pc, value):
    win_ref[1 + pd, row, 1 + pc] = value.astype(BF)
    if pc == 1:
        left = roll_up(value, 1)
        win_ref[1 + pd, row, 0] = left.astype(BF)
    if pd == 1:
        above = roll_up(value, SPAN)
        win_ref[0, row, 1 + pc] = above.astype(BF)
        if pc == 1:
            win_ref[0, row, 0] = roll_up(left, SPAN).astype(BF)


def rounded(value):
    return value.astype(BF).astype(F32)


def neighbours(low, high):
    parts = []
    for value in (low, high):
        for nd in range(2):
            moved = roll_up(value, -SPAN) if nd else value
            parts.append(moved.astype(BF))
            parts.append(roll_up(moved, -1).astype(BF))
    return jnp.concatenate(parts, axis=0)


def forward_kernel(near_ref, yv_ref, yc_ref, yclo_ref, gota_ref, gotb_ref, mask_ref, place_ref, w1_ref, w2_ref, up3_ref, w4_ref, all_ref, cwin_ref, hwin_ref, preh_ref, preq_ref, q_ref, m_ref, gm_ref):
    seen = mask_ref[0:1]
    seen_next = mask_ref[1:2]
    own = mask_ref[2:3]
    odd = parity("col") == 1
    gota, gotb = gota_ref[...].astype(F32), gotb_ref[...].astype(F32)
    left = jnp.where(odd, gota, gotb) * flag(lax.axis_index("col") > 0)
    rims = jnp.concatenate([left, jnp.where(odd, gotb, gota)], axis=1).astype(BF)
    top, bottom = place_ref[0], place_ref[1]
    fill_full(all_ref, near_ref[0, 64:256].astype(F32) + dot(rims[0:192], top), 0, 3)
    fill_full(all_ref, yv_ref[...].astype(F32) + dot(rims[192:448], top), 3, 4)
    outside = jnp.concatenate([dot(rims[448:512], top), dot(rims[0:192], bottom)], axis=0)
    fill_full(all_ref, near_ref[1].astype(F32) + outside, 7, 4)
    w1 = w1_ref[...]
    for hr in range(5):
        for pd in range(2):
            for pc in range(2):
                col = all_ref[2 * pd : 2 * pd + 3, 2 * hr : 2 * hr + 3, 2 * pc : 2 * pc + 3].reshape(432, LANES)
                pre = dot(w1, col)
                if 1 <= hr <= 3:
                    preh_ref[hr - 1, pd, pc] = pre
                h = rounded(pre * sigmoid(pre)) * (seen if hr < 3 else seen_next)
                put_half(hwin_ref, hr, pd, pc, h)
    quarters = []
    for qr in range(2):
        col = hwin_ref[:, 2 * qr : 2 * qr + 3].reshape(864, LANES)
        pre = dot(w2_ref[...], col)
        preq_ref[qr] = pre
        quarters.append(rounded(pre * sigmoid(pre)) * (seen_next if qr else seen))
    q_ref[...] = (quarters[0] * own).astype(BF)
    up = dot(up3_ref[...], neighbours(quarters[0], quarters[1]))
    fill_full(cwin_ref, yclo_ref[...].astype(F32) + dot(rims[192:256], bottom), 0, 1)
    fill_full(cwin_ref, yc_ref[...].astype(F32) + dot(rims[256:512], bottom), 1, 4)
    w4 = w4_ref[...]
    for p, (pr, pd, pc) in enumerate(PAIRS):
        h = hwin_ref[1 + pd, 1 + pr, 1 + pc].astype(F32)
        pre = up[p * 32 : p * 32 + 32] + h
        m_ref[p] = (rounded(pre * sigmoid(pre)) * own).astype(BF)
        col = cwin_ref[2 * pd : 2 * pd + 3, 2 * pr : 2 * pr + 3, 2 * pc : 2 * pc + 3].reshape(432, LANES)
        gm = rounded(dot(w4, col) * slope(pre)) * seen
        gm_ref[pr, pd, pc] = gm.astype(BF)


def full_grad_kernel(cwin_ref, m_ref, out_ref):
    total = None
    for p, (pr, pd, pc) in enumerate(PAIRS):
        col = cwin_ref[2 * pd : 2 * pd + 3, 2 * pr : 2 * pr + 3, 2 * pc : 2 * pc + 3].reshape(432, LANES)
        part = dot_nt(col, m_ref[p])
        total = part if total is None else total + part
    store_groups(out_ref, total, 0, 112, 32)


def store_groups(out_ref, total, base, rows, width):
    size = total.shape[0]
    for group in range(128 // width):
        low, high = group * rows, min((group + 1) * rows, size)
        out_ref[base : base + high - low, group * width : (group + 1) * width] = total[low:high]
        if high - low < rows:
            out_ref[base + high - low : base + rows, group * width : (group + 1) * width] = jnp.zeros((rows - high + low, width), F32)


def backward_kernel(stage, gm_ref, gota_ref, gotb_ref, vwin_ref, hwin_ref, preh_ref, preq_ref, q_ref, g4_ref, mask_ref, w3_ref, up2_ref, ewin_ref, pack_ref, send_ref, mwin_ref):
    seen = mask_ref[0:1]
    seen_next = mask_ref[1:2]
    own = mask_ref[2:3]
    odd = parity("row") == 1
    inner = flag(lax.axis_index("row") > 0)
    for pd in range(2):
        for pc in range(2):
            last = [ref[1, pd, pc].astype(F32) for ref in (gota_ref, gotb_ref)]
            put_half(mwin_ref, 0, pd, pc, jnp.where(odd, last[0], last[1]) * inner)
            put_half(mwin_ref, 4, pd, pc, jnp.where(odd, last[1], last[0]))
            put_half(mwin_ref, 3, pd, pc, jnp.where(odd, gotb_ref[0, pd, pc].astype(F32), gota_ref[0, pd, pc].astype(F32)))
            for pr in range(2):
                put_half(mwin_ref, 1 + pr, pd, pc, gm_ref[pr, pd, pc].astype(F32))
    quarters = []
    for qr in range(2):
        col = mwin_ref[:, 2 * qr : 2 * qr + 3].reshape(864, LANES)
        gq = rounded(dot(w3_ref[...], col) * slope(preq_ref[qr])) * (seen_next if qr else seen)
        quarters.append(gq)
        if qr == 0:
            store_groups(pack_ref, dot_nt(col, q_ref[...]), 672, 448, 64)
    up = dot(up2_ref[...], neighbours(quarters[0], quarters[1]))
    up_next = dot(up2_ref[0:128, 0:256], neighbours(quarters[1], quarters[1])[0:256])
    total = None
    for p, (pr, pd, pc) in enumerate(PAIRS + [(2, 0, 0), (2, 0, 1), (2, 1, 0), (2, 1, 1)]):
        conv = up[p * 32 : p * 32 + 32] if pr < 2 else up_next[(p - 8) * 32 : (p - 8) * 32 + 32]
        gm = mwin_ref[1 + pd, 1 + pr, 1 + pc].astype(F32)
        gh = rounded((conv + gm) * slope(preh_ref[pr, pd, pc])) * (seen if pr < 2 else seen_next)
        ewin_ref[pd, pr, pc] = gh.astype(BF)
        if pc == 0:
            right = roll_up(gh, -1)
            ewin_ref[pd, pr, 2] = right.astype(BF)
        if pd == 0:
            below = roll_up(gh, -SPAN)
            ewin_ref[2, pr, pc] = below.astype(BF)
            if pc == 0:
                ewin_ref[2, pr, 2] = roll_up(right, -SPAN).astype(BF)
        if pr < 2:
            col = vwin_ref[2 * pd : 2 * pd + 3, 2 * pr + 2 : 2 * pr + 5, 2 * pc : 2 * pc + 3].reshape(432, LANES)
            part = dot_nt(col, (gh * own).astype(BF))
            total = part if total is None else total + part
    store_groups(pack_ref, total, 0, 112, 32)
    pack_ref[112:224] = g4_ref[...]
    col = hwin_ref[:, 0:3].reshape(864, LANES)
    store_groups(pack_ref, dot_nt(col, (quarters[0] * own).astype(BF)), 224, 448, 64)
    pack_ref[1120:PACK] = jnp.zeros((PACK - 1120, 128), F32)
    send_ref[...] = half(pack_ref, stage, False)[...].astype(BF)


def volume_kernel(ewin_ref, cwin_ref, up1_ref, spread_ref, order_ref, out_ref, z_ref):
    up1 = up1_ref[...]
    for pr, pd, pc in PAIRS:
        near = jnp.concatenate(
            [ewin_ref[pd + nd, pr + nr, pc + nc] for nr, nd, nc in PAIRS], axis=0
        )
        up = dot(up1, near)
        for f, (fr, fd, fc) in enumerate(PAIRS):
            r, d, c = 2 * pr + fr, 2 * pd + fd, 2 * pc + fc
            value = up[f * 16 : f * 16 + 16] + cwin_ref[1 + d, 1 + r, 1 + c].astype(F32)
            z_ref[r * 64 + d * 16 : r * 64 + d * 16 + 16, c * LANES : (c + 1) * LANES] = value.astype(BF)
    early = jnp.concatenate([z_ref[:, c * LANES : c * LANES + 256] for c in range(4)], axis=1)
    late = jnp.concatenate([z_ref[:, c * LANES + 128 : (c + 1) * LANES] for c in range(4)], axis=1)
    wide = jnp.concatenate([dot_nt(early, spread_ref[0:768]), dot_nt(late, spread_ref[768:1024])], axis=1).astype(BF)
    wide = lax.dot_general(order_ref[...], wide, (((0,), (0,)), ((), ())), preferred_element_type=F32).astype(BF)
    for d in range(QD):
        out_ref[:, d] = wide[:, d * 128 : (d + 1) * 128].reshape(16, 16, 128)


def side_of(axis, step):
    return jnp.where((lax.axis_index(axis) & step) != 0, 1, 0)


def half(ref, stage, mine):
    count = ref.shape[0] // 2
    side = side_of(*stage)
    return ref.at[pl.ds(pl.multiple_of((side if mine else 1 - side) * count, 16), count)]


def quarter_of(ref, parts, other):
    count = ref.shape[0] // parts
    place = (lax.axis_index("row") & (parts - 1)) ^ other
    return ref.at[pl.ds(pl.multiple_of(place * count, 16), count)]


def fold_kernel(stage, parts, kept_ref, got_ref, own_ref, *send_refs):
    total_ref = send_refs[-1]
    total_ref[...] = half(kept_ref, stage, True)[...] + got_ref[...].astype(F32)
    own_ref[...] = quarter_of(total_ref, parts, 0)[...]
    for other in range(1, parts):
        send_refs[other - 1][...] = quarter_of(total_ref, parts, other)[...].astype(BF)


def unfold_kernel(parts, *refs):
    out_ref = refs[-1]
    for other in range(parts):
        quarter_of(out_ref, parts, other)[...] = refs[other][...]


def finish_kernel(scale, stage, own_ref, got_ref, g1_ref, g2_ref, g3_ref, g4_ref, full_ref):
    half(full_ref, stage, True)[...] = own_ref[...].astype(F32)
    half(full_ref, stage, False)[...] = got_ref[...].astype(F32)
    for ref, base, rows, width in ((g1_ref, 0, 112, 32), (g4_ref, 112, 112, 32), (g2_ref, 224, 448, 64), (g3_ref, 672, 448, 64)):
        small = ref.shape[1]
        taps = rows // small
        back = ref is g3_ref or ref is g4_ref
        for group in range(128 // width):
            count = min(taps, 27 - group * taps)
            block = full_ref[base : base + count * small, group * width : (group + 1) * width] * scale
            block = block.reshape(count, small, width)
            if back:
                for t in range(count):
                    ref[26 - group * taps - t] = block[t]
            else:
                ref[group * taps : group * taps + count] = block


def call(kernel, outs, scratch=(), flops=0, name=None):
    shapes = [jax.ShapeDtypeStruct(shape, dtype) for shape, dtype in outs]
    return pl.pallas_call(
        kernel,
        out_shape=shapes,
        scratch_shapes=list(scratch),
        compiler_params=pltpu.CompilerParams(vmem_limit_bytes=LIMIT),
        cost_estimate=pl.CostEstimate(flops=flops, bytes_accessed=4000000, transcendentals=0),
        name=name,
    )


def swapped(value, row_step, col_step):
    rows, cols = lax.axis_size("row"), lax.axis_size("col")
    pairs = [(r * cols + c, (r ^ row_step) * cols + (c ^ col_step)) for r in range(rows) for c in range(cols)]
    return lax.ppermute(value, ("row", "col"), pairs)


def paired(value, axis, first):
    count = lax.axis_size(axis)
    pairs = []
    for low in range(first, count + first, 2):
        high = (low + 1) % count
        pairs += [(low, high), (high, low)]
    return lax.ppermute(value, axis, pairs)


def tree_sum(terms):
    terms = [term.astype(F32) for term in terms]
    while len(terms) > 1:
        terms = [low + high for low, high in zip(terms[::2], terms[1::2])]
    return terms[0]


def by_tap(weight, swap):
    order = (2, 3, 4, 1, 0) if swap else (2, 3, 4, 0, 1)
    moved = weight.transpose(order)
    return moved.reshape((27,) + moved.shape[3:])


def from_tap(grad, swap):
    cube = grad.reshape((3, 3, 3) + grad.shape[1:])
    return cube.transpose((4, 3, 0, 1, 2) if swap else (3, 4, 0, 1, 2))


def shards(volume, cotangent, w_half, w_quarter, w_back_half, w_back_full):
    rows, cols = lax.axis_size("row"), lax.axis_size("col")
    cells = volume.size // volume.shape[0] * rows * cols
    scale = 1.0 / math.sqrt(cells)
    spread, rims, place, order = [jnp.asarray(a) for a in constants()]
    vol = volume.reshape(16, QD, 16, 128)
    cot = cotangent.reshape(16, QD, 16, 128)
    vol_a, vol_b = paired(vol, "row", 0), paired(vol, "row", 1)
    yv, yc, cot_last = call(
        own_kernel,
        [((256, 4 * LANES), BF), ((256, 4 * LANES), BF), ((64, 4 * LANES), BF)],
        name="own",
    )(vol, cot, spread, order)
    cot_row = lax.ppermute(cot_last, "row", [(i, (i + 1) % rows) for i in range(rows)])
    w1, w2, w3, w4, up1, up2, up3, mask = call(
        prepare_kernel,
        [((32, 432), BF), ((64, 864), BF), ((64, 864), BF), ((32, 432), BF), ((128, 256), BF), ((256, 512), BF), ((256, 512), BF), ((8, LANES), F32)],
        name="prepare",
    )(by_tap(w_half, True), by_tap(w_quarter, True), by_tap(w_back_half, False), by_tap(w_back_full, False))
    near, cot_lo, send_a, send_b = call(
        rows_kernel,
        [((2, 256, 4 * LANES), BF), ((64, 4 * LANES), BF), ((512, 128), BF), ((512, 128), BF)],
        [pltpu.VMEM((2, 512, 128), BF)],
        name="rows",
    )(vol_a, vol_b, yv, yc, cot_row, spread, order, rims)
    rim_a, rim_b = paired(send_a, "col", 0), paired(send_b, "col", 1)
    vwin, cwin, hwin, preh, preq, quarter, mixed, gm = call(
        forward_kernel,
        [
            ((5, 11, 5, 16, LANES), BF),
            ((5, 5, 5, 16, LANES), BF),
            ((3, 5, 3, 32, LANES), BF),
            ((3, 2, 2, 32, LANES), F32),
            ((2, 64, LANES), F32),
            ((64, LANES), BF),
            ((8, 32, LANES), BF),
            ((2, 2, 2, 32, LANES), BF),
        ],
        name="forward",
    )(near, yv, yc, cot_lo, rim_a, rim_b, mask, place, w1, w2, up3, w4)
    gm_a, gm_b = paired(gm, "row", 0), paired(gm, "row", 1)
    (g4,) = call(full_grad_kernel, [((112, 128), F32)], flops=2 * 432 * 32 * LANES * 64, name="full_grad")(cwin, mixed)
    core = ("col", 1)
    parts = min(4, rows)
    ewin, kept, send = call(
        functools.partial(backward_kernel, core),
        [((3, 3, 3, 32, LANES), BF), ((PACK, 128), F32), ((PACK // 2, 128), BF)],
        [pltpu.VMEM((3, 5, 3, 32, LANES), BF)],
        name="backward",
    )(gm, gm_a, gm_b, vwin, hwin, preh, preq, quarter, g4, mask, w3, up2)
    share = PACK // 2 // parts
    kept, *sends = call(
        functools.partial(fold_kernel, core, parts),
        [((share, 128), F32)] + [((share, 128), BF)] * (parts - 1),
        [pltpu.VMEM((PACK // 2, 128), F32)],
        name="fold",
    )(kept, swapped(send, 0, 1))
    part = tree_sum([kept] + [swapped(send, other + 1, 0) for other, send in enumerate(sends)]).astype(BF)
    for group in ([("row", 4), ("col", 2)], [("col", 4), ("col", 8), ("col", 16)]):
        group = [(axis, step) for axis, step in group if step < lax.axis_size(axis)]
        terms = [part]
        for index in range(1, 2 ** len(group)):
            chosen = [stage for bit, stage in enumerate(group) if index >> bit & 1]
            moves = [sum(step for axis, step in chosen if axis == name) for name in ("row", "col")]
            terms.append(swapped(part, *moves))
        part = tree_sum(terms).astype(BF)
    (part,) = call(functools.partial(unfold_kernel, parts), [((PACK // 2, 128), BF)], name="unfold")(
        part, *[swapped(part, other, 0) for other in range(1, parts)]
    )
    (grad_volume,) = call(
        volume_kernel, [((16, QD, 16, 128), BF)], [pltpu.VMEM((256, 4 * LANES), BF)], flops=2 * 256 * 1024 * 4000, name="volume"
    )(ewin, cwin, up1, spread, order)
    g1, g2, g3, g4 = call(
        functools.partial(finish_kernel, scale, core),
        [((27, 16, 32), F32), ((27, 32, 64), F32), ((27, 32, 64), F32), ((27, 16, 32), F32)],
        [pltpu.VMEM((PACK, 128), F32)],
        name="finish",
    )(part, swapped(part, 0, 1))
    return (
        grad_volume.reshape(volume.shape),
        from_tap(g1, True),
        from_tap(g2, True),
        from_tap(g3, False),
        from_tap(g4, False),
    )


def solution(mesh):
    return jax.shard_map(
        shards,
        mesh=mesh,
        in_specs=(P(None, None, "row", "col"), P(None, None, "row", "col"), P(), P(), P(), P()),
        out_specs=(P(None, None, "row", "col"), P(), P(), P(), P()),
        check_vma=False,
    )
```

```python
import functools
import math

import jax
import jax.numpy as jnp
import numpy as np
from jax import lax
from jax.experimental import pallas as pl
from jax.experimental.pallas import tpu as pltpu
from jax.sharding import PartitionSpec as P

BF = jnp.bfloat16
F32 = jnp.float32

QD, QC, HALO = 8, 32, 2
SPAN = QC + 2 * HALO
LANES = 384
PACK = 1152
LIMIT = 24 * 1024 * 1024


def lane_of(d, c):
    return SPAN * d + c + HALO


def constants():
    spread = np.zeros((QD * 128, 4 * 256), np.float32)
    rims = np.zeros((4 * LANES, 128), np.float32)
    place = np.zeros((2, 256, 4 * LANES), np.float32)
    for d in range(QD):
        for phase in range(4):
            for c in range(QC):
                spread[d * 128 + 4 * c + phase, phase * 256 + lane_of(d, c) - (0 if d < 6 else 128)] = 1
            for e in range(2):
                for side in range(2):
                    slot = phase * 16 + d * 2 + e
                    column = e if side == 0 else QC - 2 + e
                    rims[phase * LANES + lane_of(d, column), side * 64 + slot] = 1
                    outside = e - 2 if side == 0 else QC + e
                    for half in range(2):
                        place[half, side * 128 + half * 64 + slot, phase * LANES + lane_of(d, outside)] = 1
    order = np.zeros((256, 256), np.float32)
    for ch in range(16):
        for pd in range(4):
            for r in range(4):
                order[r * 64 + pd * 16 + ch, ch * 16 + pd * 4 + r] = 1
    return [np.asarray(a, BF) for a in (spread, rims, place, order)]


def dot(a, b):
    return lax.dot_general(a, b, (((1,), (0,)), ((), ())), preferred_element_type=F32)


def dot_nt(a, b):
    return lax.dot_general(a, b, (((1,), (1,)), ((), ())), preferred_element_type=F32)


def sigmoid(t):
    return 1.0 / (1.0 + jnp.exp(-t))


def slope(t):
    s = sigmoid(t)
    return s * (1.0 + t * (1.0 - s))


def by_rows(x_ref, order_ref):
    wide = jnp.concatenate([x_ref[:, d].reshape(256, 128) for d in range(QD)], axis=1)
    return dot(order_ref[...], wide).astype(BF)


def to_lanes(rows, spread_ref):
    early = dot(rows[:, :768], spread_ref[0:768])
    late = dot(rows[:, 768:], spread_ref[768:1024])
    pieces = []
    for pc in range(4):
        low, high = pc * 256, pc * 256 + 128
        pieces += [early[:, low:high], early[:, high : low + 256] + late[:, low:high], late[:, high : low + 256]]
    return jnp.concatenate(pieces, axis=1)


def own_kernel(vol_ref, cot_ref, spread_ref, order_ref, rims_ref, yv_ref, yc_ref, cot_last_ref, first_ref, last_ref):
    yv_ref[...] = to_lanes(by_rows(vol_ref, order_ref), spread_ref).astype(BF)
    rows = by_rows(cot_ref, order_ref)
    cot_last_ref[...] = rows[192:256]
    yc_ref[...] = to_lanes(rows, spread_ref).astype(BF)
    edges = [dot(ref[...], rims_ref[...]) for ref in (yv_ref, yc_ref)]
    first_ref[...] = jnp.concatenate([edge[:, :64] for edge in edges], axis=1).astype(BF)
    last_ref[...] = jnp.concatenate([edge[:, 64:] for edge in edges], axis=1).astype(BF)


def flag(condition):
    return jnp.where(condition, 1.0, 0.0).astype(F32)


def rim_kernel(left_ref, right_ref, out_ref):
    out_ref[:, :128] = (left_ref[...].astype(F32) * flag(lax.axis_index("col") > 0)).astype(BF)
    out_ref[:, 128:] = right_ref[...]


UP_TAP = {(0, 0): 1, (1, 0): 0, (1, 1): 2}
PAIRS = [(a, b, c) for a in range(2) for b in range(2) for c in range(2)]


def write_masks(mask_ref):
    lane = lax.broadcasted_iota(jnp.int32, (1, LANES), 1)
    c = lane
    for d in range(1, QD):
        c = jnp.where(lane >= d * SPAN, lane - d * SPAN, c)
    c = c - HALO
    inside = lane < QD * SPAN
    last_col = lax.axis_index("col") == lax.axis_size("col") - 1
    last_row = lax.axis_index("row") == lax.axis_size("row") - 1
    bound = jnp.where(last_col, QC, LANES)
    seen = jnp.where(inside & (c < bound), 1.0, 0.0).astype(F32)
    mask_ref[...] = jnp.zeros(mask_ref.shape, F32)
    mask_ref[0:1] = seen
    mask_ref[1:2] = seen * jnp.where(last_row, 0.0, 1.0)
    mask_ref[2:3] = jnp.where(inside & (c >= 0) & (c < QC), 1.0, 0.0).astype(F32)


def prepare_kernel(wh_ref, wq_ref, wbh_ref, wbf_ref, w1_ref, w2_ref, w3_ref, w4_ref, up1_ref, up2_ref, up3_ref, mask_ref):
    write_masks(mask_ref)
    for ref, out, eye, back in ((wh_ref, w1_ref, 32, False), (wq_ref, w2_ref, 64, False), (wbh_ref, w3_ref, 64, True), (wbf_ref, w4_ref, 32, True)):
        small, large = ref.shape[1], ref.shape[2]
        if back:
            flat = jnp.concatenate([ref[26 - k] for k in range(27)], axis=0)
        else:
            flat = ref[...].reshape(27 * small, large)
        rows = lax.broadcasted_iota(jnp.int32, (eye, eye), 0)
        cols = lax.broadcasted_iota(jnp.int32, (eye, eye), 1)
        unit = jnp.where(rows == cols, 1.0, 0.0).astype(BF)
        out[...] = dot_nt(unit, flat).astype(BF)
    for ref, out, back in ((wh_ref, up1_ref, True), (wq_ref, up2_ref, True), (wbh_ref, up3_ref, False)):
        small, large = ref.shape[1], ref.shape[2]
        out[...] = jnp.zeros(out.shape, BF)
        for p, (pr, pd, pc) in enumerate(PAIRS):
            for n, (nr, nd, nc) in enumerate(PAIRS):
                taps = [UP_TAP.get(key) for key in ((pd, nd), (pr, nr), (pc, nc))]
                if None in taps:
                    continue
                j = taps[0] * 9 + taps[1] * 3 + taps[2]
                out[p * small : (p + 1) * small, n * large : (n + 1) * large] = ref[26 - j if back else j]


def roll_up(x, steps):
    return pltpu.roll(x, steps % LANES, x.ndim - 1)


def fill_full(win_ref, y, base, count):
    pieces = [y[:, pc * LANES : (pc + 1) * LANES] for pc in range(4)]
    pieces = [roll_up(pieces[3], 1)] + pieces
    for c in range(5):
        piece = pieces[c].reshape(count, 4, 16, LANES)
        for pd in range(4):
            win_ref[1 + pd, base : base + count, c] = piece[:, pd].astype(BF)
        last = piece[:, 3].reshape(count * 16, LANES)
        win_ref[0, base : base + count, c] = roll_up(last, SPAN).reshape(count, 16, LANES).astype(BF)


def put_half(win_ref, row, pd, pc, value):
    win_ref[1 + pd, row, 1 + pc] = value.astype(BF)
    if pc == 1:
        left = roll_up(value, 1)
        win_ref[1 + pd, row, 0] = left.astype(BF)
    if pd == 1:
        above = roll_up(value, SPAN)
        win_ref[0, row, 1 + pc] = above.astype(BF)
        if pc == 1:
            win_ref[0, row, 0] = roll_up(left, SPAN).astype(BF)


def rounded(value):
    return value.astype(BF).astype(F32)


def neighbours(low, high):
    parts = []
    for value in (low, high):
        for nd in range(2):
            moved = roll_up(value, -SPAN) if nd else value
            parts.append(moved.astype(BF))
            parts.append(roll_up(moved, -1).astype(BF))
    return jnp.concatenate(parts, axis=0)


def forward_kernel(xlo_ref, xhi_ref, yv_ref, yc_ref, cot_lo_ref, own_rim_ref, lo_rim_ref, hi_rim_ref, mask_ref, spread_ref, place_ref, order_ref, w1_ref, w2_ref, up3_ref, w4_ref, all_ref, cwin_ref, hwin_ref, preh_ref, preq_ref, q_ref, m_ref, gm_ref, gm_last_ref):
    seen = mask_ref[0:1]
    seen_next = mask_ref[1:2]
    own = mask_ref[2:3]
    inner = flag(lax.axis_index("row") > 0)
    to_vol, to_cot = place_ref[0], place_ref[1]
    y = to_lanes(by_rows(xlo_ref, order_ref)[64:256], spread_ref) + dot(lo_rim_ref[64:256], to_vol)
    fill_full(all_ref, y * inner, 0, 3)
    fill_full(all_ref, yv_ref[...].astype(F32) + dot(own_rim_ref[...], to_vol), 3, 4)
    y = to_lanes(by_rows(xhi_ref, order_ref), spread_ref) + dot(hi_rim_ref[...], to_vol)
    fill_full(all_ref, y, 7, 4)
    w1 = w1_ref[...]
    for hr in range(5):
        for pd in range(2):
            for pc in range(2):
                col = all_ref[2 * pd : 2 * pd + 3, 2 * hr : 2 * hr + 3, 2 * pc : 2 * pc + 3].reshape(432, LANES)
                pre = dot(w1, col)
                if 1 <= hr <= 3:
                    preh_ref[hr - 1, pd, pc] = pre
                h = rounded(pre * sigmoid(pre)) * (seen if hr < 3 else seen_next)
                put_half(hwin_ref, hr, pd, pc, h)
    quarters = []
    for qr in range(2):
        col = hwin_ref[:, 2 * qr : 2 * qr + 3].reshape(864, LANES)
        pre = dot(w2_ref[...], col)
        preq_ref[qr] = pre
        quarters.append(rounded(pre * sigmoid(pre)) * (seen_next if qr else seen))
    q_ref[...] = (quarters[0] * own).astype(BF)
    up = dot(up3_ref[...], neighbours(quarters[0], quarters[1]))
    y = to_lanes(cot_lo_ref[...], spread_ref) + dot(lo_rim_ref[192:256], to_cot)
    fill_full(cwin_ref, y * inner, 0, 1)
    fill_full(cwin_ref, yc_ref[...].astype(F32) + dot(own_rim_ref[...], to_cot), 1, 4)
    w4 = w4_ref[...]
    for p, (pr, pd, pc) in enumerate(PAIRS):
        h = hwin_ref[1 + pd, 1 + pr, 1 + pc].astype(F32)
        pre = up[p * 32 : p * 32 + 32] + h
        m_ref[p] = (rounded(pre * sigmoid(pre)) * own).astype(BF)
        col = cwin_ref[2 * pd : 2 * pd + 3, 2 * pr : 2 * pr + 3, 2 * pc : 2 * pc + 3].reshape(432, LANES)
        gm = rounded(dot(w4, col) * slope(pre)) * seen
        gm_ref[pr, pd, pc] = gm.astype(BF)
        if pr == 1:
            gm_last_ref[pd, pc] = gm.astype(BF)


def full_grad_kernel(cwin_ref, m_ref, out_ref):
    total = None
    for p, (pr, pd, pc) in enumerate(PAIRS):
        col = cwin_ref[2 * pd : 2 * pd + 3, 2 * pr : 2 * pr + 3, 2 * pc : 2 * pc + 3].reshape(432, LANES)
        part = dot_nt(col, m_ref[p])
        total = part if total is None else total + part
    store_groups(out_ref, total, 0, 112, 32)


def store_groups(out_ref, total, base, rows, width):
    size = total.shape[0]
    for group in range(128 // width):
        low, high = group * rows, min((group + 1) * rows, size)
        out_ref[base : base + high - low, group * width : (group + 1) * width] = total[low:high]
        if high - low < rows:
            out_ref[base + high - low : base + rows, group * width : (group + 1) * width] = jnp.zeros((rows - high + low, width), F32)


def backward_kernel(stage, gm_ref, gmlo_ref, gmhi_ref, vwin_ref, hwin_ref, preh_ref, preq_ref, q_ref, g4_ref, mask_ref, w3_ref, up2_ref, ewin_ref, pack_ref, send_ref, mwin_ref):
    seen = mask_ref[0:1]
    seen_next = mask_ref[1:2]
    own = mask_ref[2:3]
    inner = flag(lax.axis_index("row") > 0)
    for pd in range(2):
        for pc in range(2):
            put_half(mwin_ref, 0, pd, pc, gmlo_ref[pd, pc].astype(F32) * inner)
            for pr in range(2):
                put_half(mwin_ref, 1 + pr, pd, pc, gm_ref[pr, pd, pc].astype(F32))
                put_half(mwin_ref, 3 + pr, pd, pc, gmhi_ref[pr, pd, pc].astype(F32))
    quarters = []
    for qr in range(2):
        col = mwin_ref[:, 2 * qr : 2 * qr + 3].reshape(864, LANES)
        gq = rounded(dot(w3_ref[...], col) * slope(preq_ref[qr])) * (seen_next if qr else seen)
        quarters.append(gq)
        if qr == 0:
            store_groups(pack_ref, dot_nt(col, q_ref[...]), 672, 448, 64)
    up = dot(up2_ref[...], neighbours(quarters[0], quarters[1]))
    up_next = dot(up2_ref[0:128, 0:256], neighbours(quarters[1], quarters[1])[0:256])
    total = None
    for p, (pr, pd, pc) in enumerate(PAIRS + [(2, 0, 0), (2, 0, 1), (2, 1, 0), (2, 1, 1)]):
        conv = up[p * 32 : p * 32 + 32] if pr < 2 else up_next[(p - 8) * 32 : (p - 8) * 32 + 32]
        gm = mwin_ref[1 + pd, 1 + pr, 1 + pc].astype(F32)
        gh = rounded((conv + gm) * slope(preh_ref[pr, pd, pc])) * (seen if pr < 2 else seen_next)
        ewin_ref[pd, pr, pc] = gh.astype(BF)
        if pc == 0:
            right = roll_up(gh, -1)
            ewin_ref[pd, pr, 2] = right.astype(BF)
        if pd == 0:
            below = roll_up(gh, -SPAN)
            ewin_ref[2, pr, pc] = below.astype(BF)
            if pc == 0:
                ewin_ref[2, pr, 2] = roll_up(right, -SPAN).astype(BF)
        if pr < 2:
            col = vwin_ref[2 * pd : 2 * pd + 3, 2 * pr + 2 : 2 * pr + 5, 2 * pc : 2 * pc + 3].reshape(432, LANES)
            part = dot_nt(col, (gh * own).astype(BF))
            total = part if total is None else total + part
    store_groups(pack_ref, total, 0, 112, 32)
    pack_ref[112:224] = g4_ref[...]
    col = hwin_ref[:, 0:3].reshape(864, LANES)
    store_groups(pack_ref, dot_nt(col, (quarters[0] * own).astype(BF)), 224, 448, 64)
    pack_ref[1120:PACK] = jnp.zeros((PACK - 1120, 128), F32)
    send_ref[...] = half(pack_ref, stage, False)[...].astype(BF)


def volume_kernel(ewin_ref, cwin_ref, up1_ref, spread_ref, order_ref, out_ref, z_ref):
    up1 = up1_ref[...]
    for pr, pd, pc in PAIRS:
        near = jnp.concatenate(
            [ewin_ref[pd + nd, pr + nr, pc + nc] for nr, nd, nc in PAIRS], axis=0
        )
        up = dot(up1, near)
        for f, (fr, fd, fc) in enumerate(PAIRS):
            r, d, c = 2 * pr + fr, 2 * pd + fd, 2 * pc + fc
            value = up[f * 16 : f * 16 + 16] + cwin_ref[1 + d, 1 + r, 1 + c].astype(F32)
            z_ref[r * 64 + d * 16 : r * 64 + d * 16 + 16, c * LANES : (c + 1) * LANES] = value.astype(BF)
    early = jnp.concatenate([z_ref[:, c * LANES : c * LANES + 256] for c in range(4)], axis=1)
    late = jnp.concatenate([z_ref[:, c * LANES + 128 : (c + 1) * LANES] for c in range(4)], axis=1)
    wide = jnp.concatenate([dot_nt(early, spread_ref[0:768]), dot_nt(late, spread_ref[768:1024])], axis=1).astype(BF)
    wide = lax.dot_general(order_ref[...], wide, (((0,), (0,)), ((), ())), preferred_element_type=F32).astype(BF)
    for d in range(QD):
        out_ref[:, d] = wide[:, d * 128 : (d + 1) * 128].reshape(16, 16, 128)


def side_of(axis, step):
    return jnp.where((lax.axis_index(axis) & step) != 0, 1, 0)


def half(ref, stage, mine):
    count = ref.shape[0] // 2
    side = side_of(*stage)
    return ref.at[pl.ds(pl.multiple_of((side if mine else 1 - side) * count, 16), count)]


def quarter_of(ref, parts, other):
    count = ref.shape[0] // parts
    place = (lax.axis_index("row") & (parts - 1)) ^ other
    return ref.at[pl.ds(pl.multiple_of(place * count, 16), count)]


def fold_kernel(stage, parts, kept_ref, got_ref, own_ref, *send_refs):
    total_ref = send_refs[-1]
    total_ref[...] = half(kept_ref, stage, True)[...] + got_ref[...].astype(F32)
    own_ref[...] = quarter_of(total_ref, parts, 0)[...]
    for other in range(1, parts):
        send_refs[other - 1][...] = quarter_of(total_ref, parts, other)[...].astype(BF)


def unfold_kernel(parts, *refs):
    out_ref = refs[-1]
    for other in range(parts):
        quarter_of(out_ref, parts, other)[...] = refs[other][...]


def finish_kernel(scale, stage, own_ref, got_ref, g1_ref, g2_ref, g3_ref, g4_ref, full_ref):
    half(full_ref, stage, True)[...] = own_ref[...].astype(F32)
    half(full_ref, stage, False)[...] = got_ref[...].astype(F32)
    for ref, base, rows, width in ((g1_ref, 0, 112, 32), (g4_ref, 112, 112, 32), (g2_ref, 224, 448, 64), (g3_ref, 672, 448, 64)):
        small = ref.shape[1]
        taps = rows // small
        back = ref is g3_ref or ref is g4_ref
        for group in range(128 // width):
            count = min(taps, 27 - group * taps)
            block = full_ref[base : base + count * small, group * width : (group + 1) * width] * scale
            block = block.reshape(count, small, width)
            if back:
                for t in range(count):
                    ref[26 - group * taps - t] = block[t]
            else:
                ref[group * taps : group * taps + count] = block


def call(kernel, outs, scratch=(), flops=0, name=None):
    shapes = [jax.ShapeDtypeStruct(shape, dtype) for shape, dtype in outs]
    return pl.pallas_call(
        kernel,
        out_shape=shapes,
        scratch_shapes=list(scratch),
        compiler_params=pltpu.CompilerParams(vmem_limit_bytes=LIMIT),
        cost_estimate=pl.CostEstimate(flops=flops, bytes_accessed=4000000, transcendentals=0),
        name=name,
    )


def swapped(value, row_step, col_step):
    rows, cols = lax.axis_size("row"), lax.axis_size("col")
    pairs = [(r * cols + c, (r ^ row_step) * cols + (c ^ col_step)) for r in range(rows) for c in range(cols)]
    return lax.ppermute(value, ("row", "col"), pairs)


def shifted(value, axis, steps):
    count = lax.axis_size(axis)
    return lax.ppermute(value, axis, [(i, (i + steps) % count) for i in range(count)])


def tree_sum(terms):
    terms = [term.astype(F32) for term in terms]
    while len(terms) > 1:
        terms = [low + high for low, high in zip(terms[::2], terms[1::2])]
    return terms[0]


def by_tap(weight, swap):
    order = (2, 3, 4, 1, 0) if swap else (2, 3, 4, 0, 1)
    moved = weight.transpose(order)
    return moved.reshape((27,) + moved.shape[3:])


def from_tap(grad, swap):
    cube = grad.reshape((3, 3, 3) + grad.shape[1:])
    return cube.transpose((4, 3, 0, 1, 2) if swap else (3, 4, 0, 1, 2))


def shards(volume, cotangent, w_half, w_quarter, w_back_half, w_back_full):
    rows, cols = lax.axis_size("row"), lax.axis_size("col")
    cells = volume.size // volume.shape[0] * rows * cols
    scale = 1.0 / math.sqrt(cells)
    spread, rims, place, order = [jnp.asarray(a) for a in constants()]
    vol = volume.reshape(16, QD, 16, 128)
    cot = cotangent.reshape(16, QD, 16, 128)
    vol_lo, vol_hi = shifted(vol, "row", 1), shifted(vol, "row", -1)
    yv, yc, cot_last, first, last = call(
        own_kernel,
        [((256, 4 * LANES), BF), ((256, 4 * LANES), BF), ((64, 1024), BF), ((256, 128), BF), ((256, 128), BF)],
        name="own",
    )(vol, cot, spread, order, rims)
    left, right = shifted(last, "col", 1), shifted(first, "col", -1)
    cot_lo = shifted(cot_last, "row", 1)
    (own_rim,) = call(rim_kernel, [((256, 256), BF)], name="rim")(left, right)
    lo_rim, hi_rim = shifted(own_rim, "row", 1), shifted(own_rim, "row", -1)
    w1, w2, w3, w4, up1, up2, up3, mask = call(
        prepare_kernel,
        [((32, 432), BF), ((64, 864), BF), ((64, 864), BF), ((32, 432), BF), ((128, 256), BF), ((256, 512), BF), ((256, 512), BF), ((8, LANES), F32)],
        name="prepare",
    )(by_tap(w_half, True), by_tap(w_quarter, True), by_tap(w_back_half, False), by_tap(w_back_full, False))
    vwin, cwin, hwin, preh, preq, quarter, mixed, gm, gm_last = call(
        forward_kernel,
        [
            ((5, 11, 5, 16, LANES), BF),
            ((5, 5, 5, 16, LANES), BF),
            ((3, 5, 3, 32, LANES), BF),
            ((3, 2, 2, 32, LANES), F32),
            ((2, 64, LANES), F32),
            ((64, LANES), BF),
            ((8, 32, LANES), BF),
            ((2, 2, 2, 32, LANES), BF),
            ((2, 2, 32, LANES), BF),
        ],
        name="forward",
    )(vol_lo, vol_hi, yv, yc, cot_lo, own_rim, lo_rim, hi_rim, mask, spread, place, order, w1, w2, up3, w4)
    gm_lo, gm_hi = shifted(gm_last, "row", 1), shifted(gm, "row", -1)
    (g4,) = call(full_grad_kernel, [((112, 128), F32)], flops=2 * 432 * 32 * LANES * 64, name="full_grad")(cwin, mixed)
    core = ("col", 1)
    parts = min(4, rows)
    ewin, kept, send = call(
        functools.partial(backward_kernel, core),
        [((3, 3, 3, 32, LANES), BF), ((PACK, 128), F32), ((PACK // 2, 128), BF)],
        [pltpu.VMEM((3, 5, 3, 32, LANES), BF)],
        name="backward",
    )(gm, gm_lo, gm_hi, vwin, hwin, preh, preq, quarter, g4, mask, w3, up2)
    share = PACK // 2 // parts
    kept, *sends = call(
        functools.partial(fold_kernel, core, parts),
        [((share, 128), F32)] + [((share, 128), BF)] * (parts - 1),
        [pltpu.VMEM((PACK // 2, 128), F32)],
        name="fold",
    )(kept, swapped(send, 0, 1))
    part = tree_sum([kept] + [swapped(send, other + 1, 0) for other, send in enumerate(sends)]).astype(BF)
    for group in ([("row", 4), ("col", 2)], [("col", 4), ("col", 8)], [("col", 16)]):
        group = [(axis, step) for axis, step in group if step < lax.axis_size(axis)]
        terms = [part]
        for index in range(1, 2 ** len(group)):
            chosen = [stage for bit, stage in enumerate(group) if index >> bit & 1]
            moves = [sum(step for axis, step in chosen if axis == name) for name in ("row", "col")]
            terms.append(swapped(part, *moves))
        part = tree_sum(terms).astype(BF)
    (part,) = call(functools.partial(unfold_kernel, parts), [((PACK // 2, 128), BF)], name="unfold")(
        part, *[swapped(part, other, 0) for other in range(1, parts)]
    )
    (grad_volume,) = call(
        volume_kernel, [((16, QD, 16, 128), BF)], [pltpu.VMEM((256, 4 * LANES), BF)], flops=2 * 256 * 1024 * 4000, name="volume"
    )(ewin, cwin, up1, spread, order)
    g1, g2, g3, g4 = call(
        functools.partial(finish_kernel, scale, core),
        [((27, 16, 32), F32), ((27, 32, 64), F32), ((27, 32, 64), F32), ((27, 16, 32), F32)],
        [pltpu.VMEM((PACK, 128), F32)],
        name="finish",
    )(part, swapped(part, 0, 1))
    return (
        grad_volume.reshape(volume.shape),
        from_tap(g1, True),
        from_tap(g2, True),
        from_tap(g3, False),
        from_tap(g4, False),
    )


def solution(mesh):
    return jax.shard_map(
        shards,
        mesh=mesh,
        in_specs=(P(None, None, "row", "col"), P(None, None, "row", "col"), P(), P(), P(), P()),
        out_specs=(P(None, None, "row", "col"), P(), P(), P(), P()),
        check_vma=False,
    )
```

```python
import functools
import math

import jax
import jax.numpy as jnp
from jax import lax
from jax.experimental import pallas as pl
from jax.experimental.pallas import tpu as pltpu
from jax.sharding import PartitionSpec as P

BF = jnp.bfloat16
F32 = jnp.float32

QD, QC, HALO = 8, 32, 2
SPAN = QC + 2 * HALO
LANES = 384
PACK = 1536
LIMIT = 24 * 1024 * 1024


def lane_of(d, c):
    return SPAN * d + c + HALO


def iota(shape, dim):
    return lax.broadcasted_iota(jnp.int32, shape, dim)


def ones_where(condition):
    return jnp.where(condition, 1.0, 0.0).astype(BF)


def tables_kernel(spread_ref, rims_ref, place_ref, order_ref):
    w, lane = iota((128, 256), 0), iota((128, 256), 1)
    for phase in range(4):
        apart = jnp.where((w & 3) == phase, lane - (w >> 2), -LANES)
        for d in range(QD):
            block = ones_where(apart == lane_of(d, 0) - (0 if d < 6 else 128))
            spread_ref[d * 128 : (d + 1) * 128, phase * 256 : (phase + 1) * 256] = block
    slot, lane = iota((LANES, 128), 1), iota((LANES, 128), 0)
    column = (slot & 1) + jnp.where(slot >= 64, QC - 2, 0)
    target = SPAN * ((slot >> 1) & 7) + HALO + column
    for phase in range(4):
        rims_ref[phase * LANES : (phase + 1) * LANES] = ones_where((lane == target) & (((slot >> 4) & 3) == phase))
    place_ref[...] = jnp.zeros(place_ref.shape, BF)
    slot, lane = iota((16, LANES), 0), iota((16, LANES), 1)
    for side in range(2):
        block = ones_where(lane == SPAN * (slot >> 1) + HALO + (slot & 1) + (QC if side else -2))
        for array in range(2):
            for phase in range(4):
                row = side * 128 + array * 64 + phase * 16
                place_ref[array, row : row + 16, phase * LANES : (phase + 1) * LANES] = block
    row, column = iota((256, 256), 0), iota((256, 256), 1)
    order_ref[...] = ones_where(column == (row & 15) * 16 + ((row >> 4) & 3) * 4 + (row >> 6))


def dot(a, b):
    return lax.dot_general(a, b, (((1,), (0,)), ((), ())), preferred_element_type=F32)


def dot_nt(a, b):
    return lax.dot_general(a, b, (((1,), (1,)), ((), ())), preferred_element_type=F32)


def sigmoid(t):
    return 1.0 / (1.0 + jnp.exp(-t))


def slope(t):
    s = sigmoid(t)
    return s * (1.0 + t * (1.0 - s))


def by_rows(x_ref, order_ref):
    wide = jnp.concatenate([x_ref[:, d].reshape(256, 128) for d in range(QD)], axis=1)
    return dot(order_ref[...], wide).astype(BF)


def to_lanes(rows, spread_ref):
    early = dot(rows[:, :768], spread_ref[0:768])
    late = dot(rows[:, 768:], spread_ref[768:1024])
    pieces = []
    for pc in range(4):
        low, high = pc * 256, pc * 256 + 128
        pieces += [early[:, low:high], early[:, high : low + 256] + late[:, low:high], late[:, high : low + 256]]
    return jnp.concatenate(pieces, axis=1)


def fetch(pairs, sems):
    copies = [pltpu.make_async_copy(source, target, sems.at[i]) for i, (source, target) in enumerate(pairs)]
    for copy in copies:
        copy.start()
    return copies


def own_kernel(vol_ref, cot_ref, spread_ref, order_ref, rims_ref, yv_ref, yc_ref, cot_last_ref, first_ref, last_ref, vol_here, cot_here, sems):
    copies = fetch(((vol_ref, vol_here), (cot_ref, cot_here)), sems)
    copies[0].wait()
    yv_ref[...] = to_lanes(by_rows(vol_here, order_ref), spread_ref).astype(BF)
    copies[1].wait()
    rows = by_rows(cot_here, order_ref)
    cot_last_ref[...] = rows[192:256]
    yc_ref[...] = to_lanes(rows, spread_ref).astype(BF)
    edges = [dot(ref[...], rims_ref[...]) for ref in (yv_ref, yc_ref)]
    first_ref[...] = jnp.concatenate([edge[:, :64] for edge in edges], axis=1).astype(BF)
    last_ref[...] = jnp.concatenate([edge[:, 64:] for edge in edges], axis=1).astype(BF)


def flag(condition):
    return jnp.where(condition, 1.0, 0.0).astype(F32)


def rim_kernel(left_ref, right_ref, out_ref):
    out_ref[:, :128] = (left_ref[...].astype(F32) * flag(lax.axis_index("col") > 0)).astype(BF)
    out_ref[:, 128:] = right_ref[...]


UP_TAP = {(0, 0): 1, (1, 0): 0, (1, 1): 2}
PAIRS = [(a, b, c) for a in range(2) for b in range(2) for c in range(2)]


def write_masks(mask_ref):
    lane = lax.broadcasted_iota(jnp.int32, (1, LANES), 1)
    c = lane
    for d in range(1, QD):
        c = jnp.where(lane >= d * SPAN, lane - d * SPAN, c)
    c = c - HALO
    inside = lane < QD * SPAN
    last_col = lax.axis_index("col") == lax.axis_size("col") - 1
    last_row = lax.axis_index("row") == lax.axis_size("row") - 1
    bound = jnp.where(last_col, QC, LANES)
    seen = jnp.where(inside & (c < bound), 1.0, 0.0).astype(F32)
    mask_ref[...] = jnp.zeros(mask_ref.shape, F32)
    mask_ref[0:1] = seen
    mask_ref[1:2] = seen * jnp.where(last_row, 0.0, 1.0)
    mask_ref[2:3] = jnp.where(inside & (c >= 0) & (c < QC), 1.0, 0.0).astype(F32)


def prepare_kernel(*refs):
    sources, outs, here, sems = refs[0:4], refs[4:12], refs[12:16], refs[16]
    copies = fetch(list(zip(sources, here)), sems)
    write_masks(outs[7])
    for copy in copies:
        copy.wait()
    wh_ref, wq_ref, wbh_ref, wbf_ref = here
    w1_ref, w2_ref, w3_ref, w4_ref, up1_ref, up2_ref, up3_ref = outs[:7]
    for ref, out, eye, back in ((wh_ref, w1_ref, 32, False), (wq_ref, w2_ref, 64, False), (wbh_ref, w3_ref, 64, True), (wbf_ref, w4_ref, 32, True)):
        small, large = ref.shape[1], ref.shape[2]
        if back:
            flat = jnp.concatenate([ref[26 - k] for k in range(27)], axis=0)
        else:
            flat = ref[...].reshape(27 * small, large)
        rows = lax.broadcasted_iota(jnp.int32, (eye, eye), 0)
        cols = lax.broadcasted_iota(jnp.int32, (eye, eye), 1)
        unit = jnp.where(rows == cols, 1.0, 0.0).astype(BF)
        out[...] = dot_nt(unit, flat).astype(BF)
    for ref, out, back in ((wh_ref, up1_ref, True), (wq_ref, up2_ref, True), (wbh_ref, up3_ref, False)):
        small, large = ref.shape[1], ref.shape[2]
        out[...] = jnp.zeros(out.shape, BF)
        for p, (pr, pd, pc) in enumerate(PAIRS):
            for n, (nr, nd, nc) in enumerate(PAIRS):
                taps = [UP_TAP.get(key) for key in ((pd, nd), (pr, nr), (pc, nc))]
                if None in taps:
                    continue
                j = taps[0] * 9 + taps[1] * 3 + taps[2]
                out[p * small : (p + 1) * small, n * large : (n + 1) * large] = ref[26 - j if back else j]


def roll_up(x, steps):
    return pltpu.roll(x, steps % LANES, x.ndim - 1)


def fill_full(win_ref, y, base, count):
    pieces = [y[:, pc * LANES : (pc + 1) * LANES] for pc in range(4)]
    pieces = [roll_up(pieces[3], 1)] + pieces
    for c in range(5):
        piece = pieces[c].reshape(count, 4, 16, LANES)
        for pd in range(4):
            win_ref[1 + pd, base : base + count, c] = piece[:, pd].astype(BF)
        last = piece[:, 3].reshape(count * 16, LANES)
        win_ref[0, base : base + count, c] = roll_up(last, SPAN).reshape(count, 16, LANES).astype(BF)


def put_half(win_ref, row, pd, pc, value):
    win_ref[1 + pd, row, 1 + pc] = value.astype(BF)
    if pc == 1:
        left = roll_up(value, 1)
        win_ref[1 + pd, row, 0] = left.astype(BF)
    if pd == 1:
        above = roll_up(value, SPAN)
        win_ref[0, row, 1 + pc] = above.astype(BF)
        if pc == 1:
            win_ref[0, row, 0] = roll_up(left, SPAN).astype(BF)


def rounded(value):
    return value.astype(BF).astype(F32)


def neighbours(low, high):
    parts = []
    for value in (low, high):
        for nd in range(2):
            moved = roll_up(value, -SPAN) if nd else value
            parts.append(moved.astype(BF))
            parts.append(roll_up(moved, -1).astype(BF))
    return jnp.concatenate(parts, axis=0)


def forward_kernel(xlo_ref, xhi_ref, yv_ref, yc_ref, cot_lo_ref, own_rim_ref, lo_rim_ref, hi_rim_ref, mask_ref, spread_ref, place_ref, order_ref, w1_ref, w2_ref, up3_ref, w4_ref, all_ref, cwin_ref, hwin_ref, preh_ref, preq_ref, q_ref, m_ref, gm_ref, gm_last_ref):
    seen = mask_ref[0:1]
    seen_next = mask_ref[1:2]
    own = mask_ref[2:3]
    inner = flag(lax.axis_index("row") > 0)
    to_vol, to_cot = place_ref[0], place_ref[1]
    y = to_lanes(by_rows(xlo_ref, order_ref)[64:256], spread_ref) + dot(lo_rim_ref[64:256], to_vol)
    fill_full(all_ref, y * inner, 0, 3)
    fill_full(all_ref, yv_ref[...].astype(F32) + dot(own_rim_ref[...], to_vol), 3, 4)
    y = to_lanes(by_rows(xhi_ref, order_ref), spread_ref) + dot(hi_rim_ref[...], to_vol)
    fill_full(all_ref, y, 7, 4)
    w1 = w1_ref[...]
    for hr in range(5):
        for pd in range(2):
            for pc in range(2):
                col = all_ref[2 * pd : 2 * pd + 3, 2 * hr : 2 * hr + 3, 2 * pc : 2 * pc + 3].reshape(432, LANES)
                pre = dot(w1, col)
                if 1 <= hr <= 3:
                    preh_ref[hr - 1, pd, pc] = pre
                h = rounded(pre * sigmoid(pre)) * (seen if hr < 3 else seen_next)
                put_half(hwin_ref, hr, pd, pc, h)
    quarters = []
    for qr in range(2):
        col = hwin_ref[:, 2 * qr : 2 * qr + 3].reshape(864, LANES)
        pre = dot(w2_ref[...], col)
        preq_ref[qr] = pre
        quarters.append(rounded(pre * sigmoid(pre)) * (seen_next if qr else seen))
    q_ref[...] = (quarters[0] * own).astype(BF)
    up = dot(up3_ref[...], neighbours(quarters[0], quarters[1]))
    y = to_lanes(cot_lo_ref[...], spread_ref) + dot(lo_rim_ref[192:256], to_cot)
    fill_full(cwin_ref, y * inner, 0, 1)
    fill_full(cwin_ref, yc_ref[...].astype(F32) + dot(own_rim_ref[...], to_cot), 1, 4)
    w4 = w4_ref[...]
    for p, (pr, pd, pc) in enumerate(PAIRS):
        h = hwin_ref[1 + pd, 1 + pr, 1 + pc].astype(F32)
        pre = up[p * 32 : p * 32 + 32] + h
        m_ref[p] = (rounded(pre * sigmoid(pre)) * own).astype(BF)
        col = cwin_ref[2 * pd : 2 * pd + 3, 2 * pr : 2 * pr + 3, 2 * pc : 2 * pc + 3].reshape(432, LANES)
        gm = rounded(dot(w4, col) * slope(pre)) * seen
        gm_ref[pr, pd, pc] = gm.astype(BF)
        if pr == 1:
            gm_last_ref[pd, pc] = gm.astype(BF)


def full_grad_kernel(cwin_ref, m_ref, out_ref):
    total = None
    for p, (pr, pd, pc) in enumerate(PAIRS):
        col = cwin_ref[2 * pd : 2 * pd + 3, 2 * pr : 2 * pr + 3, 2 * pc : 2 * pc + 3].reshape(432, LANES)
        part = dot_nt(col, m_ref[p])
        total = part if total is None else total + part
    store_groups(out_ref, total, 0, 112, 32)


def store_groups(out_ref, total, base, rows, width):
    size = total.shape[0]
    for group in range(128 // width):
        low, high = group * rows, min((group + 1) * rows, size)
        out_ref[base : base + high - low, group * width : (group + 1) * width] = total[low:high]
        if high - low < rows:
            out_ref[base + high - low : base + rows, group * width : (group + 1) * width] = jnp.zeros((rows - high + low, width), F32)


def backward_kernel(stage, gm_ref, gmlo_ref, gmhi_ref, vwin_ref, hwin_ref, preh_ref, preq_ref, q_ref, g4_ref, mask_ref, w3_ref, up2_ref, ewin_ref, pack_ref, send_ref, mwin_ref):
    seen = mask_ref[0:1]
    seen_next = mask_ref[1:2]
    own = mask_ref[2:3]
    inner = flag(lax.axis_index("row") > 0)
    for pd in range(2):
        for pc in range(2):
            put_half(mwin_ref, 0, pd, pc, gmlo_ref[pd, pc].astype(F32) * inner)
            for pr in range(2):
                put_half(mwin_ref, 1 + pr, pd, pc, gm_ref[pr, pd, pc].astype(F32))
                put_half(mwin_ref, 3 + pr, pd, pc, gmhi_ref[pr, pd, pc].astype(F32))
    quarters = []
    for qr in range(2):
        col = mwin_ref[:, 2 * qr : 2 * qr + 3].reshape(864, LANES)
        gq = rounded(dot(w3_ref[...], col) * slope(preq_ref[qr])) * (seen_next if qr else seen)
        quarters.append(gq)
        if qr == 0:
            store_groups(pack_ref, dot_nt(col, q_ref[...]), 672, 448, 64)
    up = dot(up2_ref[...], neighbours(quarters[0], quarters[1]))
    up_next = dot(up2_ref[0:128, 0:256], neighbours(quarters[1], quarters[1])[0:256])
    total = None
    for p, (pr, pd, pc) in enumerate(PAIRS + [(2, 0, 0), (2, 0, 1), (2, 1, 0), (2, 1, 1)]):
        conv = up[p * 32 : p * 32 + 32] if pr < 2 else up_next[(p - 8) * 32 : (p - 8) * 32 + 32]
        gm = mwin_ref[1 + pd, 1 + pr, 1 + pc].astype(F32)
        gh = rounded((conv + gm) * slope(preh_ref[pr, pd, pc])) * (seen if pr < 2 else seen_next)
        ewin_ref[pd, pr, pc] = gh.astype(BF)
        if pc == 0:
            right = roll_up(gh, -1)
            ewin_ref[pd, pr, 2] = right.astype(BF)
        if pd == 0:
            below = roll_up(gh, -SPAN)
            ewin_ref[2, pr, pc] = below.astype(BF)
            if pc == 0:
                ewin_ref[2, pr, 2] = roll_up(right, -SPAN).astype(BF)
        if pr < 2:
            col = vwin_ref[2 * pd : 2 * pd + 3, 2 * pr + 2 : 2 * pr + 5, 2 * pc : 2 * pc + 3].reshape(432, LANES)
            part = dot_nt(col, (gh * own).astype(BF))
            total = part if total is None else total + part
    store_groups(pack_ref, total, 0, 112, 32)
    pack_ref[112:224] = g4_ref[...]
    col = hwin_ref[:, 0:3].reshape(864, LANES)
    store_groups(pack_ref, dot_nt(col, (quarters[0] * own).astype(BF)), 224, 448, 64)
    pack_ref[1120:PACK] = jnp.zeros((PACK - 1120, 128), F32)
    send_ref[...] = half(pack_ref, stage, False)[...].astype(BF)


def volume_kernel(ewin_ref, cwin_ref, up1_ref, spread_ref, order_ref, out_ref, z_ref):
    up1 = up1_ref[...]
    for pr, pd, pc in PAIRS:
        near = jnp.concatenate(
            [ewin_ref[pd + nd, pr + nr, pc + nc] for nr, nd, nc in PAIRS], axis=0
        )
        up = dot(up1, near)
        for f, (fr, fd, fc) in enumerate(PAIRS):
            r, d, c = 2 * pr + fr, 2 * pd + fd, 2 * pc + fc
            value = up[f * 16 : f * 16 + 16] + cwin_ref[1 + d, 1 + r, 1 + c].astype(F32)
            z_ref[r * 64 + d * 16 : r * 64 + d * 16 + 16, c * LANES : (c + 1) * LANES] = value.astype(BF)
    early = jnp.concatenate([z_ref[:, c * LANES : c * LANES + 256] for c in range(4)], axis=1)
    late = jnp.concatenate([z_ref[:, c * LANES + 128 : (c + 1) * LANES] for c in range(4)], axis=1)
    wide = jnp.concatenate([dot_nt(early, spread_ref[0:768]), dot_nt(late, spread_ref[768:1024])], axis=1).astype(BF)
    wide = lax.dot_general(order_ref[...], wide, (((0,), (0,)), ((), ())), preferred_element_type=F32).astype(BF)
    for d in range(QD):
        out_ref[:, d] = wide[:, d * 128 : (d + 1) * 128].reshape(16, 16, 128)


def side_of(axis, step):
    return jnp.where((lax.axis_index(axis) & step) != 0, 1, 0)


def half(ref, stage, mine):
    count = ref.shape[0] // 2
    side = side_of(*stage)
    return ref.at[pl.ds(pl.multiple_of((side if mine else 1 - side) * count, 16), count)]


def fold_kernel(stage, kept_ref, got_ref, out_ref):
    out_ref[...] = (half(kept_ref, stage, True)[...] + got_ref[...].astype(F32)).astype(BF)


def sum_kernel(terms, copies, x_ref, out_ref):
    size = x_ref.shape[0] // terms
    total = x_ref[0:size].astype(F32)
    for i in range(1, terms):
        total = total + x_ref[i * size : (i + 1) * size].astype(F32)
    total = total.astype(BF)
    for i in range(copies):
        out_ref[i * size : (i + 1) * size] = total


def finish_kernel(scale, stage, own_ref, got_ref, g1_ref, g2_ref, g3_ref, g4_ref, full_ref):
    half(full_ref, stage, True)[...] = own_ref[...].astype(F32)
    half(full_ref, stage, False)[...] = got_ref[...].astype(F32)
    for ref, base, rows, width in ((g1_ref, 0, 112, 32), (g4_ref, 112, 112, 32), (g2_ref, 224, 448, 64), (g3_ref, 672, 448, 64)):
        small = ref.shape[1]
        taps = rows // small
        back = ref is g3_ref or ref is g4_ref
        for group in range(128 // width):
            count = min(taps, 27 - group * taps)
            block = full_ref[base : base + count * small, group * width : (group + 1) * width] * scale
            block = block.reshape(count, small, width)
            if back:
                for t in range(count):
                    ref[26 - group * taps - t] = block[t]
            else:
                ref[group * taps : group * taps + count] = block


def call(kernel, outs, scratch=(), flops=0, far=None, name=None):
    shapes = [jax.ShapeDtypeStruct(shape, dtype) for shape, dtype in outs]
    specs = {}
    if far:
        specs["in_specs"] = [pl.BlockSpec(memory_space=pltpu.HBM)] * far[0] + [pl.BlockSpec(memory_space=pltpu.VMEM)] * far[1]
    return pl.pallas_call(
        kernel,
        out_shape=shapes,
        scratch_shapes=list(scratch),
        **specs,
        compiler_params=pltpu.CompilerParams(vmem_limit_bytes=LIMIT),
        cost_estimate=pl.CostEstimate(flops=flops, bytes_accessed=4000000, transcendentals=0),
        name=name,
    )


def swapped(value, row_step, col_step):
    rows, cols = lax.axis_size("row"), lax.axis_size("col")
    pairs = [(r * cols + c, (r ^ row_step) * cols + (c ^ col_step)) for r in range(rows) for c in range(cols)]
    return lax.ppermute(value, ("row", "col"), pairs)


def shifted(value, axis, steps):
    count = lax.axis_size(axis)
    return lax.ppermute(value, axis, [(i, (i + steps) % count) for i in range(count)])


def exchanged(value, row_bits, col_bits):
    rows, cols = lax.axis_size("row"), lax.axis_size("col")
    if not row_bits and not col_bits:
        return value
    groups = {}
    for r in range(rows):
        for c in range(cols):
            groups.setdefault((r & ~row_bits, c & ~col_bits), []).append(r * cols + c)
    return lax.all_to_all(value, ("row", "col"), 0, 0, axis_index_groups=list(groups.values()), tiled=True)


def held(value):
    return pltpu.with_memory_space_constraint(value, pltpu.HBM)


def by_tap(weight, swap):
    order = (2, 3, 4, 1, 0) if swap else (2, 3, 4, 0, 1)
    moved = weight.transpose(order)
    return moved.reshape((27,) + moved.shape[3:])


def from_tap(grad, swap):
    cube = grad.reshape((3, 3, 3) + grad.shape[1:])
    return cube.transpose((4, 3, 0, 1, 2) if swap else (3, 4, 0, 1, 2))


def shards(volume, cotangent, w_half, w_quarter, w_back_half, w_back_full):
    rows, cols = lax.axis_size("row"), lax.axis_size("col")
    cells = volume.size // volume.shape[0] * rows * cols
    scale = 1.0 / math.sqrt(cells)
    spread, rims, place, order = call(
        tables_kernel,
        [((QD * 128, 1024), BF), ((4 * LANES, 128), BF), ((2, 256, 4 * LANES), BF), ((256, 256), BF)],
        name="tables",
    )()
    vol = volume.reshape(16, QD, 16, 128)
    cot = cotangent.reshape(16, QD, 16, 128)
    vol_lo, vol_hi = shifted(vol, "row", 1), shifted(vol, "row", -1)
    yv, yc, cot_last, first, last = call(
        own_kernel,
        [((256, 4 * LANES), BF), ((256, 4 * LANES), BF), ((64, 1024), BF), ((256, 128), BF), ((256, 128), BF)],
        [pltpu.VMEM(vol.shape, BF), pltpu.VMEM(cot.shape, BF), pltpu.SemaphoreType.DMA((2,))],
        far=(2, 3),
        name="own",
    )(held(vol), held(cot), spread, order, rims)
    left, right = shifted(last, "col", 1), shifted(first, "col", -1)
    cot_lo = shifted(cot_last, "row", 1)
    (own_rim,) = call(rim_kernel, [((256, 256), BF)], name="rim")(left, right)
    lo_rim, hi_rim = shifted(own_rim, "row", 1), shifted(own_rim, "row", -1)
    weights = by_tap(w_half, True), by_tap(w_quarter, True), by_tap(w_back_half, False), by_tap(w_back_full, False)
    w1, w2, w3, w4, up1, up2, up3, mask = call(
        prepare_kernel,
        [((32, 432), BF), ((64, 864), BF), ((64, 864), BF), ((32, 432), BF), ((128, 256), BF), ((256, 512), BF), ((256, 512), BF), ((8, LANES), F32)],
        [pltpu.VMEM(weight.shape, BF) for weight in weights] + [pltpu.SemaphoreType.DMA((4,))],
        far=(4, 0),
        name="prepare",
    )(*[held(weight) for weight in weights])
    vwin, cwin, hwin, preh, preq, quarter, mixed, gm, gm_last = call(
        forward_kernel,
        [
            ((5, 11, 5, 16, LANES), BF),
            ((5, 5, 5, 16, LANES), BF),
            ((3, 5, 3, 32, LANES), BF),
            ((3, 2, 2, 32, LANES), F32),
            ((2, 64, LANES), F32),
            ((64, LANES), BF),
            ((8, 32, LANES), BF),
            ((2, 2, 2, 32, LANES), BF),
            ((2, 2, 32, LANES), BF),
        ],
        name="forward",
    )(vol_lo, vol_hi, yv, yc, cot_lo, own_rim, lo_rim, hi_rim, mask, spread, place, order, w1, w2, up3, w4)
    gm_lo, gm_hi = shifted(gm_last, "row", 1), shifted(gm, "row", -1)
    (g4,) = call(full_grad_kernel, [((112, 128), F32)], flops=2 * 432 * 32 * LANES * 64, name="full_grad")(cwin, mixed)
    core = ("col", 1)
    ewin, kept, send = call(
        functools.partial(backward_kernel, core),
        [((3, 3, 3, 32, LANES), BF), ((PACK, 128), F32), ((PACK // 2, 128), BF)],
        [pltpu.VMEM((3, 5, 3, 32, LANES), BF)],
        name="backward",
    )(gm, gm_lo, gm_hi, vwin, hwin, preh, preq, quarter, g4, mask, w3, up2)
    (part,) = call(functools.partial(fold_kernel, core), [((PACK // 2, 128), BF)], name="fold")(kept, swapped(send, 0, 1))
    along = [(7 & (rows - 1), 2 & (cols - 1)), (0, 28 & (cols - 1))]
    sizes = [2 ** (r.bit_count() + c.bit_count()) for r, c in along]
    share = PACK // 2 // sizes[0]
    for bits, size, later in zip(along, sizes, sizes[::-1]):
        part = exchanged(part.reshape(size, share, 128), *bits).reshape(size * share, 128)
        (part,) = call(functools.partial(sum_kernel, size, later), [((later * share, 128), BF)], name="sum")(part)
    part = exchanged(part.reshape(sizes[0], share, 128), *along[0]).reshape(PACK // 2, 128)
    (grad_volume,) = call(
        volume_kernel, [((16, QD, 16, 128), BF)], [pltpu.VMEM((256, 4 * LANES), BF)], flops=2 * 256 * 1024 * 4000, name="volume"
    )(ewin, cwin, up1, spread, order)
    g1, g2, g3, g4 = call(
        functools.partial(finish_kernel, scale, core),
        [((27, 16, 32), F32), ((27, 32, 64), F32), ((27, 32, 64), F32), ((27, 16, 32), F32)],
        [pltpu.VMEM((PACK, 128), F32)],
        name="finish",
    )(part, swapped(part, 0, 1))
    return (
        grad_volume.reshape(volume.shape),
        from_tap(g1, True),
        from_tap(g2, True),
        from_tap(g3, False),
        from_tap(g4, False),
    )


def solution(mesh):
    return jax.shard_map(
        shards,
        mesh=mesh,
        in_specs=(P(None, None, "row", "col"), P(None, None, "row", "col"), P(), P(), P(), P()),
        out_specs=(P(None, None, "row", "col"), P(), P(), P(), P()),
        check_vma=False,
    )
```

```python
import functools
import math

import jax
import jax.numpy as jnp
from jax import lax
from jax.experimental import pallas as pl
from jax.experimental.pallas import tpu as pltpu
from jax.sharding import PartitionSpec as P

BF = jnp.bfloat16
F32 = jnp.float32

QD, QC, HALO = 8, 32, 2
SPAN = QC + 2 * HALO
LANES = 384
PACK = 1536
LIMIT = 24 * 1024 * 1024


def lane_of(d, c):
    return SPAN * d + c + HALO


def iota(shape, dim):
    return lax.broadcasted_iota(jnp.int32, shape, dim)


def ones_where(condition):
    return jnp.where(condition, 1.0, 0.0).astype(BF)


def tables_kernel(spread_ref, rims_ref, place_ref, order_ref):
    w, lane = iota((128, 256), 0), iota((128, 256), 1)
    for phase in range(4):
        apart = jnp.where((w & 3) == phase, lane - (w >> 2), -LANES)
        for d in range(QD):
            block = ones_where(apart == lane_of(d, 0) - (0 if d < 6 else 128))
            spread_ref[d * 128 : (d + 1) * 128, phase * 256 : (phase + 1) * 256] = block
    slot, lane = iota((LANES, 128), 1), iota((LANES, 128), 0)
    column = (slot & 1) + jnp.where(slot >= 64, QC - 2, 0)
    target = SPAN * ((slot >> 1) & 7) + HALO + column
    for phase in range(4):
        rims_ref[phase * LANES : (phase + 1) * LANES] = ones_where((lane == target) & (((slot >> 4) & 3) == phase))
    place_ref[...] = jnp.zeros(place_ref.shape, BF)
    slot, lane = iota((16, LANES), 0), iota((16, LANES), 1)
    for side in range(2):
        block = ones_where(lane == SPAN * (slot >> 1) + HALO + (slot & 1) + (QC if side else -2))
        for array in range(2):
            for phase in range(4):
                row = side * 128 + array * 64 + phase * 16
                place_ref[array, row : row + 16, phase * LANES : (phase + 1) * LANES] = block
    row, column = iota((256, 256), 0), iota((256, 256), 1)
    order_ref[...] = ones_where(column == (row & 15) * 16 + ((row >> 4) & 3) * 4 + (row >> 6))


def dot(a, b):
    return lax.dot_general(a, b, (((1,), (0,)), ((), ())), preferred_element_type=F32)


def dot_nt(a, b):
    return lax.dot_general(a, b, (((1,), (1,)), ((), ())), preferred_element_type=F32)


def sigmoid(t):
    return 1.0 / (1.0 + jnp.exp(-t))


def slope(t):
    s = sigmoid(t)
    return s * (1.0 + t * (1.0 - s))


def by_rows(x_ref, order_ref):
    wide = jnp.concatenate([x_ref[:, d].reshape(256, 128) for d in range(QD)], axis=1)
    return dot(order_ref[...], wide).astype(BF)


def to_lanes(rows, spread_ref):
    early = dot(rows[:, :768], spread_ref[0:768])
    late = dot(rows[:, 768:], spread_ref[768:1024])
    pieces = []
    for pc in range(4):
        low, high = pc * 256, pc * 256 + 128
        pieces += [early[:, low:high], early[:, high : low + 256] + late[:, low:high], late[:, high : low + 256]]
    return jnp.concatenate(pieces, axis=1)


def fetch(pairs, sems):
    copies = [pltpu.make_async_copy(source, target, sems.at[i]) for i, (source, target) in enumerate(pairs)]
    for copy in copies:
        copy.start()
    return copies


def own_kernel(vol_ref, cot_ref, spread_ref, order_ref, rims_ref, yv_ref, yc_ref, main_ref, first_ref, last_ref, vol_here, cot_here, sems):
    copies = fetch(((vol_ref, vol_here), (cot_ref, cot_here)), sems)
    copies[0].wait()
    rows = by_rows(vol_here, order_ref)
    main_ref[0:64] = rows[192:256]
    yv_ref[...] = to_lanes(rows, spread_ref).astype(BF)
    copies[1].wait()
    rows = by_rows(cot_here, order_ref)
    main_ref[64:128] = rows[192:256]
    yc_ref[...] = to_lanes(rows, spread_ref).astype(BF)
    edges = [dot(ref[...], rims_ref[...]) for ref in (yv_ref, yc_ref)]
    first_ref[...] = jnp.concatenate([edge[:, :64] for edge in edges], axis=1).astype(BF)
    last_ref[...] = jnp.concatenate([edge[:, 64:] for edge in edges], axis=1).astype(BF)


def flag(condition):
    return jnp.where(condition, 1.0, 0.0).astype(F32)


def rim_kernel(left_ref, right_ref, out_ref, corner_ref):
    out_ref[:, :128] = (left_ref[...].astype(F32) * flag(lax.axis_index("col") > 0)).astype(BF)
    out_ref[:, 128:] = right_ref[...]
    corner_ref[...] = out_ref[192:256]


UP_TAP = {(0, 0): 1, (1, 0): 0, (1, 1): 2}
PAIRS = [(a, b, c) for a in range(2) for b in range(2) for c in range(2)]


def write_masks(mask_ref):
    lane = lax.broadcasted_iota(jnp.int32, (1, LANES), 1)
    c = lane
    for d in range(1, QD):
        c = jnp.where(lane >= d * SPAN, lane - d * SPAN, c)
    c = c - HALO
    inside = lane < QD * SPAN
    last_col = lax.axis_index("col") == lax.axis_size("col") - 1
    last_row = lax.axis_index("row") == lax.axis_size("row") - 1
    bound = jnp.where(last_col, QC, LANES)
    seen = jnp.where(inside & (c < bound), 1.0, 0.0).astype(F32)
    mask_ref[...] = jnp.zeros(mask_ref.shape, F32)
    mask_ref[0:1] = seen
    mask_ref[1:2] = seen * jnp.where(last_row, 0.0, 1.0)
    mask_ref[2:3] = jnp.where(inside & (c >= 0) & (c < QC), 1.0, 0.0).astype(F32)


def prepare_kernel(*refs):
    sources, outs, here, sems = refs[0:4], refs[4:12], refs[12:16], refs[16]
    copies = fetch(list(zip(sources, here)), sems)
    write_masks(outs[7])
    for copy in copies:
        copy.wait()
    wh_ref, wq_ref, wbh_ref, wbf_ref = here
    w1_ref, w2_ref, w3_ref, w4_ref, up1_ref, up2_ref, up3_ref = outs[:7]
    for ref, out, eye, back in ((wh_ref, w1_ref, 32, False), (wq_ref, w2_ref, 64, False), (wbh_ref, w3_ref, 64, True), (wbf_ref, w4_ref, 32, True)):
        small, large = ref.shape[1], ref.shape[2]
        if back:
            flat = jnp.concatenate([ref[26 - k] for k in range(27)], axis=0)
        else:
            flat = ref[...].reshape(27 * small, large)
        rows = lax.broadcasted_iota(jnp.int32, (eye, eye), 0)
        cols = lax.broadcasted_iota(jnp.int32, (eye, eye), 1)
        unit = jnp.where(rows == cols, 1.0, 0.0).astype(BF)
        out[...] = dot_nt(unit, flat).astype(BF)
    for ref, out, back in ((wh_ref, up1_ref, True), (wq_ref, up2_ref, True), (wbh_ref, up3_ref, False)):
        small, large = ref.shape[1], ref.shape[2]
        out[...] = jnp.zeros(out.shape, BF)
        for p, (pr, pd, pc) in enumerate(PAIRS):
            for n, (nr, nd, nc) in enumerate(PAIRS):
                taps = [UP_TAP.get(key) for key in ((pd, nd), (pr, nr), (pc, nc))]
                if None in taps:
                    continue
                j = taps[0] * 9 + taps[1] * 3 + taps[2]
                out[p * small : (p + 1) * small, n * large : (n + 1) * large] = ref[26 - j if back else j]


def roll_up(x, steps):
    return pltpu.roll(x, steps % LANES, x.ndim - 1)


def fill_full(win_ref, y, base, count):
    pieces = [y[:, pc * LANES : (pc + 1) * LANES] for pc in range(4)]
    pieces = [roll_up(pieces[3], 1)] + pieces
    for c in range(5):
        piece = pieces[c].reshape(count, 4, 16, LANES)
        for pd in range(4):
            win_ref[1 + pd, base : base + count, c] = piece[:, pd].astype(BF)
        last = piece[:, 3].reshape(count * 16, LANES)
        win_ref[0, base : base + count, c] = roll_up(last, SPAN).reshape(count, 16, LANES).astype(BF)


def put_half(win_ref, row, pd, pc, value):
    win_ref[1 + pd, row, 1 + pc] = value.astype(BF)
    if pc == 1:
        left = roll_up(value, 1)
        win_ref[1 + pd, row, 0] = left.astype(BF)
    if pd == 1:
        above = roll_up(value, SPAN)
        win_ref[0, row, 1 + pc] = above.astype(BF)
        if pc == 1:
            win_ref[0, row, 0] = roll_up(left, SPAN).astype(BF)


def rounded(value):
    return value.astype(BF).astype(F32)


def neighbours(low, high):
    parts = []
    for value in (low, high):
        for nd in range(2):
            moved = roll_up(value, -SPAN) if nd else value
            parts.append(moved.astype(BF))
            parts.append(roll_up(moved, -1).astype(BF))
    return jnp.concatenate(parts, axis=0)


def half_kernel(main_ref, yv_ref, own_rim_ref, lo_rim_ref, mask_ref, spread_ref, place_ref, w1_ref, vwin_ref, preh_ref, h_ref, h_last_ref):
    seen = mask_ref[0:1]
    to_vol = place_ref[0]
    y = to_lanes(main_ref[0:64], spread_ref) + dot(lo_rim_ref[...], to_vol)
    fill_full(vwin_ref, y * flag(lax.axis_index("row") > 0), 0, 1)
    fill_full(vwin_ref, yv_ref[...].astype(F32) + dot(own_rim_ref[...], to_vol), 1, 4)
    w1 = w1_ref[...]
    for pr, pd, pc in PAIRS:
        col = vwin_ref[2 * pd : 2 * pd + 3, 2 * pr : 2 * pr + 3, 2 * pc : 2 * pc + 3].reshape(432, LANES)
        pre = dot(w1, col)
        preh_ref[pr, pd, pc] = pre
        h_ref[pr, pd, pc] = (pre * sigmoid(pre) * seen).astype(BF)
        if pr == 1:
            h_last_ref[pd, pc] = h_ref[pr, pd, pc]


def cotangent_kernel(main_ref, yc_ref, own_rim_ref, lo_rim_ref, spread_ref, place_ref, w4_ref, cwin_ref, pull_ref):
    to_cot = place_ref[1]
    y = to_lanes(main_ref[64:128], spread_ref) + dot(lo_rim_ref[...], to_cot)
    fill_full(cwin_ref, y * flag(lax.axis_index("row") > 0), 0, 1)
    fill_full(cwin_ref, yc_ref[...].astype(F32) + dot(own_rim_ref[...], to_cot), 1, 4)
    w4 = w4_ref[...]
    for p, (pr, pd, pc) in enumerate(PAIRS):
        col = cwin_ref[2 * pd : 2 * pd + 3, 2 * pr : 2 * pr + 3, 2 * pc : 2 * pc + 3].reshape(432, LANES)
        pull_ref[p] = dot(w4, col)


def middle_kernel(h_ref, hlo_ref, hhi_ref, pull_ref, mask_ref, w2_ref, up3_ref, hwin_ref, preq_ref, q_ref, m_ref, gm_ref, gm_last_ref):
    seen = mask_ref[0:1]
    seen_next = mask_ref[1:2]
    own = mask_ref[2:3]
    inner = flag(lax.axis_index("row") > 0)
    for pd in range(2):
        for pc in range(2):
            put_half(hwin_ref, 0, pd, pc, hlo_ref[pd, pc].astype(F32) * inner)
            for pr in range(2):
                put_half(hwin_ref, 1 + pr, pd, pc, h_ref[pr, pd, pc].astype(F32))
                put_half(hwin_ref, 3 + pr, pd, pc, hhi_ref[pr, pd, pc].astype(F32) * seen_next)
    quarters = []
    for qr in range(2):
        col = hwin_ref[:, 2 * qr : 2 * qr + 3].reshape(864, LANES)
        pre = dot(w2_ref[...], col)
        preq_ref[qr] = pre
        quarters.append(rounded(pre * sigmoid(pre)) * (seen_next if qr else seen))
    q_ref[...] = (quarters[0] * own).astype(BF)
    up = dot(up3_ref[...], neighbours(quarters[0], quarters[1]))
    for p, (pr, pd, pc) in enumerate(PAIRS):
        pre = up[p * 32 : p * 32 + 32] + h_ref[pr, pd, pc].astype(F32)
        m_ref[p] = (rounded(pre * sigmoid(pre)) * own).astype(BF)
        gm = rounded(pull_ref[p] * slope(pre)) * seen
        gm_ref[pr, pd, pc] = gm.astype(BF)
        if pr == 1:
            gm_last_ref[pd, pc] = gm.astype(BF)


def full_grad_kernel(cwin_ref, m_ref, out_ref):
    total = None
    for p, (pr, pd, pc) in enumerate(PAIRS):
        col = cwin_ref[2 * pd : 2 * pd + 3, 2 * pr : 2 * pr + 3, 2 * pc : 2 * pc + 3].reshape(432, LANES)
        part = dot_nt(col, m_ref[p])
        total = part if total is None else total + part
    store_groups(out_ref, total, 0, 112, 32)


def store_groups(out_ref, total, base, rows, width):
    size = total.shape[0]
    for group in range(128 // width):
        low, high = group * rows, min((group + 1) * rows, size)
        out_ref[base : base + high - low, group * width : (group + 1) * width] = total[low:high]
        if high - low < rows:
            out_ref[base + high - low : base + rows, group * width : (group + 1) * width] = jnp.zeros((rows - high + low, width), F32)


def put_upper(win_ref, pd, pc, value):
    win_ref[pd, pc] = value.astype(BF)
    if pc == 0:
        right = roll_up(value, -1)
        win_ref[pd, 2] = right.astype(BF)
    if pd == 0:
        win_ref[2, pc] = roll_up(value, -SPAN).astype(BF)
        if pc == 0:
            win_ref[2, 2] = roll_up(right, -SPAN).astype(BF)


def backward_kernel(stage, gm_ref, gmlo_ref, gmhi_ref, vwin_ref, hwin_ref, preh_ref, preq_ref, q_ref, g4_ref, mask_ref, w3_ref, up2_ref, ewin_ref, gh_first_ref, pack_ref, send_ref, mwin_ref):
    seen = mask_ref[0:1]
    seen_next = mask_ref[1:2]
    own = mask_ref[2:3]
    inner = flag(lax.axis_index("row") > 0)
    for pd in range(2):
        for pc in range(2):
            put_half(mwin_ref, 0, pd, pc, gmlo_ref[pd, pc].astype(F32) * inner)
            for pr in range(2):
                put_half(mwin_ref, 1 + pr, pd, pc, gm_ref[pr, pd, pc].astype(F32))
                put_half(mwin_ref, 3 + pr, pd, pc, gmhi_ref[pr, pd, pc].astype(F32))
    quarters = []
    for qr in range(2):
        col = mwin_ref[:, 2 * qr : 2 * qr + 3].reshape(864, LANES)
        gq = rounded(dot(w3_ref[...], col) * slope(preq_ref[qr])) * (seen_next if qr else seen)
        quarters.append(gq)
        if qr == 0:
            store_groups(pack_ref, dot_nt(col, q_ref[...]), 672, 448, 64)
    up = dot(up2_ref[...], neighbours(quarters[0], quarters[1]))
    total = None
    for p, (pr, pd, pc) in enumerate(PAIRS):
        conv = up[p * 32 : p * 32 + 32]
        gm = mwin_ref[1 + pd, 1 + pr, 1 + pc].astype(F32)
        gh = rounded((conv + gm) * slope(preh_ref[pr, pd, pc])) * seen
        put_upper(ewin_ref.at[:, pr], pd, pc, gh)
        if pr == 0:
            gh_first_ref[pd, pc] = gh.astype(BF)
        col = vwin_ref[2 * pd : 2 * pd + 3, 2 * pr : 2 * pr + 3, 2 * pc : 2 * pc + 3].reshape(432, LANES)
        part = dot_nt(col, (gh * own).astype(BF))
        total = part if total is None else total + part
    store_groups(pack_ref, total, 0, 112, 32)
    pack_ref[112:224] = g4_ref[...]
    col = hwin_ref[:, 0:3].reshape(864, LANES)
    store_groups(pack_ref, dot_nt(col, (quarters[0] * own).astype(BF)), 224, 448, 64)
    pack_ref[1120:PACK] = jnp.zeros((PACK - 1120, 128), F32)
    send_ref[...] = half(pack_ref, stage, False)[...].astype(BF)


def volume_kernel(ewin_ref, next_ref, cwin_ref, up1_ref, spread_ref, order_ref, out_ref, z_ref, ext_ref):
    below = flag(lax.axis_index("row") < lax.axis_size("row") - 1)
    for pd in range(2):
        for pc in range(2):
            put_upper(ext_ref, pd, pc, next_ref[pd, pc].astype(F32) * below)
    up1 = up1_ref[...]
    for pr, pd, pc in PAIRS:
        near = jnp.concatenate(
            [
                ewin_ref[pd + nd, pr + nr, pc + nc] if pr + nr < 2 else ext_ref[pd + nd, pc + nc]
                for nr, nd, nc in PAIRS
            ],
            axis=0,
        )
        up = dot(up1, near)
        for f, (fr, fd, fc) in enumerate(PAIRS):
            r, d, c = 2 * pr + fr, 2 * pd + fd, 2 * pc + fc
            value = up[f * 16 : f * 16 + 16] + cwin_ref[1 + d, 1 + r, 1 + c].astype(F32)
            z_ref[r * 64 + d * 16 : r * 64 + d * 16 + 16, c * LANES : (c + 1) * LANES] = value.astype(BF)
    early = jnp.concatenate([z_ref[:, c * LANES : c * LANES + 256] for c in range(4)], axis=1)
    late = jnp.concatenate([z_ref[:, c * LANES + 128 : (c + 1) * LANES] for c in range(4)], axis=1)
    wide = jnp.concatenate([dot_nt(early, spread_ref[0:768]), dot_nt(late, spread_ref[768:1024])], axis=1).astype(BF)
    wide = lax.dot_general(order_ref[...], wide, (((0,), (0,)), ((), ())), preferred_element_type=F32).astype(BF)
    for d in range(QD):
        out_ref[:, d] = wide[:, d * 128 : (d + 1) * 128].reshape(16, 16, 128)


def side_of(axis, step):
    return jnp.where((lax.axis_index(axis) & step) != 0, 1, 0)


def half(ref, stage, mine):
    count = ref.shape[0] // 2
    side = side_of(*stage)
    return ref.at[pl.ds(pl.multiple_of((side if mine else 1 - side) * count, 16), count)]


def fold_kernel(stage, kept_ref, got_ref, out_ref):
    out_ref[...] = (half(kept_ref, stage, True)[...] + got_ref[...].astype(F32)).astype(BF)


def sum_kernel(terms, copies, x_ref, out_ref):
    size = x_ref.shape[0] // terms
    total = x_ref[0:size].astype(F32)
    for i in range(1, terms):
        total = total + x_ref[i * size : (i + 1) * size].astype(F32)
    total = total.astype(BF)
    for i in range(copies):
        out_ref[i * size : (i + 1) * size] = total


def finish_kernel(scale, stage, own_ref, got_ref, g1_ref, g2_ref, g3_ref, g4_ref, full_ref):
    half(full_ref, stage, True)[...] = own_ref[...].astype(F32)
    half(full_ref, stage, False)[...] = got_ref[...].astype(F32)
    for ref, base, rows, width in ((g1_ref, 0, 112, 32), (g4_ref, 112, 112, 32), (g2_ref, 224, 448, 64), (g3_ref, 672, 448, 64)):
        small = ref.shape[1]
        taps = rows // small
        back = ref is g3_ref or ref is g4_ref
        for group in range(128 // width):
            count = min(taps, 27 - group * taps)
            block = full_ref[base : base + count * small, group * width : (group + 1) * width] * scale
            block = block.reshape(count, small, width)
            if back:
                for t in range(count):
                    ref[26 - group * taps - t] = block[t]
            else:
                ref[group * taps : group * taps + count] = block


def call(kernel, outs, scratch=(), flops=0, far=None, name=None):
    shapes = [jax.ShapeDtypeStruct(shape, dtype) for shape, dtype in outs]
    specs = {}
    if far:
        specs["in_specs"] = [pl.BlockSpec(memory_space=pltpu.HBM)] * far[0] + [pl.BlockSpec(memory_space=pltpu.VMEM)] * far[1]
    return pl.pallas_call(
        kernel,
        out_shape=shapes,
        scratch_shapes=list(scratch),
        **specs,
        compiler_params=pltpu.CompilerParams(vmem_limit_bytes=LIMIT),
        cost_estimate=pl.CostEstimate(flops=flops, bytes_accessed=4000000, transcendentals=0),
        name=name,
    )


def swapped(value, row_step, col_step):
    rows, cols = lax.axis_size("row"), lax.axis_size("col")
    pairs = [(r * cols + c, (r ^ row_step) * cols + (c ^ col_step)) for r in range(rows) for c in range(cols)]
    return lax.ppermute(value, ("row", "col"), pairs)


def shifted(value, axis, steps):
    count = lax.axis_size(axis)
    return lax.ppermute(value, axis, [(i, (i + steps) % count) for i in range(count)])


def exchanged(value, row_bits, col_bits):
    rows, cols = lax.axis_size("row"), lax.axis_size("col")
    if not row_bits and not col_bits:
        return value
    groups = {}
    for r in range(rows):
        for c in range(cols):
            groups.setdefault((r & ~row_bits, c & ~col_bits), []).append(r * cols + c)
    return lax.all_to_all(value, ("row", "col"), 0, 0, axis_index_groups=list(groups.values()), tiled=True)


def held(value):
    return pltpu.with_memory_space_constraint(value, pltpu.HBM)


def by_tap(weight, swap):
    order = (2, 3, 4, 1, 0) if swap else (2, 3, 4, 0, 1)
    moved = weight.transpose(order)
    return moved.reshape((27,) + moved.shape[3:])


def from_tap(grad, swap):
    cube = grad.reshape((3, 3, 3) + grad.shape[1:])
    return cube.transpose((4, 3, 0, 1, 2) if swap else (3, 4, 0, 1, 2))


def shards(volume, cotangent, w_half, w_quarter, w_back_half, w_back_full):
    rows, cols = lax.axis_size("row"), lax.axis_size("col")
    cells = volume.size // volume.shape[0] * rows * cols
    scale = 1.0 / math.sqrt(cells)
    spread, rims, place, order = call(
        tables_kernel,
        [((QD * 128, 1024), BF), ((4 * LANES, 128), BF), ((2, 256, 4 * LANES), BF), ((256, 256), BF)],
        name="tables",
    )()
    vol = volume.reshape(16, QD, 16, 128)
    cot = cotangent.reshape(16, QD, 16, 128)
    yv, yc, main, first, last = call(
        own_kernel,
        [((256, 4 * LANES), BF), ((256, 4 * LANES), BF), ((128, 1024), BF), ((256, 128), BF), ((256, 128), BF)],
        [pltpu.VMEM(vol.shape, BF), pltpu.VMEM(cot.shape, BF), pltpu.SemaphoreType.DMA((2,))],
        far=(2, 3),
        name="own",
    )(held(vol), held(cot), spread, order, rims)
    left, right = shifted(last, "col", 1), shifted(first, "col", -1)
    main_lo = shifted(main, "row", 1)
    own_rim, corner = call(rim_kernel, [((256, 256), BF), ((64, 256), BF)], name="rim")(left, right)
    lo_rim = shifted(corner, "row", 1)
    weights = by_tap(w_half, True), by_tap(w_quarter, True), by_tap(w_back_half, False), by_tap(w_back_full, False)
    w1, w2, w3, w4, up1, up2, up3, mask = call(
        prepare_kernel,
        [((32, 432), BF), ((64, 864), BF), ((64, 864), BF), ((32, 432), BF), ((128, 256), BF), ((256, 512), BF), ((256, 512), BF), ((8, LANES), F32)],
        [pltpu.VMEM(weight.shape, BF) for weight in weights] + [pltpu.SemaphoreType.DMA((4,))],
        far=(4, 0),
        name="prepare",
    )(*[held(weight) for weight in weights])
    full_window, half_rows = (5, 5, 5, 16, LANES), (2, 2, 2, 32, LANES)
    vwin, preh, half_act, half_last = call(
        half_kernel,
        [(full_window, BF), (half_rows, F32), (half_rows, BF), (half_rows[1:], BF)],
        name="half",
    )(main_lo, yv, own_rim, lo_rim, mask, spread, place, w1)
    half_lo, half_hi = shifted(half_last, "row", 1), shifted(half_act, "row", -1)
    cwin, pull = call(
        cotangent_kernel, [(full_window, BF), ((8, 32, LANES), F32)], flops=2 * 432 * 32 * LANES * 64, name="cotangent"
    )(main_lo, yc, own_rim, lo_rim, spread, place, w4)
    hwin, preq, quarter, mixed, gm, gm_last = call(
        middle_kernel,
        [((3, 5, 3, 32, LANES), BF), ((2, 64, LANES), F32), ((64, LANES), BF), ((8, 32, LANES), BF), (half_rows, BF), (half_rows[1:], BF)],
        name="middle",
    )(half_act, half_lo, half_hi, pull, mask, w2, up3)
    gm_lo, gm_hi = shifted(gm_last, "row", 1), shifted(gm, "row", -1)
    (g4,) = call(full_grad_kernel, [((112, 128), F32)], flops=2 * 432 * 32 * LANES * 64, name="full_grad")(cwin, mixed)
    core = ("col", 1)
    ewin, gh_first, kept, send = call(
        functools.partial(backward_kernel, core),
        [((3, 2, 3, 32, LANES), BF), (half_rows[1:], BF), ((PACK, 128), F32), ((PACK // 2, 128), BF)],
        [pltpu.VMEM((3, 5, 3, 32, LANES), BF)],
        name="backward",
    )(gm, gm_lo, gm_hi, vwin, hwin, preh, preq, quarter, g4, mask, w3, up2)
    (part,) = call(functools.partial(fold_kernel, core), [((PACK // 2, 128), BF)], name="fold")(kept, swapped(send, 0, 1))
    along = [(7 & (rows - 1), 2 & (cols - 1)), (0, 28 & (cols - 1))]
    sizes = [2 ** (r.bit_count() + c.bit_count()) for r, c in along]
    share = PACK // 2 // sizes[0]
    for bits, size, later in zip(along, sizes, sizes[::-1]):
        part = exchanged(part.reshape(size, share, 128), *bits).reshape(size * share, 128)
        (part,) = call(functools.partial(sum_kernel, size, later), [((later * share, 128), BF)], name="sum")(part)
    part = exchanged(part.reshape(sizes[0], share, 128), *along[0]).reshape(PACK // 2, 128)
    (grad_volume,) = call(
        volume_kernel, [((16, QD, 16, 128), BF)], [pltpu.VMEM((256, 4 * LANES), BF), pltpu.VMEM((3, 3, 32, LANES), BF)], flops=2 * 256 * 1024 * 4000, name="volume"
    )(ewin, shifted(gh_first, "row", -1), cwin, up1, spread, order)
    g1, g2, g3, g4 = call(
        functools.partial(finish_kernel, scale, core),
        [((27, 16, 32), F32), ((27, 32, 64), F32), ((27, 32, 64), F32), ((27, 16, 32), F32)],
        [pltpu.VMEM((PACK, 128), F32)],
        name="finish",
    )(part, swapped(part, 0, 1))
    return (
        grad_volume.reshape(volume.shape),
        from_tap(g1, True),
        from_tap(g2, True),
        from_tap(g3, False),
        from_tap(g4, False),
    )


def solution(mesh):
    return jax.shard_map(
        shards,
        mesh=mesh,
        in_specs=(P(None, None, "row", "col"), P(None, None, "row", "col"), P(), P(), P(), P()),
        out_specs=(P(None, None, "row", "col"), P(), P(), P(), P()),
        check_vma=False,
    )
```

```python
import functools
import math

import jax
import jax.numpy as jnp
from jax import lax
from jax.experimental import pallas as pl
from jax.experimental.pallas import tpu as pltpu
from jax.sharding import PartitionSpec as P

BF = jnp.bfloat16
F32 = jnp.float32

QD, QC, HALO = 8, 32, 2
SPAN = QC + 2 * HALO
LANES = 384
PACK = 1536
LIMIT = 24 * 1024 * 1024


def lane_of(d, c):
    return SPAN * d + c + HALO


def iota(shape, dim):
    return lax.broadcasted_iota(jnp.int32, shape, dim)


def ones_where(condition):
    return jnp.where(condition, 1.0, 0.0).astype(BF)


def tables_kernel(spread_ref, rims_ref, place_ref, order_ref):
    w, lane = iota((128, 256), 0), iota((128, 256), 1)
    for phase in range(4):
        apart = jnp.where((w & 3) == phase, lane - (w >> 2), -LANES)
        for d in range(QD):
            block = ones_where(apart == lane_of(d, 0) - (0 if d < 6 else 128))
            spread_ref[d * 128 : (d + 1) * 128, phase * 256 : (phase + 1) * 256] = block
    slot, row = iota((QD * 128, 128), 1), iota((QD * 128, 128), 0)
    column = (slot & 1) + jnp.where(slot >= 64, QC - 2, 0)
    rims_ref[...] = ones_where(row == ((slot >> 1) & 7) * 128 + 4 * column + ((slot >> 4) & 3))
    place_ref[...] = jnp.zeros(place_ref.shape, BF)
    slot, lane = iota((16, LANES), 0), iota((16, LANES), 1)
    for side in range(2):
        block = ones_where(lane == SPAN * (slot >> 1) + HALO + (slot & 1) + (QC if side else -2))
        for array in range(2):
            for phase in range(4):
                row = side * 128 + array * 64 + phase * 16
                place_ref[array, row : row + 16, phase * LANES : (phase + 1) * LANES] = block
    row, column = iota((256, 256), 0), iota((256, 256), 1)
    order_ref[...] = ones_where(column == (row & 15) * 16 + ((row >> 4) & 3) * 4 + (row >> 6))


def dot(a, b):
    return lax.dot_general(a, b, (((1,), (0,)), ((), ())), preferred_element_type=F32)


def dot_nt(a, b):
    return lax.dot_general(a, b, (((1,), (1,)), ((), ())), preferred_element_type=F32)


def sigmoid(t):
    return 1.0 / (1.0 + jnp.exp(-t))


def slope(t):
    s = sigmoid(t)
    return s * (1.0 + t * (1.0 - s))


def by_rows(x_ref, order_ref):
    wide = jnp.concatenate([x_ref[:, d].reshape(256, 128) for d in range(QD)], axis=1)
    return dot(order_ref[...], wide).astype(BF)


def to_lanes(rows, spread_ref):
    early = dot(rows[:, :768], spread_ref[0:768])
    late = dot(rows[:, 768:], spread_ref[768:1024])
    pieces = []
    for pc in range(4):
        low, high = pc * 256, pc * 256 + 128
        pieces += [early[:, low:high], early[:, high : low + 256] + late[:, low:high], late[:, high : low + 256]]
    return jnp.concatenate(pieces, axis=1)


def fetch(pairs, sems):
    copies = [pltpu.make_async_copy(source, target, sems.at[i]) for i, (source, target) in enumerate(pairs)]
    for copy in copies:
        copy.start()
    return copies


def edge_kernel(vol_ref, cot_ref, order_ref, rims_ref, vol_rows_ref, cot_rows_ref, main_ref, first_ref, last_ref, first_low_ref, last_low_ref, vol_here, cot_here, sems):
    copies = fetch(((vol_ref, vol_here), (cot_ref, cot_here)), sems)
    edges = []
    for i, (here, rows_ref) in enumerate(((vol_here, vol_rows_ref), (cot_here, cot_rows_ref))):
        copies[i].wait()
        rows = by_rows(here, order_ref)
        rows_ref[...] = rows
        main_ref[i * 64 : i * 64 + 64] = rows[192:256]
        edges.append(dot(rows, rims_ref[...]))
    first_ref[...] = jnp.concatenate([edge[:, :64] for edge in edges], axis=1).astype(BF)
    last_ref[...] = jnp.concatenate([edge[:, 64:] for edge in edges], axis=1).astype(BF)
    first_low_ref[...] = first_ref[192:256]
    last_low_ref[...] = last_ref[192:256]


def own_kernel(vol_rows_ref, cot_rows_ref, spread_ref, yv_ref, yc_ref):
    yv_ref[...] = to_lanes(vol_rows_ref[...], spread_ref).astype(BF)
    yc_ref[...] = to_lanes(cot_rows_ref[...], spread_ref).astype(BF)


def flag(condition):
    return jnp.where(condition, 1.0, 0.0).astype(F32)


def rims_of(left_ref, right_ref):
    left = left_ref[...].astype(F32) * flag(lax.axis_index("col") > 0)
    return jnp.concatenate([left.astype(BF), right_ref[...]], axis=1)


UP_TAP = {(0, 0): 1, (1, 0): 0, (1, 1): 2}
PAIRS = [(a, b, c) for a in range(2) for b in range(2) for c in range(2)]


def write_masks(mask_ref):
    lane = lax.broadcasted_iota(jnp.int32, (1, LANES), 1)
    c = lane
    for d in range(1, QD):
        c = jnp.where(lane >= d * SPAN, lane - d * SPAN, c)
    c = c - HALO
    inside = lane < QD * SPAN
    last_col = lax.axis_index("col") == lax.axis_size("col") - 1
    last_row = lax.axis_index("row") == lax.axis_size("row") - 1
    bound = jnp.where(last_col, QC, LANES)
    seen = jnp.where(inside & (c < bound), 1.0, 0.0).astype(F32)
    mask_ref[...] = jnp.zeros(mask_ref.shape, F32)
    mask_ref[0:1] = seen
    mask_ref[1:2] = seen * jnp.where(last_row, 0.0, 1.0)
    mask_ref[2:3] = jnp.where(inside & (c >= 0) & (c < QC), 1.0, 0.0).astype(F32)


def prepare_kernel(*refs):
    sources, outs, here, sems = refs[0:4], refs[4:12], refs[12:16], refs[16]
    copies = fetch(list(zip(sources, here)), sems)
    write_masks(outs[7])
    for copy in copies:
        copy.wait()
    wh_ref, wq_ref, wbh_ref, wbf_ref = here
    w1_ref, w2_ref, w3_ref, w4_ref, up1_ref, up2_ref, up3_ref = outs[:7]
    for ref, out, eye, back in ((wh_ref, w1_ref, 32, False), (wq_ref, w2_ref, 64, False), (wbh_ref, w3_ref, 64, True), (wbf_ref, w4_ref, 32, True)):
        small, large = ref.shape[1], ref.shape[2]
        if back:
            flat = jnp.concatenate([ref[26 - k] for k in range(27)], axis=0)
        else:
            flat = ref[...].reshape(27 * small, large)
        rows = lax.broadcasted_iota(jnp.int32, (eye, eye), 0)
        cols = lax.broadcasted_iota(jnp.int32, (eye, eye), 1)
        unit = jnp.where(rows == cols, 1.0, 0.0).astype(BF)
        out[...] = dot_nt(unit, flat).astype(BF)
    for ref, out, back in ((wh_ref, up1_ref, True), (wq_ref, up2_ref, True), (wbh_ref, up3_ref, False)):
        small, large = ref.shape[1], ref.shape[2]
        out[...] = jnp.zeros(out.shape, BF)
        for p, (pr, pd, pc) in enumerate(PAIRS):
            for n, (nr, nd, nc) in enumerate(PAIRS):
                taps = [UP_TAP.get(key) for key in ((pd, nd), (pr, nr), (pc, nc))]
                if None in taps:
                    continue
                j = taps[0] * 9 + taps[1] * 3 + taps[2]
                out[p * small : (p + 1) * small, n * large : (n + 1) * large] = ref[26 - j if back else j]


def roll_up(x, steps):
    return pltpu.roll(x, steps % LANES, x.ndim - 1)


def fill_full(win_ref, y, base, count):
    pieces = [y[:, pc * LANES : (pc + 1) * LANES] for pc in range(4)]
    pieces = [roll_up(pieces[3], 1)] + pieces
    for c in range(5):
        piece = pieces[c].reshape(count, 4, 16, LANES)
        for pd in range(4):
            win_ref[1 + pd, base : base + count, c] = piece[:, pd].astype(BF)
        last = piece[:, 3].reshape(count * 16, LANES)
        win_ref[0, base : base + count, c] = roll_up(last, SPAN).reshape(count, 16, LANES).astype(BF)


def put_half(win_ref, row, pd, pc, value):
    win_ref[1 + pd, row, 1 + pc] = value.astype(BF)
    if pc == 1:
        left = roll_up(value, 1)
        win_ref[1 + pd, row, 0] = left.astype(BF)
    if pd == 1:
        above = roll_up(value, SPAN)
        win_ref[0, row, 1 + pc] = above.astype(BF)
        if pc == 1:
            win_ref[0, row, 0] = roll_up(left, SPAN).astype(BF)


def rounded(value):
    return value.astype(BF).astype(F32)


def neighbours(low, high):
    parts = []
    for value in (low, high):
        for nd in range(2):
            moved = roll_up(value, -SPAN) if nd else value
            parts.append(moved.astype(BF))
            parts.append(roll_up(moved, -1).astype(BF))
    return jnp.concatenate(parts, axis=0)


def half_kernel(main_ref, yv_ref, left_ref, right_ref, low_left_ref, low_right_ref, mask_ref, spread_ref, place_ref, w1_ref, vwin_ref, preh_ref, h_ref, h_last_ref):
    seen = mask_ref[0:1]
    to_vol = place_ref[0]
    y = to_lanes(main_ref[0:64], spread_ref) + dot(rims_of(low_left_ref, low_right_ref), to_vol)
    fill_full(vwin_ref, y * flag(lax.axis_index("row") > 0), 0, 1)
    fill_full(vwin_ref, yv_ref[...].astype(F32) + dot(rims_of(left_ref, right_ref), to_vol), 1, 4)
    w1 = w1_ref[...]
    for pr, pd, pc in PAIRS:
        col = vwin_ref[2 * pd : 2 * pd + 3, 2 * pr : 2 * pr + 3, 2 * pc : 2 * pc + 3].reshape(432, LANES)
        pre = dot(w1, col)
        preh_ref[pr, pd, pc] = pre
        h_ref[pr, pd, pc] = (pre * sigmoid(pre) * seen).astype(BF)
        if pr == 1:
            h_last_ref[pd, pc] = h_ref[pr, pd, pc]


def cotangent_kernel(main_ref, yc_ref, left_ref, right_ref, low_left_ref, low_right_ref, spread_ref, place_ref, w4_ref, cwin_ref, pull_ref):
    to_cot = place_ref[1]
    y = to_lanes(main_ref[64:128], spread_ref) + dot(rims_of(low_left_ref, low_right_ref), to_cot)
    fill_full(cwin_ref, y * flag(lax.axis_index("row") > 0), 0, 1)
    fill_full(cwin_ref, yc_ref[...].astype(F32) + dot(rims_of(left_ref, right_ref), to_cot), 1, 4)
    w4 = w4_ref[...]
    for p, (pr, pd, pc) in enumerate(PAIRS):
        col = cwin_ref[2 * pd : 2 * pd + 3, 2 * pr : 2 * pr + 3, 2 * pc : 2 * pc + 3].reshape(432, LANES)
        pull_ref[p] = dot(w4, col)


def middle_kernel(h_ref, hlo_ref, hhi_ref, pull_ref, mask_ref, w2_ref, up3_ref, hwin_ref, preq_ref, q_ref, m_ref, gm_ref, gm_last_ref):
    seen = mask_ref[0:1]
    seen_next = mask_ref[1:2]
    own = mask_ref[2:3]
    inner = flag(lax.axis_index("row") > 0)
    for pd in range(2):
        for pc in range(2):
            put_half(hwin_ref, 0, pd, pc, hlo_ref[pd, pc].astype(F32) * inner)
            for pr in range(2):
                put_half(hwin_ref, 1 + pr, pd, pc, h_ref[pr, pd, pc].astype(F32))
                put_half(hwin_ref, 3 + pr, pd, pc, hhi_ref[pr, pd, pc].astype(F32) * seen_next)
    quarters = []
    for qr in range(2):
        col = hwin_ref[:, 2 * qr : 2 * qr + 3].reshape(864, LANES)
        pre = dot(w2_ref[...], col)
        preq_ref[qr] = pre
        quarters.append(rounded(pre * sigmoid(pre)) * (seen_next if qr else seen))
    q_ref[...] = (quarters[0] * own).astype(BF)
    up = dot(up3_ref[...], neighbours(quarters[0], quarters[1]))
    for p, (pr, pd, pc) in enumerate(PAIRS):
        pre = up[p * 32 : p * 32 + 32] + h_ref[pr, pd, pc].astype(F32)
        m_ref[p] = (rounded(pre * sigmoid(pre)) * own).astype(BF)
        gm = rounded(pull_ref[p] * slope(pre)) * seen
        gm_ref[pr, pd, pc] = gm.astype(BF)
        if pr == 1:
            gm_last_ref[pd, pc] = gm.astype(BF)


def full_grad_kernel(cwin_ref, m_ref, out_ref):
    total = None
    for p, (pr, pd, pc) in enumerate(PAIRS):
        col = cwin_ref[2 * pd : 2 * pd + 3, 2 * pr : 2 * pr + 3, 2 * pc : 2 * pc + 3].reshape(432, LANES)
        part = dot_nt(col, m_ref[p])
        total = part if total is None else total + part
    store_groups(out_ref, total, 0, 112, 32)


def store_groups(out_ref, total, base, rows, width):
    size = total.shape[0]
    for group in range(128 // width):
        low, high = group * rows, min((group + 1) * rows, size)
        out_ref[base : base + high - low, group * width : (group + 1) * width] = total[low:high]
        if high - low < rows:
            out_ref[base + high - low : base + rows, group * width : (group + 1) * width] = jnp.zeros((rows - high + low, width), F32)


def put_upper(win_ref, pd, pc, value):
    win_ref[pd, pc] = value.astype(BF)
    if pc == 0:
        right = roll_up(value, -1)
        win_ref[pd, 2] = right.astype(BF)
    if pd == 0:
        win_ref[2, pc] = roll_up(value, -SPAN).astype(BF)
        if pc == 0:
            win_ref[2, 2] = roll_up(right, -SPAN).astype(BF)


def backward_kernel(stage, gm_ref, gmlo_ref, gmhi_ref, vwin_ref, hwin_ref, preh_ref, preq_ref, q_ref, g4_ref, mask_ref, w3_ref, up2_ref, ewin_ref, gh_first_ref, pack_ref, send_ref, mwin_ref):
    seen = mask_ref[0:1]
    seen_next = mask_ref[1:2]
    own = mask_ref[2:3]
    inner = flag(lax.axis_index("row") > 0)
    for pd in range(2):
        for pc in range(2):
            put_half(mwin_ref, 0, pd, pc, gmlo_ref[pd, pc].astype(F32) * inner)
            for pr in range(2):
                put_half(mwin_ref, 1 + pr, pd, pc, gm_ref[pr, pd, pc].astype(F32))
                put_half(mwin_ref, 3 + pr, pd, pc, gmhi_ref[pr, pd, pc].astype(F32))
    quarters = []
    for qr in range(2):
        col = mwin_ref[:, 2 * qr : 2 * qr + 3].reshape(864, LANES)
        gq = rounded(dot(w3_ref[...], col) * slope(preq_ref[qr])) * (seen_next if qr else seen)
        quarters.append(gq)
        if qr == 0:
            store_groups(pack_ref, dot_nt(col, q_ref[...]), 672, 448, 64)
    up = dot(up2_ref[...], neighbours(quarters[0], quarters[1]))
    total = None
    for p, (pr, pd, pc) in enumerate(PAIRS):
        conv = up[p * 32 : p * 32 + 32]
        gm = mwin_ref[1 + pd, 1 + pr, 1 + pc].astype(F32)
        gh = rounded((conv + gm) * slope(preh_ref[pr, pd, pc])) * seen
        put_upper(ewin_ref.at[:, pr], pd, pc, gh)
        if pr == 0:
            gh_first_ref[pd, pc] = gh.astype(BF)
        col = vwin_ref[2 * pd : 2 * pd + 3, 2 * pr : 2 * pr + 3, 2 * pc : 2 * pc + 3].reshape(432, LANES)
        part = dot_nt(col, (gh * own).astype(BF))
        total = part if total is None else total + part
    store_groups(pack_ref, total, 0, 112, 32)
    pack_ref[112:224] = g4_ref[...]
    col = hwin_ref[:, 0:3].reshape(864, LANES)
    store_groups(pack_ref, dot_nt(col, (quarters[0] * own).astype(BF)), 224, 448, 64)
    pack_ref[1120:PACK] = jnp.zeros((PACK - 1120, 128), F32)
    send_ref[...] = half(pack_ref, stage, False)[...].astype(BF)


def volume_kernel(ewin_ref, next_ref, cwin_ref, up1_ref, spread_ref, order_ref, out_ref, z_ref, ext_ref):
    below = flag(lax.axis_index("row") < lax.axis_size("row") - 1)
    for pd in range(2):
        for pc in range(2):
            put_upper(ext_ref, pd, pc, next_ref[pd, pc].astype(F32) * below)
    up1 = up1_ref[...]
    for pr, pd, pc in PAIRS:
        near = jnp.concatenate(
            [
                ewin_ref[pd + nd, pr + nr, pc + nc] if pr + nr < 2 else ext_ref[pd + nd, pc + nc]
                for nr, nd, nc in PAIRS
            ],
            axis=0,
        )
        up = dot(up1, near)
        for f, (fr, fd, fc) in enumerate(PAIRS):
            r, d, c = 2 * pr + fr, 2 * pd + fd, 2 * pc + fc
            value = up[f * 16 : f * 16 + 16] + cwin_ref[1 + d, 1 + r, 1 + c].astype(F32)
            z_ref[r * 64 + d * 16 : r * 64 + d * 16 + 16, c * LANES : (c + 1) * LANES] = value.astype(BF)
    early = jnp.concatenate([z_ref[:, c * LANES : c * LANES + 256] for c in range(4)], axis=1)
    late = jnp.concatenate([z_ref[:, c * LANES + 128 : (c + 1) * LANES] for c in range(4)], axis=1)
    wide = jnp.concatenate([dot_nt(early, spread_ref[0:768]), dot_nt(late, spread_ref[768:1024])], axis=1).astype(BF)
    wide = lax.dot_general(order_ref[...], wide, (((0,), (0,)), ((), ())), preferred_element_type=F32).astype(BF)
    for d in range(QD):
        out_ref[:, d] = wide[:, d * 128 : (d + 1) * 128].reshape(16, 16, 128)


def side_of(axis, step):
    return jnp.where((lax.axis_index(axis) & step) != 0, 1, 0)


def half(ref, stage, mine):
    count = ref.shape[0] // 2
    side = side_of(*stage)
    return ref.at[pl.ds(pl.multiple_of((side if mine else 1 - side) * count, 16), count)]


def fold_kernel(stage, kept_ref, got_ref, out_ref):
    out_ref[...] = (half(kept_ref, stage, True)[...] + got_ref[...].astype(F32)).astype(BF)


def sum_kernel(terms, copies, x_ref, out_ref):
    size = x_ref.shape[0] // terms
    total = x_ref[0:size].astype(F32)
    for i in range(1, terms):
        total = total + x_ref[i * size : (i + 1) * size].astype(F32)
    total = total.astype(BF)
    for i in range(copies):
        out_ref[i * size : (i + 1) * size] = total


def finish_kernel(scale, stage, own_ref, got_ref, g1_ref, g2_ref, g3_ref, g4_ref, full_ref):
    half(full_ref, stage, True)[...] = own_ref[...].astype(F32)
    half(full_ref, stage, False)[...] = got_ref[...].astype(F32)
    for ref, base, rows, width in ((g1_ref, 0, 112, 32), (g4_ref, 112, 112, 32), (g2_ref, 224, 448, 64), (g3_ref, 672, 448, 64)):
        small = ref.shape[1]
        taps = rows // small
        back = ref is g3_ref or ref is g4_ref
        for group in range(128 // width):
            count = min(taps, 27 - group * taps)
            block = full_ref[base : base + count * small, group * width : (group + 1) * width] * scale
            block = block.reshape(count, small, width)
            if back:
                for t in range(count):
                    ref[26 - group * taps - t] = block[t]
            else:
                ref[group * taps : group * taps + count] = block


def call(kernel, outs, scratch=(), flops=0, far=None, name=None):
    shapes = [jax.ShapeDtypeStruct(shape, dtype) for shape, dtype in outs]
    specs = {}
    if far:
        specs["in_specs"] = [pl.BlockSpec(memory_space=pltpu.HBM)] * far[0] + [pl.BlockSpec(memory_space=pltpu.VMEM)] * far[1]
    return pl.pallas_call(
        kernel,
        out_shape=shapes,
        scratch_shapes=list(scratch),
        **specs,
        compiler_params=pltpu.CompilerParams(vmem_limit_bytes=LIMIT),
        cost_estimate=pl.CostEstimate(flops=flops, bytes_accessed=4000000, transcendentals=0),
        name=name,
    )


def swapped(value, row_step, col_step):
    rows, cols = lax.axis_size("row"), lax.axis_size("col")
    pairs = [(r * cols + c, (r ^ row_step) * cols + (c ^ col_step)) for r in range(rows) for c in range(cols)]
    return lax.ppermute(value, ("row", "col"), pairs)


def shifted(value, axis, steps):
    count = lax.axis_size(axis)
    return lax.ppermute(value, axis, [(i, (i + steps) % count) for i in range(count)])


def diagonal(value, row_step, col_step):
    rows, cols = lax.axis_size("row"), lax.axis_size("col")
    pairs = [(r * cols + c, (r + row_step) % rows * cols + (c + col_step) % cols) for r in range(rows) for c in range(cols)]
    return lax.ppermute(value, ("row", "col"), pairs)


def exchanged(value, row_bits, col_bits):
    rows, cols = lax.axis_size("row"), lax.axis_size("col")
    if not row_bits and not col_bits:
        return value
    groups = {}
    for r in range(rows):
        for c in range(cols):
            groups.setdefault((r & ~row_bits, c & ~col_bits), []).append(r * cols + c)
    return lax.all_to_all(value, ("row", "col"), 0, 0, axis_index_groups=list(groups.values()), tiled=True)


def held(value):
    return pltpu.with_memory_space_constraint(value, pltpu.HBM)


def by_tap(weight, swap):
    order = (2, 3, 4, 1, 0) if swap else (2, 3, 4, 0, 1)
    moved = weight.transpose(order)
    return moved.reshape((27,) + moved.shape[3:])


def from_tap(grad, swap):
    cube = grad.reshape((3, 3, 3) + grad.shape[1:])
    return cube.transpose((4, 3, 0, 1, 2) if swap else (3, 4, 0, 1, 2))


def shards(volume, cotangent, w_half, w_quarter, w_back_half, w_back_full):
    rows, cols = lax.axis_size("row"), lax.axis_size("col")
    cells = volume.size // volume.shape[0] * rows * cols
    scale = 1.0 / math.sqrt(cells)
    spread, rims, place, order = call(
        tables_kernel,
        [((QD * 128, 1024), BF), ((QD * 128, 128), BF), ((2, 256, 4 * LANES), BF), ((256, 256), BF)],
        name="tables",
    )()
    vol = volume.reshape(16, QD, 16, 128)
    cot = cotangent.reshape(16, QD, 16, 128)
    vol_rows, cot_rows, main, first, last, first_low, last_low = call(
        edge_kernel,
        [((256, 1024), BF), ((256, 1024), BF), ((128, 1024), BF), ((256, 128), BF), ((256, 128), BF), ((64, 128), BF), ((64, 128), BF)],
        [pltpu.VMEM(vol.shape, BF), pltpu.VMEM(cot.shape, BF), pltpu.SemaphoreType.DMA((2,))],
        far=(2, 2),
        name="edge",
    )(held(vol), held(cot), order, rims)
    main_lo = shifted(main, "row", 1)
    edges = [shifted(last, "col", 1), shifted(first, "col", -1), diagonal(last_low, 1, 1), diagonal(first_low, 1, -1)]
    yv, yc = call(own_kernel, [((256, 4 * LANES), BF), ((256, 4 * LANES), BF)], flops=2 * 256 * 1024 * 4000, name="own")(vol_rows, cot_rows, spread)
    weights = by_tap(w_half, True), by_tap(w_quarter, True), by_tap(w_back_half, False), by_tap(w_back_full, False)
    w1, w2, w3, w4, up1, up2, up3, mask = call(
        prepare_kernel,
        [((32, 432), BF), ((64, 864), BF), ((64, 864), BF), ((32, 432), BF), ((128, 256), BF), ((256, 512), BF), ((256, 512), BF), ((8, LANES), F32)],
        [pltpu.VMEM(weight.shape, BF) for weight in weights] + [pltpu.SemaphoreType.DMA((4,))],
        far=(4, 0),
        name="prepare",
    )(*[held(weight) for weight in weights])
    full_window, half_rows = (5, 5, 5, 16, LANES), (2, 2, 2, 32, LANES)
    vwin, preh, half_act, half_last = call(
        half_kernel,
        [(full_window, BF), (half_rows, F32), (half_rows, BF), (half_rows[1:], BF)],
        name="half",
    )(main_lo, yv, *edges, mask, spread, place, w1)
    half_lo, half_hi = shifted(half_last, "row", 1), shifted(half_act, "row", -1)
    cwin, pull = call(
        cotangent_kernel, [(full_window, BF), ((8, 32, LANES), F32)], flops=2 * 432 * 32 * LANES * 64, name="cotangent"
    )(main_lo, yc, *edges, spread, place, w4)
    hwin, preq, quarter, mixed, gm, gm_last = call(
        middle_kernel,
        [((3, 5, 3, 32, LANES), BF), ((2, 64, LANES), F32), ((64, LANES), BF), ((8, 32, LANES), BF), (half_rows, BF), (half_rows[1:], BF)],
        name="middle",
    )(half_act, half_lo, half_hi, pull, mask, w2, up3)
    gm_lo, gm_hi = shifted(gm_last, "row", 1), shifted(gm, "row", -1)
    (g4,) = call(full_grad_kernel, [((112, 128), F32)], flops=2 * 432 * 32 * LANES * 64, name="full_grad")(cwin, mixed)
    core = ("col", 1)
    ewin, gh_first, kept, send = call(
        functools.partial(backward_kernel, core),
        [((3, 2, 3, 32, LANES), BF), (half_rows[1:], BF), ((PACK, 128), F32), ((PACK // 2, 128), BF)],
        [pltpu.VMEM((3, 5, 3, 32, LANES), BF)],
        name="backward",
    )(gm, gm_lo, gm_hi, vwin, hwin, preh, preq, quarter, g4, mask, w3, up2)
    (part,) = call(functools.partial(fold_kernel, core), [((PACK // 2, 128), BF)], name="fold")(kept, swapped(send, 0, 1))
    part, gh_next = lax.optimization_barrier((part, shifted(gh_first, "row", -1)))
    along = [(7 & (rows - 1), 2 & (cols - 1)), (0, 28 & (cols - 1))]
    sizes = [2 ** (r.bit_count() + c.bit_count()) for r, c in along]
    share = PACK // 2 // sizes[0]
    for bits, size, later in zip(along, sizes, sizes[::-1]):
        part = exchanged(part.reshape(size, share, 128), *bits).reshape(size * share, 128)
        (part,) = call(functools.partial(sum_kernel, size, later), [((later * share, 128), BF)], name="sum")(part)
    part = exchanged(part.reshape(sizes[0], share, 128), *along[0]).reshape(PACK // 2, 128)
    (grad_volume,) = call(
        volume_kernel, [((16, QD, 16, 128), BF)], [pltpu.VMEM((256, 4 * LANES), BF), pltpu.VMEM((3, 3, 32, LANES), BF)], flops=2 * 256 * 1024 * 4000, name="volume"
    )(ewin, gh_next, cwin, up1, spread, order)
    part, grad_volume = lax.optimization_barrier((part, grad_volume))
    g1, g2, g3, g4 = call(
        functools.partial(finish_kernel, scale, core),
        [((27, 16, 32), F32), ((27, 32, 64), F32), ((27, 32, 64), F32), ((27, 16, 32), F32)],
        [pltpu.VMEM((PACK, 128), F32)],
        name="finish",
    )(part, swapped(part, 0, 1))
    return (
        grad_volume.reshape(volume.shape),
        from_tap(g1, True),
        from_tap(g2, True),
        from_tap(g3, False),
        from_tap(g4, False),
    )


def solution(mesh):
    return jax.shard_map(
        shards,
        mesh=mesh,
        in_specs=(P(None, None, "row", "col"), P(None, None, "row", "col"), P(), P(), P(), P()),
        out_specs=(P(None, None, "row", "col"), P(), P(), P(), P()),
        check_vma=False,
    )
```

```python
import functools
import math

import jax
import jax.numpy as jnp
from jax import lax
from jax.experimental import pallas as pl
from jax.experimental.pallas import tpu as pltpu
from jax.sharding import PartitionSpec as P

BF = jnp.bfloat16
F32 = jnp.float32

QD, QC, HALO = 8, 32, 2
SPAN = QC + 2 * HALO
LANES = 384
PACK = 1280
LIMIT = 24 * 1024 * 1024


def lane_of(d, c):
    return SPAN * d + c + HALO


def iota(shape, dim):
    return lax.broadcasted_iota(jnp.int32, shape, dim)


def ones_where(condition):
    return jnp.where(condition, 1.0, 0.0).astype(BF)


def tables_kernel(spread_ref, rims_ref, place_ref, order_ref):
    w, lane = iota((128, 256), 0), iota((128, 256), 1)
    for phase in range(4):
        apart = jnp.where((w & 3) == phase, lane - (w >> 2), -LANES)
        for d in range(QD):
            block = ones_where(apart == lane_of(d, 0) - (0 if d < 6 else 128))
            spread_ref[d * 128 : (d + 1) * 128, phase * 256 : (phase + 1) * 256] = block
    slot, row = iota((QD * 128, 128), 1), iota((QD * 128, 128), 0)
    column = (slot & 1) + jnp.where(slot >= 64, QC - 2, 0)
    rims_ref[...] = ones_where(row == ((slot >> 1) & 7) * 128 + 4 * column + ((slot >> 4) & 3))
    place_ref[...] = jnp.zeros(place_ref.shape, BF)
    slot, lane = iota((16, LANES), 0), iota((16, LANES), 1)
    for side in range(2):
        block = ones_where(lane == SPAN * (slot >> 1) + HALO + (slot & 1) + (QC if side else -2))
        for array in range(2):
            for phase in range(4):
                row = side * 128 + array * 64 + phase * 16
                place_ref[array, row : row + 16, phase * LANES : (phase + 1) * LANES] = block
    row, column = iota((256, 256), 0), iota((256, 256), 1)
    order_ref[...] = ones_where(column == (row & 15) * 16 + ((row >> 4) & 3) * 4 + (row >> 6))


def dot(a, b):
    return lax.dot_general(a, b, (((1,), (0,)), ((), ())), preferred_element_type=F32)


def dot_nt(a, b):
    return lax.dot_general(a, b, (((1,), (1,)), ((), ())), preferred_element_type=F32)


def sigmoid(t):
    return 1.0 / (1.0 + jnp.exp(-t))


def slope(t):
    s = sigmoid(t)
    return s * (1.0 + t * (1.0 - s))


def by_rows(x_ref, order_ref):
    wide = jnp.concatenate([x_ref[:, d].reshape(256, 128) for d in range(QD)], axis=1)
    return dot(order_ref[...], wide).astype(BF)


def to_lanes(rows, spread_ref):
    early = dot(rows[:, :768], spread_ref[0:768])
    late = dot(rows[:, 768:], spread_ref[768:1024])
    pieces = []
    for pc in range(4):
        low, high = pc * 256, pc * 256 + 128
        pieces += [early[:, low:high], early[:, high : low + 256] + late[:, low:high], late[:, high : low + 256]]
    return jnp.concatenate(pieces, axis=1)


def fetch(pairs, sems):
    copies = [pltpu.make_async_copy(source, target, sems.at[i]) for i, (source, target) in enumerate(pairs)]
    for copy in copies:
        copy.start()
    return copies


def edge_kernel(vol_ref, cot_ref, order_ref, rims_ref, vol_rows_ref, cot_rows_ref, main_ref, first_ref, last_ref, first_low_ref, last_low_ref, vol_here, cot_here, sems):
    copies = fetch(((vol_ref, vol_here), (cot_ref, cot_here)), sems)
    edges = []
    for i, (here, rows_ref) in enumerate(((vol_here, vol_rows_ref), (cot_here, cot_rows_ref))):
        copies[i].wait()
        rows = by_rows(here, order_ref)
        rows_ref[...] = rows
        main_ref[i * 64 : i * 64 + 64] = rows[192:256]
        edges.append(dot(rows, rims_ref[...]))
    first_ref[...] = jnp.concatenate([edge[:, :64] for edge in edges], axis=1).astype(BF)
    last_ref[...] = jnp.concatenate([edge[:, 64:] for edge in edges], axis=1).astype(BF)
    first_low_ref[...] = first_ref[192:256]
    last_low_ref[...] = last_ref[192:256]


def own_kernel(vol_rows_ref, cot_rows_ref, spread_ref, yv_ref, yc_ref):
    yv_ref[...] = to_lanes(vol_rows_ref[...], spread_ref).astype(BF)
    yc_ref[...] = to_lanes(cot_rows_ref[...], spread_ref).astype(BF)


def flag(condition):
    return jnp.where(condition, 1.0, 0.0).astype(F32)


def rims_of(left_ref, right_ref):
    left = left_ref[...].astype(F32) * flag(lax.axis_index("col") > 0)
    return jnp.concatenate([left.astype(BF), right_ref[...]], axis=1)


UP_TAP = {(0, 0): 1, (1, 0): 0, (1, 1): 2}
PAIRS = [(a, b, c) for a in range(2) for b in range(2) for c in range(2)]


def write_masks(mask_ref):
    lane = lax.broadcasted_iota(jnp.int32, (1, LANES), 1)
    c = lane
    for d in range(1, QD):
        c = jnp.where(lane >= d * SPAN, lane - d * SPAN, c)
    c = c - HALO
    inside = lane < QD * SPAN
    last_col = lax.axis_index("col") == lax.axis_size("col") - 1
    last_row = lax.axis_index("row") == lax.axis_size("row") - 1
    bound = jnp.where(last_col, QC, LANES)
    seen = jnp.where(inside & (c < bound), 1.0, 0.0).astype(F32)
    mask_ref[...] = jnp.zeros(mask_ref.shape, F32)
    mask_ref[0:1] = seen
    mask_ref[1:2] = seen * jnp.where(last_row, 0.0, 1.0)
    mask_ref[2:3] = jnp.where(inside & (c >= 0) & (c < QC), 1.0, 0.0).astype(F32)


def prepare_kernel(*refs):
    sources, outs, here, sems = refs[0:4], refs[4:12], refs[12:16], refs[16]
    copies = fetch(list(zip(sources, here)), sems)
    write_masks(outs[7])
    for copy in copies:
        copy.wait()
    wh_ref, wq_ref, wbh_ref, wbf_ref = here
    w1_ref, w2_ref, w3_ref, w4_ref, up1_ref, up2_ref, up3_ref = outs[:7]
    for ref, out, eye, back in ((wh_ref, w1_ref, 32, False), (wq_ref, w2_ref, 64, False), (wbh_ref, w3_ref, 64, True), (wbf_ref, w4_ref, 32, True)):
        small, large = ref.shape[1], ref.shape[2]
        if back:
            flat = jnp.concatenate([ref[26 - k] for k in range(27)], axis=0)
        else:
            flat = ref[...].reshape(27 * small, large)
        rows = lax.broadcasted_iota(jnp.int32, (eye, eye), 0)
        cols = lax.broadcasted_iota(jnp.int32, (eye, eye), 1)
        unit = jnp.where(rows == cols, 1.0, 0.0).astype(BF)
        out[...] = dot_nt(unit, flat).astype(BF)
    for ref, out, back in ((wh_ref, up1_ref, True), (wq_ref, up2_ref, True), (wbh_ref, up3_ref, False)):
        small, large = ref.shape[1], ref.shape[2]
        out[...] = jnp.zeros(out.shape, BF)
        for p, (pr, pd, pc) in enumerate(PAIRS):
            for n, (nr, nd, nc) in enumerate(PAIRS):
                taps = [UP_TAP.get(key) for key in ((pd, nd), (pr, nr), (pc, nc))]
                if None in taps:
                    continue
                j = taps[0] * 9 + taps[1] * 3 + taps[2]
                out[p * small : (p + 1) * small, n * large : (n + 1) * large] = ref[26 - j if back else j]


def roll_up(x, steps):
    return pltpu.roll(x, steps % LANES, x.ndim - 1)


def fill_full(win_ref, y, base, count):
    pieces = [y[:, pc * LANES : (pc + 1) * LANES] for pc in range(4)]
    pieces = [roll_up(pieces[3], 1)] + pieces
    for c in range(5):
        piece = pieces[c].reshape(count, 4, 16, LANES)
        for pd in range(4):
            win_ref[1 + pd, base : base + count, c] = piece[:, pd].astype(BF)
        last = piece[:, 3].reshape(count * 16, LANES)
        win_ref[0, base : base + count, c] = roll_up(last, SPAN).reshape(count, 16, LANES).astype(BF)


def put_half(win_ref, row, pd, pc, value):
    win_ref[1 + pd, row, 1 + pc] = value.astype(BF)
    if pc == 1:
        left = roll_up(value, 1)
        win_ref[1 + pd, row, 0] = left.astype(BF)
    if pd == 1:
        above = roll_up(value, SPAN)
        win_ref[0, row, 1 + pc] = above.astype(BF)
        if pc == 1:
            win_ref[0, row, 0] = roll_up(left, SPAN).astype(BF)


def packed(values):
    tails = [pltpu.roll(value[:, 256:], 32 * i, 1) if i else value[:, 256:] for i, value in enumerate(values)]
    tail = (tails[0] + tails[1]) + (tails[2] + tails[3])
    return jnp.concatenate([value[:, :256] for value in values] + [tail], axis=1).astype(BF)


def unpacked(value, i):
    tail = value[:, 1024:]
    tail = pltpu.roll(tail, 128 - 32 * i, 1) if i else tail
    tail = jnp.where(iota(tail.shape, 1) < 32, tail, 0.0)
    return jnp.concatenate([value[:, 256 * i : 256 * i + 256], tail], axis=1)


def rounded(value):
    return value.astype(BF).astype(F32)


def neighbours(low, high):
    parts = []
    for value in (low, high):
        for nd in range(2):
            moved = roll_up(value, -SPAN) if nd else value
            parts.append(moved.astype(BF))
            parts.append(roll_up(moved, -1).astype(BF))
    return jnp.concatenate(parts, axis=0)


def half_kernel(main_ref, yv_ref, left_ref, right_ref, low_left_ref, low_right_ref, mask_ref, spread_ref, place_ref, w1_ref, vwin_ref, preh_ref, h_ref, h_all_ref, h_last_ref):
    seen = mask_ref[0:1]
    to_vol = place_ref[0]
    y = to_lanes(main_ref[0:64], spread_ref) + dot(rims_of(low_left_ref, low_right_ref), to_vol)
    fill_full(vwin_ref, y * flag(lax.axis_index("row") > 0), 0, 1)
    fill_full(vwin_ref, yv_ref[...].astype(F32) + dot(rims_of(left_ref, right_ref), to_vol), 1, 4)
    w1 = w1_ref[...]
    for pr, pd, pc in PAIRS:
        col = vwin_ref[2 * pd : 2 * pd + 3, 2 * pr : 2 * pr + 3, 2 * pc : 2 * pc + 3].reshape(432, LANES)
        pre = dot(w1, col)
        preh_ref[pr, pd, pc] = pre
        h_ref[pr, pd, pc] = (pre * sigmoid(pre) * seen).astype(BF)
    for pr in range(2):
        h_all_ref[pr] = packed([h_ref[pr, pd, pc].astype(F32) for pd in range(2) for pc in range(2)])
    h_last_ref[...] = h_all_ref[1]


def cotangent_kernel(main_ref, yc_ref, left_ref, right_ref, low_left_ref, low_right_ref, spread_ref, place_ref, w4_ref, cwin_ref, pull_ref):
    to_cot = place_ref[1]
    y = to_lanes(main_ref[64:128], spread_ref) + dot(rims_of(low_left_ref, low_right_ref), to_cot)
    fill_full(cwin_ref, y * flag(lax.axis_index("row") > 0), 0, 1)
    fill_full(cwin_ref, yc_ref[...].astype(F32) + dot(rims_of(left_ref, right_ref), to_cot), 1, 4)
    w4 = w4_ref[...]
    for p, (pr, pd, pc) in enumerate(PAIRS):
        col = cwin_ref[2 * pd : 2 * pd + 3, 2 * pr : 2 * pr + 3, 2 * pc : 2 * pc + 3].reshape(432, LANES)
        pull_ref[p] = dot(w4, col)


def middle_kernel(h_ref, hlo_ref, hhi_ref, pull_ref, mask_ref, w2_ref, up3_ref, hwin_ref, preq_ref, q_ref, m_ref, gm_ref, gm_all_ref, gm_last_ref):
    seen = mask_ref[0:1]
    seen_next = mask_ref[1:2]
    own = mask_ref[2:3]
    inner = flag(lax.axis_index("row") > 0)
    for pd in range(2):
        for pc in range(2):
            phase = 2 * pd + pc
            put_half(hwin_ref, 0, pd, pc, unpacked(hlo_ref[...].astype(F32), phase) * inner)
            for pr in range(2):
                put_half(hwin_ref, 1 + pr, pd, pc, h_ref[pr, pd, pc].astype(F32))
                put_half(hwin_ref, 3 + pr, pd, pc, unpacked(hhi_ref[pr].astype(F32), phase) * seen_next)
    quarters = []
    for qr in range(2):
        col = hwin_ref[:, 2 * qr : 2 * qr + 3].reshape(864, LANES)
        pre = dot(w2_ref[...], col)
        preq_ref[qr] = pre
        quarters.append(rounded(pre * sigmoid(pre)) * (seen_next if qr else seen))
    q_ref[...] = (quarters[0] * own).astype(BF)
    up = dot(up3_ref[...], neighbours(quarters[0], quarters[1]))
    for p, (pr, pd, pc) in enumerate(PAIRS):
        pre = up[p * 32 : p * 32 + 32] + h_ref[pr, pd, pc].astype(F32)
        m_ref[p] = (rounded(pre * sigmoid(pre)) * own).astype(BF)
        gm = rounded(pull_ref[p] * slope(pre)) * seen
        gm_ref[pr, pd, pc] = gm.astype(BF)
    for pr in range(2):
        gm_all_ref[pr] = packed([gm_ref[pr, pd, pc].astype(F32) for pd in range(2) for pc in range(2)])
    gm_last_ref[...] = gm_all_ref[1]


def full_grad_kernel(cwin_ref, m_ref, out_ref):
    total = None
    for p, (pr, pd, pc) in enumerate(PAIRS):
        col = cwin_ref[2 * pd : 2 * pd + 3, 2 * pr : 2 * pr + 3, 2 * pc : 2 * pc + 3].reshape(432, LANES)
        part = dot_nt(col, m_ref[p])
        total = part if total is None else total + part
    store_groups(out_ref, total, 0, 112, 32)


def store_groups(out_ref, total, base, rows, width):
    size = total.shape[0]
    for group in range(128 // width):
        low, high = group * rows, min((group + 1) * rows, size)
        out_ref[base : base + high - low, group * width : (group + 1) * width] = total[low:high]
        if high - low < rows:
            out_ref[base + high - low : base + rows, group * width : (group + 1) * width] = jnp.zeros((rows - high + low, width), F32)


def put_upper(win_ref, pd, pc, value):
    win_ref[pd, pc] = value.astype(BF)
    if pc == 0:
        right = roll_up(value, -1)
        win_ref[pd, 2] = right.astype(BF)
    if pd == 0:
        win_ref[2, pc] = roll_up(value, -SPAN).astype(BF)
        if pc == 0:
            win_ref[2, 2] = roll_up(right, -SPAN).astype(BF)


def backward_kernel(stage, gm_ref, gmlo_ref, gmhi_ref, vwin_ref, hwin_ref, preh_ref, preq_ref, q_ref, g4_ref, mask_ref, w3_ref, up2_ref, ewin_ref, gh_first_ref, pack_ref, send_ref, mwin_ref):
    seen = mask_ref[0:1]
    seen_next = mask_ref[1:2]
    own = mask_ref[2:3]
    inner = flag(lax.axis_index("row") > 0)
    for pd in range(2):
        for pc in range(2):
            phase = 2 * pd + pc
            put_half(mwin_ref, 0, pd, pc, unpacked(gmlo_ref[...].astype(F32), phase) * inner)
            for pr in range(2):
                put_half(mwin_ref, 1 + pr, pd, pc, gm_ref[pr, pd, pc].astype(F32))
                put_half(mwin_ref, 3 + pr, pd, pc, unpacked(gmhi_ref[pr].astype(F32), phase))
    quarters = []
    for qr in range(2):
        col = mwin_ref[:, 2 * qr : 2 * qr + 3].reshape(864, LANES)
        gq = rounded(dot(w3_ref[...], col) * slope(preq_ref[qr])) * (seen_next if qr else seen)
        quarters.append(gq)
        if qr == 0:
            store_groups(pack_ref, dot_nt(col, q_ref[...]), 672, 448, 64)
    up = dot(up2_ref[...], neighbours(quarters[0], quarters[1]))
    total = None
    first_row = []
    for p, (pr, pd, pc) in enumerate(PAIRS):
        conv = up[p * 32 : p * 32 + 32]
        gm = mwin_ref[1 + pd, 1 + pr, 1 + pc].astype(F32)
        gh = rounded((conv + gm) * slope(preh_ref[pr, pd, pc])) * seen
        put_upper(ewin_ref.at[:, pr], pd, pc, gh)
        if pr == 0:
            first_row.append(gh)
        col = vwin_ref[2 * pd : 2 * pd + 3, 2 * pr : 2 * pr + 3, 2 * pc : 2 * pc + 3].reshape(432, LANES)
        part = dot_nt(col, (gh * own).astype(BF))
        total = part if total is None else total + part
    gh_first_ref[...] = packed(first_row)
    store_groups(pack_ref, total, 0, 112, 32)
    pack_ref[112:224] = g4_ref[...]
    col = hwin_ref[:, 0:3].reshape(864, LANES)
    store_groups(pack_ref, dot_nt(col, (quarters[0] * own).astype(BF)), 224, 448, 64)
    pack_ref[1120:PACK] = jnp.zeros((PACK - 1120, 128), F32)
    send_ref[...] = half(pack_ref, stage, False)[...].astype(BF)


def volume_kernel(ewin_ref, next_ref, cwin_ref, up1_ref, spread_ref, order_ref, out_ref, z_ref, ext_ref):
    below = flag(lax.axis_index("row") < lax.axis_size("row") - 1)
    for pd in range(2):
        for pc in range(2):
            put_upper(ext_ref, pd, pc, unpacked(next_ref[...].astype(F32), 2 * pd + pc) * below)
    up1 = up1_ref[...]
    for pr, pd, pc in PAIRS:
        near = jnp.concatenate(
            [
                ewin_ref[pd + nd, pr + nr, pc + nc] if pr + nr < 2 else ext_ref[pd + nd, pc + nc]
                for nr, nd, nc in PAIRS
            ],
            axis=0,
        )
        up = dot(up1, near)
        for f, (fr, fd, fc) in enumerate(PAIRS):
            r, d, c = 2 * pr + fr, 2 * pd + fd, 2 * pc + fc
            value = up[f * 16 : f * 16 + 16] + cwin_ref[1 + d, 1 + r, 1 + c].astype(F32)
            z_ref[r * 64 + d * 16 : r * 64 + d * 16 + 16, c * LANES : (c + 1) * LANES] = value.astype(BF)
    early = jnp.concatenate([z_ref[:, c * LANES : c * LANES + 256] for c in range(4)], axis=1)
    late = jnp.concatenate([z_ref[:, c * LANES + 128 : (c + 1) * LANES] for c in range(4)], axis=1)
    wide = jnp.concatenate([dot_nt(early, spread_ref[0:768]), dot_nt(late, spread_ref[768:1024])], axis=1).astype(BF)
    wide = lax.dot_general(order_ref[...], wide, (((0,), (0,)), ((), ())), preferred_element_type=F32).astype(BF)
    for d in range(QD):
        out_ref[:, d] = wide[:, d * 128 : (d + 1) * 128].reshape(16, 16, 128)


def side_of(axis, step):
    return jnp.where((lax.axis_index(axis) & step) != 0, 1, 0)


def half(ref, stage, mine):
    count = ref.shape[0] // 2
    side = side_of(*stage)
    return ref.at[pl.ds(pl.multiple_of((side if mine else 1 - side) * count, 16), count)]


def fold_kernel(stage, kept_ref, got_ref, out_ref):
    out_ref[...] = (half(kept_ref, stage, True)[...] + got_ref[...].astype(F32)).astype(BF)


def sum_kernel(terms, copies, x_ref, out_ref):
    size = x_ref.shape[0] // terms
    total = jnp.sum(x_ref[...].astype(F32).reshape(terms, size, 128), axis=0, keepdims=True)
    out_ref[...] = jnp.broadcast_to(total, (copies, size, 128)).reshape(copies * size, 128).astype(BF)


def finish_kernel(scale, stage, own_ref, got_ref, g1_ref, g2_ref, g3_ref, g4_ref, full_ref):
    half(full_ref, stage, True)[...] = own_ref[...].astype(F32)
    half(full_ref, stage, False)[...] = got_ref[...].astype(F32)
    for ref, base, rows, width in ((g1_ref, 0, 112, 32), (g4_ref, 112, 112, 32), (g2_ref, 224, 448, 64), (g3_ref, 672, 448, 64)):
        small = ref.shape[1]
        taps = rows // small
        back = ref is g3_ref or ref is g4_ref
        for group in range(128 // width):
            count = min(taps, 27 - group * taps)
            block = full_ref[base : base + count * small, group * width : (group + 1) * width] * scale
            block = block.reshape(count, small, width)
            if back:
                for t in range(count):
                    ref[26 - group * taps - t] = block[t]
            else:
                ref[group * taps : group * taps + count] = block


def call(kernel, outs, scratch=(), flops=0, far=None, name=None):
    shapes = [jax.ShapeDtypeStruct(shape, dtype) for shape, dtype in outs]
    specs = {}
    if far:
        specs["in_specs"] = [pl.BlockSpec(memory_space=pltpu.HBM)] * far[0] + [pl.BlockSpec(memory_space=pltpu.VMEM)] * far[1]
    return pl.pallas_call(
        kernel,
        out_shape=shapes,
        scratch_shapes=list(scratch),
        **specs,
        compiler_params=pltpu.CompilerParams(vmem_limit_bytes=LIMIT),
        cost_estimate=pl.CostEstimate(flops=flops, bytes_accessed=4000000, transcendentals=0),
        name=name,
    )


def swapped(value, row_step, col_step):
    rows, cols = lax.axis_size("row"), lax.axis_size("col")
    pairs = [(r * cols + c, (r ^ row_step) * cols + (c ^ col_step)) for r in range(rows) for c in range(cols)]
    return lax.ppermute(value, ("row", "col"), pairs)


def shifted(value, axis, steps):
    count = lax.axis_size(axis)
    return lax.ppermute(value, axis, [(i, (i + steps) % count) for i in range(count)])


def diagonal(value, row_step, col_step):
    rows, cols = lax.axis_size("row"), lax.axis_size("col")
    pairs = [(r * cols + c, (r + row_step) % rows * cols + (c + col_step) % cols) for r in range(rows) for c in range(cols)]
    return lax.ppermute(value, ("row", "col"), pairs)


def exchanged(value, row_bits, col_bits):
    rows, cols = lax.axis_size("row"), lax.axis_size("col")
    if not row_bits and not col_bits:
        return value
    groups = {}
    for r in range(rows):
        for c in range(cols):
            groups.setdefault((r & ~row_bits, c & ~col_bits), []).append(r * cols + c)
    return lax.all_to_all(value, ("row", "col"), 0, 0, axis_index_groups=list(groups.values()), tiled=True)


def held(value):
    return pltpu.with_memory_space_constraint(value, pltpu.HBM)


def by_tap(weight, swap):
    order = (2, 3, 4, 1, 0) if swap else (2, 3, 4, 0, 1)
    moved = weight.transpose(order)
    return moved.reshape((27,) + moved.shape[3:])


def from_tap(grad, swap):
    cube = grad.reshape((3, 3, 3) + grad.shape[1:])
    return cube.transpose((4, 3, 0, 1, 2) if swap else (3, 4, 0, 1, 2))


def shards(volume, cotangent, w_half, w_quarter, w_back_half, w_back_full):
    rows, cols = lax.axis_size("row"), lax.axis_size("col")
    cells = volume.size // volume.shape[0] * rows * cols
    scale = 1.0 / math.sqrt(cells)
    spread, rims, place, order = call(
        tables_kernel,
        [((QD * 128, 1024), BF), ((QD * 128, 128), BF), ((2, 256, 4 * LANES), BF), ((256, 256), BF)],
        name="tables",
    )()
    vol = volume.reshape(16, QD, 16, 128)
    cot = cotangent.reshape(16, QD, 16, 128)
    vol_rows, cot_rows, main, first, last, first_low, last_low = call(
        edge_kernel,
        [((256, 1024), BF), ((256, 1024), BF), ((128, 1024), BF), ((256, 128), BF), ((256, 128), BF), ((64, 128), BF), ((64, 128), BF)],
        [pltpu.VMEM(vol.shape, BF), pltpu.VMEM(cot.shape, BF), pltpu.SemaphoreType.DMA((2,))],
        far=(2, 2),
        name="edge",
    )(held(vol), held(cot), order, rims)
    main_lo = shifted(main, "row", 1)
    edges = [shifted(last, "col", 1), shifted(first, "col", -1), diagonal(last_low, 1, 1), diagonal(first_low, 1, -1)]
    yv, yc = call(own_kernel, [((256, 4 * LANES), BF), ((256, 4 * LANES), BF)], flops=2 * 256 * 1024 * 4000, name="own")(vol_rows, cot_rows, spread)
    weights = by_tap(w_half, True), by_tap(w_quarter, True), by_tap(w_back_half, False), by_tap(w_back_full, False)
    w1, w2, w3, w4, up1, up2, up3, mask = call(
        prepare_kernel,
        [((32, 432), BF), ((64, 864), BF), ((64, 864), BF), ((32, 432), BF), ((128, 256), BF), ((256, 512), BF), ((256, 512), BF), ((8, LANES), F32)],
        [pltpu.VMEM(weight.shape, BF) for weight in weights] + [pltpu.SemaphoreType.DMA((4,))],
        far=(4, 0),
        name="prepare",
    )(*[held(weight) for weight in weights])
    full_window, half_rows = (5, 5, 5, 16, LANES), (2, 2, 2, 32, LANES)
    vwin, preh, half_act, half_all, half_last = call(
        half_kernel,
        [(full_window, BF), (half_rows, F32), (half_rows, BF), ((2, 32, 1152), BF), ((32, 1152), BF)],
        name="half",
    )(main_lo, yv, *edges, mask, spread, place, w1)
    half_lo, half_hi = shifted(half_last, "row", 1), shifted(half_all, "row", -1)
    cwin, pull = call(
        cotangent_kernel, [(full_window, BF), ((8, 32, LANES), F32)], flops=2 * 432 * 32 * LANES * 64, name="cotangent"
    )(main_lo, yc, *edges, spread, place, w4)
    hwin, preq, quarter, mixed, gm, gm_all, gm_last = call(
        middle_kernel,
        [((3, 5, 3, 32, LANES), BF), ((2, 64, LANES), F32), ((64, LANES), BF), ((8, 32, LANES), BF), (half_rows, BF), ((2, 32, 1152), BF), ((32, 1152), BF)],
        name="middle",
    )(half_act, half_lo, half_hi, pull, mask, w2, up3)
    gm_lo, gm_hi = shifted(gm_last, "row", 1), shifted(gm_all, "row", -1)
    (g4,) = call(full_grad_kernel, [((112, 128), F32)], flops=2 * 432 * 32 * LANES * 64, name="full_grad")(cwin, mixed)
    core = ("col", 1)
    ewin, gh_first, kept, send = call(
        functools.partial(backward_kernel, core),
        [((3, 2, 3, 32, LANES), BF), ((32, 1152), BF), ((PACK, 128), F32), ((PACK // 2, 128), BF)],
        [pltpu.VMEM((3, 5, 3, 32, LANES), BF)],
        name="backward",
    )(gm, gm_lo, gm_hi, vwin, hwin, preh, preq, quarter, g4, mask, w3, up2)
    (part,) = call(functools.partial(fold_kernel, core), [((PACK // 2, 128), BF)], name="fold")(kept, swapped(send, 0, 1))
    gh_next = shifted(gh_first, "row", -1)
    along = [(7 & (rows - 1), 2 & (cols - 1)), (0, 28 & (cols - 1))]
    sizes = [2 ** (r.bit_count() + c.bit_count()) for r, c in along]
    share = PACK // 2 // sizes[0]
    for bits, size, later in zip(along, sizes, sizes[::-1]):
        part = exchanged(part.reshape(size, share, 128), *bits).reshape(size * share, 128)
        (part,) = call(functools.partial(sum_kernel, size, later), [((later * share, 128), BF)], name="sum")(part)
    part, gh_next = lax.optimization_barrier((part, gh_next))
    part = exchanged(part.reshape(sizes[0], share, 128), *along[0]).reshape(PACK // 2, 128)
    (grad_volume,) = call(
        volume_kernel, [((16, QD, 16, 128), BF)], [pltpu.VMEM((256, 4 * LANES), BF), pltpu.VMEM((3, 3, 32, LANES), BF)], flops=2 * 256 * 1024 * 4000, name="volume"
    )(ewin, gh_next, cwin, up1, spread, order)
    part, grad_volume = lax.optimization_barrier((part, grad_volume))
    g1, g2, g3, g4 = call(
        functools.partial(finish_kernel, scale, core),
        [((27, 16, 32), F32), ((27, 32, 64), F32), ((27, 32, 64), F32), ((27, 16, 32), F32)],
        [pltpu.VMEM((PACK, 128), F32)],
        name="finish",
    )(part, swapped(part, 0, 1))
    return (
        grad_volume.reshape(volume.shape),
        from_tap(g1, True),
        from_tap(g2, True),
        from_tap(g3, False),
        from_tap(g4, False),
    )


def solution(mesh):
    return jax.shard_map(
        shards,
        mesh=mesh,
        in_specs=(P(None, None, "row", "col"), P(None, None, "row", "col"), P(), P(), P(), P()),
        out_specs=(P(None, None, "row", "col"), P(), P(), P(), P()),
        check_vma=False,
    )
```

```python
import functools
import math

import jax
import jax.numpy as jnp
from jax import lax
from jax.experimental import pallas as pl
from jax.experimental.pallas import tpu as pltpu
from jax.sharding import PartitionSpec as P

BF = jnp.bfloat16
F32 = jnp.float32

QD, QC, HALO = 8, 32, 2
SPAN = QC + 2 * HALO
LANES = 384
PACK = 1280
LIMIT = 24 * 1024 * 1024


def lane_of(d, c):
    return SPAN * d + c + HALO


def iota(shape, dim):
    return lax.broadcasted_iota(jnp.int32, shape, dim)


def ones_where(condition):
    return jnp.where(condition, 1.0, 0.0).astype(BF)


def lane_tables(spread_ref, place_ref):
    w, lane = iota((128, 256), 0), iota((128, 256), 1)
    for phase in range(4):
        apart = jnp.where((w & 3) == phase, lane - (w >> 2), -LANES)
        for d in range(QD):
            block = ones_where(apart == lane_of(d, 0) - (0 if d < 6 else 128))
            spread_ref[d * 128 : (d + 1) * 128, phase * 256 : (phase + 1) * 256] = block
    place_ref[...] = jnp.zeros(place_ref.shape, BF)
    slot, lane = iota((16, LANES), 0), iota((16, LANES), 1)
    for side in range(2):
        block = ones_where(lane == SPAN * (slot >> 1) + HALO + (slot & 1) + (QC if side else -2))
        for array in range(2):
            for phase in range(4):
                row = side * 128 + array * 64 + phase * 16
                place_ref[array, row : row + 16, phase * LANES : (phase + 1) * LANES] = block


def row_tables(rims_ref, order_ref):
    slot, row = iota((QD * 128, 128), 1), iota((QD * 128, 128), 0)
    column = (slot & 1) + jnp.where(slot >= 64, QC - 2, 0)
    rims_ref[...] = ones_where(row == ((slot >> 1) & 7) * 128 + 4 * column + ((slot >> 4) & 3))
    row, column = iota((256, 256), 0), iota((256, 256), 1)
    order_ref[...] = ones_where(column == (row & 15) * 16 + ((row >> 4) & 3) * 4 + (row >> 6))


def dot(a, b):
    return lax.dot_general(a, b, (((1,), (0,)), ((), ())), preferred_element_type=F32)


def dot_nt(a, b):
    return lax.dot_general(a, b, (((1,), (1,)), ((), ())), preferred_element_type=F32)


def sigmoid(t):
    return 1.0 / (1.0 + jnp.exp(-t))


def slope(t):
    s = sigmoid(t)
    return s * (1.0 + t * (1.0 - s))


def by_rows(x_ref, order_ref):
    wide = jnp.concatenate([x_ref[:, d].reshape(256, 128) for d in range(QD)], axis=1)
    return dot(order_ref[...], wide).astype(BF)


def to_lanes(rows, spread_ref):
    early = dot(rows[:, :768], spread_ref[0:768])
    late = dot(rows[:, 768:], spread_ref[768:1024])
    pieces = []
    for pc in range(4):
        low, high = pc * 256, pc * 256 + 128
        pieces += [early[:, low:high], early[:, high : low + 256] + late[:, low:high], late[:, high : low + 256]]
    return jnp.concatenate(pieces, axis=1)


def fetch(pairs, sems):
    copies = [pltpu.make_async_copy(source, target, sems.at[i]) for i, (source, target) in enumerate(pairs)]
    for copy in copies:
        copy.start()
    return copies


def edge_kernel(vol_ref, cot_ref, order_ref, vol_rows_ref, cot_rows_ref, main_ref, first_ref, last_ref, first_low_ref, last_low_ref, vol_here, cot_here, rims_ref, sems):
    copies = fetch(((vol_ref, vol_here), (cot_ref, cot_here)), sems)
    row_tables(rims_ref, order_ref)
    edges = []
    for i, (here, rows_ref) in enumerate(((vol_here, vol_rows_ref), (cot_here, cot_rows_ref))):
        copies[i].wait()
        rows = by_rows(here, order_ref)
        rows_ref[...] = rows
        main_ref[i * 64 : i * 64 + 64] = rows[192:256]
        edges.append(dot(rows, rims_ref[...]))
    first_ref[...] = jnp.concatenate([edge[:, :64] for edge in edges], axis=1).astype(BF)
    last_ref[...] = jnp.concatenate([edge[:, 64:] for edge in edges], axis=1).astype(BF)
    first_low_ref[...] = first_ref[192:256]
    last_low_ref[...] = last_ref[192:256]


def own_kernel(vol_rows_ref, cot_rows_ref, yv_ref, yc_ref, spread_ref, place_ref):
    lane_tables(spread_ref, place_ref)
    yv_ref[...] = to_lanes(vol_rows_ref[...], spread_ref).astype(BF)
    yc_ref[...] = to_lanes(cot_rows_ref[...], spread_ref).astype(BF)


def flag(condition):
    return jnp.where(condition, 1.0, 0.0).astype(F32)


def rims_of(left_ref, right_ref):
    left = left_ref[...].astype(F32) * flag(lax.axis_index("col") > 0)
    return jnp.concatenate([left.astype(BF), right_ref[...]], axis=1)


UP_TAP = {(0, 0): 1, (1, 0): 0, (1, 1): 2}
PAIRS = [(a, b, c) for a in range(2) for b in range(2) for c in range(2)]


def write_masks(mask_ref):
    lane = lax.broadcasted_iota(jnp.int32, (1, LANES), 1)
    c = lane
    for d in range(1, QD):
        c = jnp.where(lane >= d * SPAN, lane - d * SPAN, c)
    c = c - HALO
    inside = lane < QD * SPAN
    last_col = lax.axis_index("col") == lax.axis_size("col") - 1
    last_row = lax.axis_index("row") == lax.axis_size("row") - 1
    bound = jnp.where(last_col, QC, LANES)
    seen = jnp.where(inside & (c < bound), 1.0, 0.0).astype(F32)
    mask_ref[...] = jnp.zeros(mask_ref.shape, F32)
    mask_ref[0:1] = seen
    mask_ref[1:2] = seen * jnp.where(last_row, 0.0, 1.0)
    mask_ref[2:3] = jnp.where(inside & (c >= 0) & (c < QC), 1.0, 0.0).astype(F32)


def prepare_kernel(*refs):
    sources, outs, here, sems = refs[0:4], refs[4:12], refs[12:16], refs[16]
    copies = fetch(list(zip(sources, here)), sems)
    write_masks(outs[7])
    for copy in copies:
        copy.wait()
    wh_ref, wq_ref, wbh_ref, wbf_ref = here
    w1_ref, w2_ref, w3_ref, w4_ref, up1_ref, up2_ref, up3_ref = outs[:7]
    for ref, out, eye, back in ((wh_ref, w1_ref, 32, False), (wq_ref, w2_ref, 64, False), (wbh_ref, w3_ref, 64, True), (wbf_ref, w4_ref, 32, True)):
        small, large = ref.shape[1], ref.shape[2]
        if back:
            flat = jnp.concatenate([ref[26 - k] for k in range(27)], axis=0)
        else:
            flat = ref[...].reshape(27 * small, large)
        rows = lax.broadcasted_iota(jnp.int32, (eye, eye), 0)
        cols = lax.broadcasted_iota(jnp.int32, (eye, eye), 1)
        unit = jnp.where(rows == cols, 1.0, 0.0).astype(BF)
        out[...] = dot_nt(unit, flat).astype(BF)
    for ref, out, back in ((wh_ref, up1_ref, True), (wq_ref, up2_ref, True), (wbh_ref, up3_ref, False)):
        small, large = ref.shape[1], ref.shape[2]
        out[...] = jnp.zeros(out.shape, BF)
        for p, (pr, pd, pc) in enumerate(PAIRS):
            for n, (nr, nd, nc) in enumerate(PAIRS):
                taps = [UP_TAP.get(key) for key in ((pd, nd), (pr, nr), (pc, nc))]
                if None in taps:
                    continue
                j = taps[0] * 9 + taps[1] * 3 + taps[2]
                out[p * small : (p + 1) * small, n * large : (n + 1) * large] = ref[26 - j if back else j]


def roll_up(x, steps):
    return pltpu.roll(x, steps % LANES, x.ndim - 1)


def fill_full(win_ref, y, base, count):
    pieces = [y[:, pc * LANES : (pc + 1) * LANES] for pc in range(4)]
    pieces = [roll_up(pieces[3], 1)] + pieces
    for c in range(5):
        piece = pieces[c].reshape(count, 4, 16, LANES)
        for pd in range(4):
            win_ref[1 + pd, base : base + count, c] = piece[:, pd].astype(BF)
        last = piece[:, 3].reshape(count * 16, LANES)
        win_ref[0, base : base + count, c] = roll_up(last, SPAN).reshape(count, 16, LANES).astype(BF)


def put_half(win_ref, row, pd, pc, value):
    win_ref[1 + pd, row, 1 + pc] = value.astype(BF)
    if pc == 1:
        left = roll_up(value, 1)
        win_ref[1 + pd, row, 0] = left.astype(BF)
    if pd == 1:
        above = roll_up(value, SPAN)
        win_ref[0, row, 1 + pc] = above.astype(BF)
        if pc == 1:
            win_ref[0, row, 0] = roll_up(left, SPAN).astype(BF)


def packed(values):
    tails = [pltpu.roll(value[:, 256:], 32 * i, 1) if i else value[:, 256:] for i, value in enumerate(values)]
    tail = (tails[0] + tails[1]) + (tails[2] + tails[3])
    return jnp.concatenate([value[:, :256] for value in values] + [tail], axis=1).astype(BF)


def unpacked(value, i):
    tail = value[:, 1024:]
    tail = pltpu.roll(tail, 128 - 32 * i, 1) if i else tail
    tail = jnp.where(iota(tail.shape, 1) < 32, tail, 0.0)
    return jnp.concatenate([value[:, 256 * i : 256 * i + 256], tail], axis=1)


def rounded(value):
    return value.astype(BF).astype(F32)


def neighbours(low, high):
    parts = []
    for value in (low, high):
        for nd in range(2):
            moved = roll_up(value, -SPAN) if nd else value
            parts.append(moved.astype(BF))
            parts.append(roll_up(moved, -1).astype(BF))
    return jnp.concatenate(parts, axis=0)


def half_kernel(main_ref, yv_ref, left_ref, right_ref, low_left_ref, low_right_ref, mask_ref, spread_ref, place_ref, w1_ref, vwin_ref, preh_ref, h_ref, h_all_ref, h_last_ref):
    seen = mask_ref[0:1]
    to_vol = place_ref[0]
    y = to_lanes(main_ref[0:64], spread_ref) + dot(rims_of(low_left_ref, low_right_ref), to_vol)
    fill_full(vwin_ref, y * flag(lax.axis_index("row") > 0), 0, 1)
    fill_full(vwin_ref, yv_ref[...].astype(F32) + dot(rims_of(left_ref, right_ref), to_vol), 1, 4)
    w1 = w1_ref[...]
    for pr, pd, pc in PAIRS:
        col = vwin_ref[2 * pd : 2 * pd + 3, 2 * pr : 2 * pr + 3, 2 * pc : 2 * pc + 3].reshape(432, LANES)
        pre = dot(w1, col)
        preh_ref[pr, pd, pc] = pre
        h_ref[pr, pd, pc] = (pre * sigmoid(pre) * seen).astype(BF)
    for pr in range(2):
        h_all_ref[pr] = packed([h_ref[pr, pd, pc].astype(F32) for pd in range(2) for pc in range(2)])
    h_last_ref[...] = h_all_ref[1]


def cotangent_kernel(main_ref, yc_ref, left_ref, right_ref, low_left_ref, low_right_ref, spread_ref, place_ref, w4_ref, cwin_ref, pull_ref):
    to_cot = place_ref[1]
    y = to_lanes(main_ref[64:128], spread_ref) + dot(rims_of(low_left_ref, low_right_ref), to_cot)
    fill_full(cwin_ref, y * flag(lax.axis_index("row") > 0), 0, 1)
    fill_full(cwin_ref, yc_ref[...].astype(F32) + dot(rims_of(left_ref, right_ref), to_cot), 1, 4)
    w4 = w4_ref[...]
    for p, (pr, pd, pc) in enumerate(PAIRS):
        col = cwin_ref[2 * pd : 2 * pd + 3, 2 * pr : 2 * pr + 3, 2 * pc : 2 * pc + 3].reshape(432, LANES)
        pull_ref[p] = dot(w4, col)


def middle_kernel(h_ref, hlo_ref, hhi_ref, pull_ref, mask_ref, w2_ref, up3_ref, hwin_ref, preq_ref, q_ref, m_ref, gm_ref, gm_all_ref, gm_last_ref):
    seen = mask_ref[0:1]
    seen_next = mask_ref[1:2]
    own = mask_ref[2:3]
    inner = flag(lax.axis_index("row") > 0)
    for pd in range(2):
        for pc in range(2):
            phase = 2 * pd + pc
            put_half(hwin_ref, 0, pd, pc, unpacked(hlo_ref[...].astype(F32), phase) * inner)
            for pr in range(2):
                put_half(hwin_ref, 1 + pr, pd, pc, h_ref[pr, pd, pc].astype(F32))
                put_half(hwin_ref, 3 + pr, pd, pc, unpacked(hhi_ref[pr].astype(F32), phase) * seen_next)
    quarters = []
    for qr in range(2):
        col = hwin_ref[:, 2 * qr : 2 * qr + 3].reshape(864, LANES)
        pre = dot(w2_ref[...], col)
        preq_ref[qr] = pre
        quarters.append(rounded(pre * sigmoid(pre)) * (seen_next if qr else seen))
    q_ref[...] = (quarters[0] * own).astype(BF)
    up = dot(up3_ref[...], neighbours(quarters[0], quarters[1]))
    for p, (pr, pd, pc) in enumerate(PAIRS):
        pre = up[p * 32 : p * 32 + 32] + h_ref[pr, pd, pc].astype(F32)
        m_ref[p] = (rounded(pre * sigmoid(pre)) * own).astype(BF)
        gm = rounded(pull_ref[p] * slope(pre)) * seen
        gm_ref[pr, pd, pc] = gm.astype(BF)
    for pr in range(2):
        gm_all_ref[pr] = packed([gm_ref[pr, pd, pc].astype(F32) for pd in range(2) for pc in range(2)])
    gm_last_ref[...] = gm_all_ref[1]


def full_grad_kernel(cwin_ref, m_ref, out_ref):
    total = None
    for p, (pr, pd, pc) in enumerate(PAIRS):
        col = cwin_ref[2 * pd : 2 * pd + 3, 2 * pr : 2 * pr + 3, 2 * pc : 2 * pc + 3].reshape(432, LANES)
        part = dot_nt(col, m_ref[p])
        total = part if total is None else total + part
    store_groups(out_ref, total, 0, 112, 32)


def store_groups(out_ref, total, base, rows, width):
    size = total.shape[0]
    for group in range(128 // width):
        low, high = group * rows, min((group + 1) * rows, size)
        out_ref[base : base + high - low, group * width : (group + 1) * width] = total[low:high]
        if high - low < rows:
            out_ref[base + high - low : base + rows, group * width : (group + 1) * width] = jnp.zeros((rows - high + low, width), F32)


def put_upper(win_ref, pd, pc, value):
    win_ref[pd, pc] = value.astype(BF)
    if pc == 0:
        right = roll_up(value, -1)
        win_ref[pd, 2] = right.astype(BF)
    if pd == 0:
        win_ref[2, pc] = roll_up(value, -SPAN).astype(BF)
        if pc == 0:
            win_ref[2, 2] = roll_up(right, -SPAN).astype(BF)


def backward_kernel(stage, gm_ref, gmlo_ref, gmhi_ref, vwin_ref, hwin_ref, preh_ref, preq_ref, q_ref, g4_ref, mask_ref, w3_ref, up2_ref, ewin_ref, gh_first_ref, pack_ref, send_ref, mwin_ref):
    seen = mask_ref[0:1]
    seen_next = mask_ref[1:2]
    own = mask_ref[2:3]
    inner = flag(lax.axis_index("row") > 0)
    for pd in range(2):
        for pc in range(2):
            phase = 2 * pd + pc
            put_half(mwin_ref, 0, pd, pc, unpacked(gmlo_ref[...].astype(F32), phase) * inner)
            for pr in range(2):
                put_half(mwin_ref, 1 + pr, pd, pc, gm_ref[pr, pd, pc].astype(F32))
                put_half(mwin_ref, 3 + pr, pd, pc, unpacked(gmhi_ref[pr].astype(F32), phase))
    quarters = []
    for qr in range(2):
        col = mwin_ref[:, 2 * qr : 2 * qr + 3].reshape(864, LANES)
        gq = rounded(dot(w3_ref[...], col) * slope(preq_ref[qr])) * (seen_next if qr else seen)
        quarters.append(gq)
        if qr == 0:
            store_groups(pack_ref, dot_nt(col, q_ref[...]), 672, 448, 64)
    up = dot(up2_ref[...], neighbours(quarters[0], quarters[1]))
    total = None
    first_row = []
    for p, (pr, pd, pc) in enumerate(PAIRS):
        conv = up[p * 32 : p * 32 + 32]
        gm = mwin_ref[1 + pd, 1 + pr, 1 + pc].astype(F32)
        gh = rounded((conv + gm) * slope(preh_ref[pr, pd, pc])) * seen
        put_upper(ewin_ref.at[:, pr], pd, pc, gh)
        if pr == 0:
            first_row.append(gh)
        col = vwin_ref[2 * pd : 2 * pd + 3, 2 * pr : 2 * pr + 3, 2 * pc : 2 * pc + 3].reshape(432, LANES)
        part = dot_nt(col, (gh * own).astype(BF))
        total = part if total is None else total + part
    gh_first_ref[...] = packed(first_row)
    store_groups(pack_ref, total, 0, 112, 32)
    pack_ref[112:224] = g4_ref[...]
    col = hwin_ref[:, 0:3].reshape(864, LANES)
    store_groups(pack_ref, dot_nt(col, (quarters[0] * own).astype(BF)), 224, 448, 64)
    pack_ref[1120:PACK] = jnp.zeros((PACK - 1120, 128), F32)
    send_ref[...] = half(pack_ref, stage, False)[...].astype(BF)


def volume_kernel(ewin_ref, next_ref, cwin_ref, up1_ref, spread_ref, order_ref, out_ref, z_ref, ext_ref):
    below = flag(lax.axis_index("row") < lax.axis_size("row") - 1)
    for pd in range(2):
        for pc in range(2):
            put_upper(ext_ref, pd, pc, unpacked(next_ref[...].astype(F32), 2 * pd + pc) * below)
    up1 = up1_ref[...]
    for pr, pd, pc in PAIRS:
        near = jnp.concatenate(
            [
                ewin_ref[pd + nd, pr + nr, pc + nc] if pr + nr < 2 else ext_ref[pd + nd, pc + nc]
                for nr, nd, nc in PAIRS
            ],
            axis=0,
        )
        up = dot(up1, near)
        for f, (fr, fd, fc) in enumerate(PAIRS):
            r, d, c = 2 * pr + fr, 2 * pd + fd, 2 * pc + fc
            value = up[f * 16 : f * 16 + 16] + cwin_ref[1 + d, 1 + r, 1 + c].astype(F32)
            z_ref[r * 64 + d * 16 : r * 64 + d * 16 + 16, c * LANES : (c + 1) * LANES] = value.astype(BF)
    early = jnp.concatenate([z_ref[:, c * LANES : c * LANES + 256] for c in range(4)], axis=1)
    late = jnp.concatenate([z_ref[:, c * LANES + 128 : (c + 1) * LANES] for c in range(4)], axis=1)
    wide = jnp.concatenate([dot_nt(early, spread_ref[0:768]), dot_nt(late, spread_ref[768:1024])], axis=1).astype(BF)
    wide = lax.dot_general(order_ref[...], wide, (((0,), (0,)), ((), ())), preferred_element_type=F32).astype(BF)
    for d in range(QD):
        out_ref[:, d] = wide[:, d * 128 : (d + 1) * 128].reshape(16, 16, 128)


def side_of(axis, step):
    return jnp.where((lax.axis_index(axis) & step) != 0, 1, 0)


def half(ref, stage, mine):
    count = ref.shape[0] // 2
    side = side_of(*stage)
    return ref.at[pl.ds(pl.multiple_of((side if mine else 1 - side) * count, 16), count)]


def fold_kernel(stage, kept_ref, got_ref, out_ref):
    out_ref[...] = (half(kept_ref, stage, True)[...] + got_ref[...].astype(F32)).astype(BF)


def sum_kernel(terms, copies, x_ref, out_ref):
    size = x_ref.shape[0] // terms
    total = jnp.sum(x_ref[...].astype(F32).reshape(terms, size, 128), axis=0, keepdims=True)
    out_ref[...] = jnp.broadcast_to(total, (copies, size, 128)).reshape(copies * size, 128).astype(BF)


def finish_kernel(scale, stage, own_ref, got_ref, g1_ref, g2_ref, g3_ref, g4_ref, full_ref):
    half(full_ref, stage, True)[...] = own_ref[...].astype(F32)
    half(full_ref, stage, False)[...] = got_ref[...].astype(F32)
    for ref, base, rows, width in ((g1_ref, 0, 112, 32), (g4_ref, 112, 112, 32), (g2_ref, 224, 448, 64), (g3_ref, 672, 448, 64)):
        small = ref.shape[1]
        taps = rows // small
        back = ref is g3_ref or ref is g4_ref
        for group in range(128 // width):
            count = min(taps, 27 - group * taps)
            block = full_ref[base : base + count * small, group * width : (group + 1) * width] * scale
            block = block.reshape(count, small, width)
            if back:
                for t in range(count):
                    ref[26 - group * taps - t] = block[t]
            else:
                ref[group * taps : group * taps + count] = block


def call(kernel, outs, scratch=(), flops=0, far=None, name=None):
    shapes = [jax.ShapeDtypeStruct(shape, dtype) for shape, dtype in outs]
    specs = {}
    if far:
        specs["in_specs"] = [pl.BlockSpec(memory_space=pltpu.HBM)] * far[0] + [pl.BlockSpec(memory_space=pltpu.VMEM)] * far[1]
    return pl.pallas_call(
        kernel,
        out_shape=shapes,
        scratch_shapes=list(scratch),
        **specs,
        compiler_params=pltpu.CompilerParams(vmem_limit_bytes=LIMIT),
        cost_estimate=pl.CostEstimate(flops=flops, bytes_accessed=4000000, transcendentals=0),
        name=name,
    )


def swapped(value, row_step, col_step):
    rows, cols = lax.axis_size("row"), lax.axis_size("col")
    pairs = [(r * cols + c, (r ^ row_step) * cols + (c ^ col_step)) for r in range(rows) for c in range(cols)]
    return lax.ppermute(value, ("row", "col"), pairs)


def shifted(value, axis, steps):
    count = lax.axis_size(axis)
    return lax.ppermute(value, axis, [(i, (i + steps) % count) for i in range(count)])


def tree_sum(terms):
    terms = [term.astype(F32) for term in terms]
    while len(terms) > 1:
        terms = [low + high for low, high in zip(terms[::2], terms[1::2])]
    return terms[0]


def diagonal(value, row_step, col_step):
    rows, cols = lax.axis_size("row"), lax.axis_size("col")
    pairs = [(r * cols + c, (r + row_step) % rows * cols + (c + col_step) % cols) for r in range(rows) for c in range(cols)]
    return lax.ppermute(value, ("row", "col"), pairs)


def exchanged(value, row_bits, col_bits):
    rows, cols = lax.axis_size("row"), lax.axis_size("col")
    if not row_bits and not col_bits:
        return value
    groups = {}
    for r in range(rows):
        for c in range(cols):
            groups.setdefault((r & ~row_bits, c & ~col_bits), []).append(r * cols + c)
    return lax.all_to_all(value, ("row", "col"), 0, 0, axis_index_groups=list(groups.values()), tiled=True)


def held(value):
    return pltpu.with_memory_space_constraint(value, pltpu.HBM)


def by_tap(weight, swap):
    order = (2, 3, 4, 1, 0) if swap else (2, 3, 4, 0, 1)
    moved = weight.transpose(order)
    return moved.reshape((27,) + moved.shape[3:])


def from_tap(grad, swap):
    cube = grad.reshape((3, 3, 3) + grad.shape[1:])
    return cube.transpose((4, 3, 0, 1, 2) if swap else (3, 4, 0, 1, 2))


def shards(volume, cotangent, w_half, w_quarter, w_back_half, w_back_full):
    rows, cols = lax.axis_size("row"), lax.axis_size("col")
    cells = volume.size // volume.shape[0] * rows * cols
    scale = 1.0 / math.sqrt(cells)
    vol = volume.reshape(16, QD, 16, 128)
    cot = cotangent.reshape(16, QD, 16, 128)
    order, vol_rows, cot_rows, main, first, last, first_low, last_low = call(
        edge_kernel,
        [((256, 256), BF), ((256, 1024), BF), ((256, 1024), BF), ((128, 1024), BF), ((256, 128), BF), ((256, 128), BF), ((64, 128), BF), ((64, 128), BF)],
        [pltpu.VMEM(vol.shape, BF), pltpu.VMEM(cot.shape, BF), pltpu.VMEM((QD * 128, 128), BF), pltpu.SemaphoreType.DMA((2,))],
        far=(2, 0),
        name="edge",
    )(held(vol), held(cot))
    main_lo = shifted(main, "row", 1)
    edges = [shifted(last, "col", 1), shifted(first, "col", -1), diagonal(last_low, 1, 1), diagonal(first_low, 1, -1)]
    yv, yc, spread, place = call(
        own_kernel,
        [((256, 4 * LANES), BF), ((256, 4 * LANES), BF), ((QD * 128, 1024), BF), ((2, 256, 4 * LANES), BF)],
        flops=2 * 256 * 1024 * 4000,
        name="own",
    )(vol_rows, cot_rows)
    weights = by_tap(w_half, True), by_tap(w_quarter, True), by_tap(w_back_half, False), by_tap(w_back_full, False)
    w1, w2, w3, w4, up1, up2, up3, mask = call(
        prepare_kernel,
        [((32, 432), BF), ((64, 864), BF), ((64, 864), BF), ((32, 432), BF), ((128, 256), BF), ((256, 512), BF), ((256, 512), BF), ((8, LANES), F32)],
        [pltpu.VMEM(weight.shape, BF) for weight in weights] + [pltpu.SemaphoreType.DMA((4,))],
        far=(4, 0),
        name="prepare",
    )(*[held(weight) for weight in weights])
    full_window, half_rows = (5, 5, 5, 16, LANES), (2, 2, 2, 32, LANES)
    vwin, preh, half_act, half_all, half_last = call(
        half_kernel,
        [(full_window, BF), (half_rows, F32), (half_rows, BF), ((2, 32, 1152), BF), ((32, 1152), BF)],
        name="half",
    )(main_lo, yv, *edges, mask, spread, place, w1)
    half_lo, half_hi = shifted(half_last, "row", 1), shifted(half_all, "row", -1)
    cwin, pull = call(
        cotangent_kernel, [(full_window, BF), ((8, 32, LANES), F32)], flops=2 * 432 * 32 * LANES * 64, name="cotangent"
    )(main_lo, yc, *edges, spread, place, w4)
    hwin, preq, quarter, mixed, gm, gm_all, gm_last = call(
        middle_kernel,
        [((3, 5, 3, 32, LANES), BF), ((2, 64, LANES), F32), ((64, LANES), BF), ((8, 32, LANES), BF), (half_rows, BF), ((2, 32, 1152), BF), ((32, 1152), BF)],
        name="middle",
    )(half_act, half_lo, half_hi, pull, mask, w2, up3)
    gm_lo, gm_hi = shifted(gm_last, "row", 1), shifted(gm_all, "row", -1)
    (g4,) = call(full_grad_kernel, [((112, 128), F32)], flops=2 * 432 * 32 * LANES * 64, name="full_grad")(cwin, mixed)
    core = ("col", 1)
    ewin, gh_first, kept, send = call(
        functools.partial(backward_kernel, core),
        [((3, 2, 3, 32, LANES), BF), ((32, 1152), BF), ((PACK, 128), F32), ((PACK // 2, 128), BF)],
        [pltpu.VMEM((3, 5, 3, 32, LANES), BF)],
        name="backward",
    )(gm, gm_lo, gm_hi, vwin, hwin, preh, preq, quarter, g4, mask, w3, up2)
    (part,) = call(functools.partial(fold_kernel, core), [((PACK // 2, 128), BF)], name="fold")(kept, swapped(send, 0, 1))
    gh_next = shifted(gh_first, "row", -1)
    near = (7 & (rows - 1), 2 & (cols - 1))
    size = 2 ** sum(bits.bit_count() for bits in near)
    share = PACK // 2 // size
    part = exchanged(part.reshape(size, share, 128), *near).reshape(size * share, 128)
    (part,) = call(functools.partial(sum_kernel, size, 1), [((share, 128), BF)], name="sum")(part)
    for steps in ((4,), (8, 16, 24)):
        if max(steps) < cols:
            part = tree_sum([part] + [swapped(part, 0, step) for step in steps]).astype(BF)
    (part,) = call(functools.partial(sum_kernel, 1, size), [((size * share, 128), BF)], name="copies")(part)
    part, gh_next = lax.optimization_barrier((part, gh_next))
    part = exchanged(part.reshape(size, share, 128), *near).reshape(PACK // 2, 128)
    (grad_volume,) = call(
        volume_kernel, [((16, QD, 16, 128), BF)], [pltpu.VMEM((256, 4 * LANES), BF), pltpu.VMEM((3, 3, 32, LANES), BF)], flops=2 * 256 * 1024 * 4000, name="volume"
    )(ewin, gh_next, cwin, up1, spread, order)
    part, grad_volume = lax.optimization_barrier((part, grad_volume))
    g1, g2, g3, g4 = call(
        functools.partial(finish_kernel, scale, core),
        [((27, 16, 32), F32), ((27, 32, 64), F32), ((27, 32, 64), F32), ((27, 16, 32), F32)],
        [pltpu.VMEM((PACK, 128), F32)],
        name="finish",
    )(part, swapped(part, 0, 1))
    return (
        grad_volume.reshape(volume.shape),
        from_tap(g1, True),
        from_tap(g2, True),
        from_tap(g3, False),
        from_tap(g4, False),
    )


def solution(mesh):
    return jax.shard_map(
        shards,
        mesh=mesh,
        in_specs=(P(None, None, "row", "col"), P(None, None, "row", "col"), P(), P(), P(), P()),
        out_specs=(P(None, None, "row", "col"), P(), P(), P(), P()),
        check_vma=False,
    )
```

```python
import functools
import math

import jax
import jax.numpy as jnp
from jax import lax
from jax.experimental import pallas as pl
from jax.experimental.pallas import tpu as pltpu
from jax.sharding import PartitionSpec as P

BF = jnp.bfloat16
F32 = jnp.float32

QD, QC, HALO = 8, 32, 2
SPAN = QC + 2 * HALO
LANES = 384
PACK = 1280
LIMIT = 24 * 1024 * 1024


def lane_of(d, c):
    return SPAN * d + c + HALO


def iota(shape, dim):
    return lax.broadcasted_iota(jnp.int32, shape, dim)


def ones_where(condition):
    return jnp.where(condition, 1.0, 0.0).astype(BF)


def lane_tables(spread_ref, place_ref):
    w, lane = iota((128, 256), 0), iota((128, 256), 1)
    for phase in range(4):
        apart = jnp.where((w & 3) == phase, lane - (w >> 2), -LANES)
        for d in range(QD):
            block = ones_where(apart == lane_of(d, 0) - (0 if d < 6 else 128))
            spread_ref[d * 128 : (d + 1) * 128, phase * 256 : (phase + 1) * 256] = block
    place_ref[...] = jnp.zeros(place_ref.shape, BF)
    slot, lane = iota((16, LANES), 0), iota((16, LANES), 1)
    for side in range(2):
        block = ones_where(lane == SPAN * (slot >> 1) + HALO + (slot & 1) + (QC if side else -2))
        for array in range(2):
            for phase in range(4):
                row = side * 128 + array * 64 + phase * 16
                place_ref[array, row : row + 16, phase * LANES : (phase + 1) * LANES] = block


def row_tables(rims_ref, order_ref):
    slot, row = iota((QD * 128, 128), 1), iota((QD * 128, 128), 0)
    column = (slot & 1) + jnp.where(slot >= 64, QC - 2, 0)
    rims_ref[...] = ones_where(row == ((slot >> 1) & 7) * 128 + 4 * column + ((slot >> 4) & 3))
    row, column = iota((256, 256), 0), iota((256, 256), 1)
    order_ref[...] = ones_where(column == (row & 15) * 16 + ((row >> 4) & 3) * 4 + (row >> 6))


def dot(a, b):
    return lax.dot_general(a, b, (((1,), (0,)), ((), ())), preferred_element_type=F32)


def dot_nt(a, b):
    return lax.dot_general(a, b, (((1,), (1,)), ((), ())), preferred_element_type=F32)


def sigmoid(t):
    return 1.0 / (1.0 + jnp.exp(-t))


def slope(t):
    s = sigmoid(t)
    return s * (1.0 + t * (1.0 - s))


def by_rows(x_ref, order_ref):
    wide = jnp.concatenate([x_ref[:, d].reshape(256, 128) for d in range(QD)], axis=1)
    return dot(order_ref[...], wide).astype(BF)


def to_lanes(rows, spread_ref):
    early = dot(rows[:, :768], spread_ref[0:768])
    late = dot(rows[:, 768:], spread_ref[768:1024])
    pieces = []
    for pc in range(4):
        low, high = pc * 256, pc * 256 + 128
        pieces += [early[:, low:high], early[:, high : low + 256] + late[:, low:high], late[:, high : low + 256]]
    return jnp.concatenate(pieces, axis=1)


def fetch(pairs, sems):
    copies = [pltpu.make_async_copy(source, target, sems.at[i]) for i, (source, target) in enumerate(pairs)]
    for copy in copies:
        copy.start()
    return copies


def edge_kernel(vol_ref, cot_ref, order_ref, vol_rows_ref, cot_rows_ref, main_ref, first_ref, last_ref, first_low_ref, last_low_ref, vol_here, cot_here, rims_ref, sems):
    copies = fetch(((vol_ref, vol_here), (cot_ref, cot_here)), sems)
    row_tables(rims_ref, order_ref)
    edges = []
    for i, (here, rows_ref) in enumerate(((vol_here, vol_rows_ref), (cot_here, cot_rows_ref))):
        copies[i].wait()
        rows = by_rows(here, order_ref)
        rows_ref[...] = rows
        main_ref[i * 64 : i * 64 + 64] = rows[192:256]
        edges.append(dot(rows, rims_ref[...]))
    first_ref[...] = jnp.concatenate([edge[:, :64] for edge in edges], axis=1).astype(BF)
    last_ref[...] = jnp.concatenate([edge[:, 64:] for edge in edges], axis=1).astype(BF)
    first_low_ref[...] = first_ref[192:256]
    last_low_ref[...] = last_ref[192:256]


def own_kernel(vol_rows_ref, cot_rows_ref, yv_ref, yc_ref, spread_ref, place_ref):
    lane_tables(spread_ref, place_ref)
    yv_ref[...] = to_lanes(vol_rows_ref[...], spread_ref).astype(BF)
    yc_ref[...] = to_lanes(cot_rows_ref[...], spread_ref).astype(BF)


def flag(condition):
    return jnp.where(condition, 1.0, 0.0).astype(F32)


def rims_of(left_ref, right_ref):
    left = left_ref[...].astype(F32) * flag(lax.axis_index("col") > 0)
    return jnp.concatenate([left.astype(BF), right_ref[...]], axis=1)


UP_TAP = {(0, 0): 1, (1, 0): 0, (1, 1): 2}
PAIRS = [(a, b, c) for a in range(2) for b in range(2) for c in range(2)]


def write_masks(mask_ref):
    lane = lax.broadcasted_iota(jnp.int32, (1, LANES), 1)
    c = lane
    for d in range(1, QD):
        c = jnp.where(lane >= d * SPAN, lane - d * SPAN, c)
    c = c - HALO
    inside = lane < QD * SPAN
    last_col = lax.axis_index("col") == lax.axis_size("col") - 1
    last_row = lax.axis_index("row") == lax.axis_size("row") - 1
    bound = jnp.where(last_col, QC, LANES)
    seen = jnp.where(inside & (c < bound), 1.0, 0.0).astype(F32)
    mask_ref[...] = jnp.zeros(mask_ref.shape, F32)
    mask_ref[0:1] = seen
    mask_ref[1:2] = seen * jnp.where(last_row, 0.0, 1.0)
    mask_ref[2:3] = jnp.where(inside & (c >= 0) & (c < QC), 1.0, 0.0).astype(F32)


def as_conv(ref, out_ref, back):
    small, large = ref.shape[1], ref.shape[2]
    if back:
        flat = jnp.concatenate([ref[26 - k] for k in range(27)], axis=0)
    else:
        flat = ref[...].reshape(27 * small, large)
    unit = ones_where(iota((large, large), 0) == iota((large, large), 1))
    out_ref[...] = dot_nt(unit, flat).astype(BF)


def as_up(ref, out_ref, back):
    small, large = ref.shape[1], ref.shape[2]
    out_ref[...] = jnp.zeros(out_ref.shape, BF)
    for p, (pr, pd, pc) in enumerate(PAIRS):
        for n, (nr, nd, nc) in enumerate(PAIRS):
            taps = [UP_TAP.get(key) for key in ((pd, nd), (pr, nr), (pc, nc))]
            if None in taps:
                continue
            j = taps[0] * 9 + taps[1] * 3 + taps[2]
            out_ref[p * small : (p + 1) * small, n * large : (n + 1) * large] = ref[26 - j if back else j]


def first_weights_kernel(wh_far, wbf_far, w1_ref, w4_ref, mask_ref, wh_ref, wbf_ref, sems):
    copies = fetch(((wh_far, wh_ref), (wbf_far, wbf_ref)), sems)
    write_masks(mask_ref)
    for copy in copies:
        copy.wait()
    as_conv(wh_ref, w1_ref, False)
    as_conv(wbf_ref, w4_ref, True)


def other_weights_kernel(wh_far, wq_far, wbh_far, after_ref, w2_ref, w3_ref, up1_ref, up2_ref, up3_ref, wh_ref, wq_ref, wbh_ref, sems):
    copies = fetch(((wh_far, wh_ref), (wq_far, wq_ref), (wbh_far, wbh_ref)), sems)
    for copy in copies:
        copy.wait()
    as_conv(wq_ref, w2_ref, False)
    as_conv(wbh_ref, w3_ref, True)
    as_up(wh_ref, up1_ref, True)
    as_up(wq_ref, up2_ref, True)
    as_up(wbh_ref, up3_ref, False)


def roll_up(x, steps):
    return pltpu.roll(x, steps % LANES, x.ndim - 1)


def fill_full(win_ref, y, base, count):
    pieces = [y[:, pc * LANES : (pc + 1) * LANES] for pc in range(4)]
    pieces = [roll_up(pieces[3], 1)] + pieces
    for c in range(5):
        piece = pieces[c].reshape(count, 4, 16, LANES)
        for pd in range(4):
            win_ref[1 + pd, base : base + count, c] = piece[:, pd].astype(BF)
        last = piece[:, 3].reshape(count * 16, LANES)
        win_ref[0, base : base + count, c] = roll_up(last, SPAN).reshape(count, 16, LANES).astype(BF)


def put_half(win_ref, row, pd, pc, value):
    win_ref[1 + pd, row, 1 + pc] = value.astype(BF)
    if pc == 1:
        left = roll_up(value, 1)
        win_ref[1 + pd, row, 0] = left.astype(BF)
    if pd == 1:
        above = roll_up(value, SPAN)
        win_ref[0, row, 1 + pc] = above.astype(BF)
        if pc == 1:
            win_ref[0, row, 0] = roll_up(left, SPAN).astype(BF)


def packed(values):
    tails = [pltpu.roll(value[:, 256:], 32 * i, 1) if i else value[:, 256:] for i, value in enumerate(values)]
    tail = (tails[0] + tails[1]) + (tails[2] + tails[3])
    return jnp.concatenate([value[:, :256] for value in values] + [tail], axis=1).astype(BF)


def unpacked(value, i):
    tail = value[:, 1024:]
    tail = pltpu.roll(tail, 128 - 32 * i, 1) if i else tail
    tail = jnp.where(iota(tail.shape, 1) < 32, tail, 0.0)
    return jnp.concatenate([value[:, 256 * i : 256 * i + 256], tail], axis=1)


def rounded(value):
    return value.astype(BF).astype(F32)


def neighbours(low, high):
    parts = []
    for value in (low, high):
        for nd in range(2):
            moved = roll_up(value, -SPAN) if nd else value
            parts.append(moved.astype(BF))
            parts.append(roll_up(moved, -1).astype(BF))
    return jnp.concatenate(parts, axis=0)


def half_kernel(main_ref, yv_ref, left_ref, right_ref, low_left_ref, low_right_ref, mask_ref, spread_ref, place_ref, w1_ref, vwin_ref, preh_ref, h_ref, h_all_ref, h_last_ref):
    seen = mask_ref[0:1]
    to_vol = place_ref[0]
    y = to_lanes(main_ref[0:64], spread_ref) + dot(rims_of(low_left_ref, low_right_ref), to_vol)
    fill_full(vwin_ref, y * flag(lax.axis_index("row") > 0), 0, 1)
    fill_full(vwin_ref, yv_ref[...].astype(F32) + dot(rims_of(left_ref, right_ref), to_vol), 1, 4)
    w1 = w1_ref[...]
    for pr, pd, pc in PAIRS:
        col = vwin_ref[2 * pd : 2 * pd + 3, 2 * pr : 2 * pr + 3, 2 * pc : 2 * pc + 3].reshape(432, LANES)
        pre = dot(w1, col)
        preh_ref[pr, pd, pc] = pre
        h_ref[pr, pd, pc] = (pre * sigmoid(pre) * seen).astype(BF)
    for pr in range(2):
        h_all_ref[pr] = packed([h_ref[pr, pd, pc].astype(F32) for pd in range(2) for pc in range(2)])
    h_last_ref[...] = h_all_ref[1]


def cotangent_kernel(main_ref, yc_ref, left_ref, right_ref, low_left_ref, low_right_ref, spread_ref, place_ref, w4_ref, cwin_ref, pull_ref):
    to_cot = place_ref[1]
    y = to_lanes(main_ref[64:128], spread_ref) + dot(rims_of(low_left_ref, low_right_ref), to_cot)
    fill_full(cwin_ref, y * flag(lax.axis_index("row") > 0), 0, 1)
    fill_full(cwin_ref, yc_ref[...].astype(F32) + dot(rims_of(left_ref, right_ref), to_cot), 1, 4)
    w4 = w4_ref[...]
    for p, (pr, pd, pc) in enumerate(PAIRS):
        col = cwin_ref[2 * pd : 2 * pd + 3, 2 * pr : 2 * pr + 3, 2 * pc : 2 * pc + 3].reshape(432, LANES)
        pull_ref[p] = dot(w4, col)


def middle_kernel(h_ref, hlo_ref, hhi_ref, pull_ref, mask_ref, w2_ref, up3_ref, hwin_ref, preq_ref, q_ref, m_ref, gm_ref, gm_all_ref, gm_last_ref):
    seen = mask_ref[0:1]
    seen_next = mask_ref[1:2]
    own = mask_ref[2:3]
    inner = flag(lax.axis_index("row") > 0)
    for pd in range(2):
        for pc in range(2):
            phase = 2 * pd + pc
            put_half(hwin_ref, 0, pd, pc, unpacked(hlo_ref[...].astype(F32), phase) * inner)
            for pr in range(2):
                put_half(hwin_ref, 1 + pr, pd, pc, h_ref[pr, pd, pc].astype(F32))
                put_half(hwin_ref, 3 + pr, pd, pc, unpacked(hhi_ref[pr].astype(F32), phase) * seen_next)
    quarters = []
    for qr in range(2):
        col = hwin_ref[:, 2 * qr : 2 * qr + 3].reshape(864, LANES)
        pre = dot(w2_ref[...], col)
        preq_ref[qr] = pre
        quarters.append(rounded(pre * sigmoid(pre)) * (seen_next if qr else seen))
    q_ref[...] = (quarters[0] * own).astype(BF)
    up = dot(up3_ref[...], neighbours(quarters[0], quarters[1]))
    for p, (pr, pd, pc) in enumerate(PAIRS):
        pre = up[p * 32 : p * 32 + 32] + h_ref[pr, pd, pc].astype(F32)
        m_ref[p] = (rounded(pre * sigmoid(pre)) * own).astype(BF)
        gm = rounded(pull_ref[p] * slope(pre)) * seen
        gm_ref[pr, pd, pc] = gm.astype(BF)
    for pr in range(2):
        gm_all_ref[pr] = packed([gm_ref[pr, pd, pc].astype(F32) for pd in range(2) for pc in range(2)])
    gm_last_ref[...] = gm_all_ref[1]


def full_grad_kernel(cwin_ref, m_ref, out_ref):
    total = None
    for p, (pr, pd, pc) in enumerate(PAIRS):
        col = cwin_ref[2 * pd : 2 * pd + 3, 2 * pr : 2 * pr + 3, 2 * pc : 2 * pc + 3].reshape(432, LANES)
        part = dot_nt(col, m_ref[p])
        total = part if total is None else total + part
    store_groups(out_ref, total, 0, 112, 32)


def store_groups(out_ref, total, base, rows, width):
    size = total.shape[0]
    for group in range(128 // width):
        low, high = group * rows, min((group + 1) * rows, size)
        out_ref[base : base + high - low, group * width : (group + 1) * width] = total[low:high]
        if high - low < rows:
            out_ref[base + high - low : base + rows, group * width : (group + 1) * width] = jnp.zeros((rows - high + low, width), F32)


def put_upper(win_ref, pd, pc, value):
    win_ref[pd, pc] = value.astype(BF)
    if pc == 0:
        right = roll_up(value, -1)
        win_ref[pd, 2] = right.astype(BF)
    if pd == 0:
        win_ref[2, pc] = roll_up(value, -SPAN).astype(BF)
        if pc == 0:
            win_ref[2, 2] = roll_up(right, -SPAN).astype(BF)


def backward_kernel(stage, gm_ref, gmlo_ref, gmhi_ref, vwin_ref, hwin_ref, preh_ref, preq_ref, q_ref, g4_ref, mask_ref, w3_ref, up2_ref, ewin_ref, gh_first_ref, pack_ref, send_ref, mwin_ref):
    seen = mask_ref[0:1]
    seen_next = mask_ref[1:2]
    own = mask_ref[2:3]
    inner = flag(lax.axis_index("row") > 0)
    for pd in range(2):
        for pc in range(2):
            phase = 2 * pd + pc
            put_half(mwin_ref, 0, pd, pc, unpacked(gmlo_ref[...].astype(F32), phase) * inner)
            for pr in range(2):
                put_half(mwin_ref, 1 + pr, pd, pc, gm_ref[pr, pd, pc].astype(F32))
                put_half(mwin_ref, 3 + pr, pd, pc, unpacked(gmhi_ref[pr].astype(F32), phase))
    quarters = []
    for qr in range(2):
        col = mwin_ref[:, 2 * qr : 2 * qr + 3].reshape(864, LANES)
        gq = rounded(dot(w3_ref[...], col) * slope(preq_ref[qr])) * (seen_next if qr else seen)
        quarters.append(gq)
        if qr == 0:
            store_groups(pack_ref, dot_nt(col, q_ref[...]), 672, 448, 64)
    up = dot(up2_ref[...], neighbours(quarters[0], quarters[1]))
    total = None
    first_row = []
    for p, (pr, pd, pc) in enumerate(PAIRS):
        conv = up[p * 32 : p * 32 + 32]
        gm = mwin_ref[1 + pd, 1 + pr, 1 + pc].astype(F32)
        gh = rounded((conv + gm) * slope(preh_ref[pr, pd, pc])) * seen
        put_upper(ewin_ref.at[:, pr], pd, pc, gh)
        if pr == 0:
            first_row.append(gh)
        col = vwin_ref[2 * pd : 2 * pd + 3, 2 * pr : 2 * pr + 3, 2 * pc : 2 * pc + 3].reshape(432, LANES)
        part = dot_nt(col, (gh * own).astype(BF))
        total = part if total is None else total + part
    gh_first_ref[...] = packed(first_row)
    store_groups(pack_ref, total, 0, 112, 32)
    pack_ref[112:224] = g4_ref[...]
    col = hwin_ref[:, 0:3].reshape(864, LANES)
    store_groups(pack_ref, dot_nt(col, (quarters[0] * own).astype(BF)), 224, 448, 64)
    pack_ref[1120:PACK] = jnp.zeros((PACK - 1120, 128), F32)
    send_ref[...] = half(pack_ref, stage, False)[...].astype(BF)


def volume_kernel(ewin_ref, next_ref, cwin_ref, up1_ref, spread_ref, order_ref, out_ref, z_ref, ext_ref):
    below = flag(lax.axis_index("row") < lax.axis_size("row") - 1)
    for pd in range(2):
        for pc in range(2):
            put_upper(ext_ref, pd, pc, unpacked(next_ref[...].astype(F32), 2 * pd + pc) * below)
    up1 = up1_ref[...]
    for pr, pd, pc in PAIRS:
        near = jnp.concatenate(
            [
                ewin_ref[pd + nd, pr + nr, pc + nc] if pr + nr < 2 else ext_ref[pd + nd, pc + nc]
                for nr, nd, nc in PAIRS
            ],
            axis=0,
        )
        up = dot(up1, near)
        for f, (fr, fd, fc) in enumerate(PAIRS):
            r, d, c = 2 * pr + fr, 2 * pd + fd, 2 * pc + fc
            value = up[f * 16 : f * 16 + 16] + cwin_ref[1 + d, 1 + r, 1 + c].astype(F32)
            z_ref[r * 64 + d * 16 : r * 64 + d * 16 + 16, c * LANES : (c + 1) * LANES] = value.astype(BF)
    early = jnp.concatenate([z_ref[:, c * LANES : c * LANES + 256] for c in range(4)], axis=1)
    late = jnp.concatenate([z_ref[:, c * LANES + 128 : (c + 1) * LANES] for c in range(4)], axis=1)
    wide = jnp.concatenate([dot_nt(early, spread_ref[0:768]), dot_nt(late, spread_ref[768:1024])], axis=1).astype(BF)
    wide = lax.dot_general(order_ref[...], wide, (((0,), (0,)), ((), ())), preferred_element_type=F32).astype(BF)
    for d in range(QD):
        out_ref[:, d] = wide[:, d * 128 : (d + 1) * 128].reshape(16, 16, 128)


def side_of(axis, step):
    return jnp.where((lax.axis_index(axis) & step) != 0, 1, 0)


def half(ref, stage, mine):
    count = ref.shape[0] // 2
    side = side_of(*stage)
    return ref.at[pl.ds(pl.multiple_of((side if mine else 1 - side) * count, 16), count)]


def fold_kernel(stage, kept_ref, got_ref, out_ref):
    out_ref[...] = (half(kept_ref, stage, True)[...] + got_ref[...].astype(F32)).astype(BF)


def sum_kernel(terms, copies, x_ref, out_ref):
    size = x_ref.shape[0] // terms
    total = jnp.sum(x_ref[...].astype(F32).reshape(terms, size, 128), axis=0, keepdims=True)
    out_ref[...] = jnp.broadcast_to(total, (copies, size, 128)).reshape(copies * size, 128).astype(BF)


def finish_kernel(scale, stage, own_ref, got_ref, g1_ref, g2_ref, g3_ref, g4_ref, full_ref):
    half(full_ref, stage, True)[...] = own_ref[...].astype(F32)
    half(full_ref, stage, False)[...] = got_ref[...].astype(F32)
    for ref, base, rows, width in ((g1_ref, 0, 112, 32), (g4_ref, 112, 112, 32), (g2_ref, 224, 448, 64), (g3_ref, 672, 448, 64)):
        small = ref.shape[1]
        taps = rows // small
        back = ref is g3_ref or ref is g4_ref
        for group in range(128 // width):
            count = min(taps, 27 - group * taps)
            block = full_ref[base : base + count * small, group * width : (group + 1) * width] * scale
            block = block.reshape(count, small, width)
            if back:
                for t in range(count):
                    ref[26 - group * taps - t] = block[t]
            else:
                ref[group * taps : group * taps + count] = block


def call(kernel, outs, scratch=(), flops=0, far=None, name=None):
    shapes = [jax.ShapeDtypeStruct(shape, dtype) for shape, dtype in outs]
    specs = {}
    if far:
        specs["in_specs"] = [pl.BlockSpec(memory_space=pltpu.HBM)] * far[0] + [pl.BlockSpec(memory_space=pltpu.VMEM)] * far[1]
    return pl.pallas_call(
        kernel,
        out_shape=shapes,
        scratch_shapes=list(scratch),
        **specs,
        compiler_params=pltpu.CompilerParams(vmem_limit_bytes=LIMIT),
        cost_estimate=pl.CostEstimate(flops=flops, bytes_accessed=4000000, transcendentals=0),
        name=name,
    )


def swapped(value, row_step, col_step):
    rows, cols = lax.axis_size("row"), lax.axis_size("col")
    pairs = [(r * cols + c, (r ^ row_step) * cols + (c ^ col_step)) for r in range(rows) for c in range(cols)]
    return lax.ppermute(value, ("row", "col"), pairs)


def shifted(value, axis, steps):
    count = lax.axis_size(axis)
    return lax.ppermute(value, axis, [(i, (i + steps) % count) for i in range(count)])


def tree_sum(terms):
    terms = [term.astype(F32) for term in terms]
    while len(terms) > 1:
        terms = [low + high for low, high in zip(terms[::2], terms[1::2])]
    return terms[0]


def diagonal(value, row_step, col_step):
    rows, cols = lax.axis_size("row"), lax.axis_size("col")
    pairs = [(r * cols + c, (r + row_step) % rows * cols + (c + col_step) % cols) for r in range(rows) for c in range(cols)]
    return lax.ppermute(value, ("row", "col"), pairs)


def exchanged(value, row_bits, col_bits):
    rows, cols = lax.axis_size("row"), lax.axis_size("col")
    if not row_bits and not col_bits:
        return value
    groups = {}
    for r in range(rows):
        for c in range(cols):
            groups.setdefault((r & ~row_bits, c & ~col_bits), []).append(r * cols + c)
    return lax.all_to_all(value, ("row", "col"), 0, 0, axis_index_groups=list(groups.values()), tiled=True)


def held(value):
    return pltpu.with_memory_space_constraint(value, pltpu.HBM)


def by_tap(weight, swap):
    order = (2, 3, 4, 1, 0) if swap else (2, 3, 4, 0, 1)
    moved = weight.transpose(order)
    return moved.reshape((27,) + moved.shape[3:])


def from_tap(grad, swap):
    cube = grad.reshape((3, 3, 3) + grad.shape[1:])
    return cube.transpose((4, 3, 0, 1, 2) if swap else (3, 4, 0, 1, 2))


def shards(volume, cotangent, w_half, w_quarter, w_back_half, w_back_full):
    rows, cols = lax.axis_size("row"), lax.axis_size("col")
    cells = volume.size // volume.shape[0] * rows * cols
    scale = 1.0 / math.sqrt(cells)
    vol = volume.reshape(16, QD, 16, 128)
    cot = cotangent.reshape(16, QD, 16, 128)
    order, vol_rows, cot_rows, main, first, last, first_low, last_low = call(
        edge_kernel,
        [((256, 256), BF), ((256, 1024), BF), ((256, 1024), BF), ((128, 1024), BF), ((256, 128), BF), ((256, 128), BF), ((64, 128), BF), ((64, 128), BF)],
        [pltpu.VMEM(vol.shape, BF), pltpu.VMEM(cot.shape, BF), pltpu.VMEM((QD * 128, 128), BF), pltpu.SemaphoreType.DMA((2,))],
        far=(2, 0),
        name="edge",
    )(held(vol), held(cot))
    main_lo = shifted(main, "row", 1)
    edges = [shifted(last, "col", 1), shifted(first, "col", -1), diagonal(last_low, 1, 1), diagonal(first_low, 1, -1)]
    yv, yc, spread, place = call(
        own_kernel,
        [((256, 4 * LANES), BF), ((256, 4 * LANES), BF), ((QD * 128, 1024), BF), ((2, 256, 4 * LANES), BF)],
        flops=2 * 256 * 1024 * 4000,
        name="own",
    )(vol_rows, cot_rows)
    wh, wq = held(by_tap(w_half, True)), held(by_tap(w_quarter, True))
    wbh, wbf = held(by_tap(w_back_half, False)), held(by_tap(w_back_full, False))
    w1, w4, mask = call(
        first_weights_kernel,
        [((32, 432), BF), ((32, 432), BF), ((8, LANES), F32)],
        [pltpu.VMEM(wh.shape, BF), pltpu.VMEM(wbf.shape, BF), pltpu.SemaphoreType.DMA((2,))],
        far=(2, 0),
        name="first_weights",
    )(wh, wbf)
    full_window, half_rows = (5, 5, 5, 16, LANES), (2, 2, 2, 32, LANES)
    vwin, preh, half_act, half_all, half_last = call(
        half_kernel,
        [(full_window, BF), (half_rows, F32), (half_rows, BF), ((2, 32, 1152), BF), ((32, 1152), BF)],
        name="half",
    )(main_lo, yv, *edges, mask, spread, place, w1)
    half_lo, half_hi = shifted(half_last, "row", 1), shifted(half_all, "row", -1)
    cwin, pull = call(
        cotangent_kernel, [(full_window, BF), ((8, 32, LANES), F32)], flops=2 * 432 * 32 * LANES * 64, name="cotangent"
    )(main_lo, yc, *edges, spread, place, w4)
    w2, w3, up1, up2, up3 = call(
        other_weights_kernel,
        [((64, 864), BF), ((64, 864), BF), ((128, 256), BF), ((256, 512), BF), ((256, 512), BF)],
        [pltpu.VMEM(weight.shape, BF) for weight in (wh, wq, wbh)] + [pltpu.SemaphoreType.DMA((3,))],
        far=(3, 1),
        name="other_weights",
    )(wh, wq, wbh, half_last)
    hwin, preq, quarter, mixed, gm, gm_all, gm_last = call(
        middle_kernel,
        [((3, 5, 3, 32, LANES), BF), ((2, 64, LANES), F32), ((64, LANES), BF), ((8, 32, LANES), BF), (half_rows, BF), ((2, 32, 1152), BF), ((32, 1152), BF)],
        name="middle",
    )(half_act, half_lo, half_hi, pull, mask, w2, up3)
    gm_lo, gm_hi = shifted(gm_last, "row", 1), shifted(gm_all, "row", -1)
    (g4,) = call(full_grad_kernel, [((112, 128), F32)], flops=2 * 432 * 32 * LANES * 64, name="full_grad")(cwin, mixed)
    core = ("col", 1)
    ewin, gh_first, kept, send = call(
        functools.partial(backward_kernel, core),
        [((3, 2, 3, 32, LANES), BF), ((32, 1152), BF), ((PACK, 128), F32), ((PACK // 2, 128), BF)],
        [pltpu.VMEM((3, 5, 3, 32, LANES), BF)],
        name="backward",
    )(gm, gm_lo, gm_hi, vwin, hwin, preh, preq, quarter, g4, mask, w3, up2)
    (part,) = call(functools.partial(fold_kernel, core), [((PACK // 2, 128), BF)], name="fold")(kept, swapped(send, 0, 1))
    gh_next = shifted(gh_first, "row", -1)
    near = (7 & (rows - 1), 2 & (cols - 1))
    size = 2 ** sum(bits.bit_count() for bits in near)
    share = PACK // 2 // size
    part = exchanged(part.reshape(size, share, 128), *near).reshape(size * share, 128)
    (part,) = call(functools.partial(sum_kernel, size, 1), [((share, 128), BF)], name="sum")(part)
    for steps in ((4,), (8, 16, 24)):
        if max(steps) < cols:
            part = tree_sum([part] + [swapped(part, 0, step) for step in steps]).astype(BF)
    (part,) = call(functools.partial(sum_kernel, 1, size), [((size * share, 128), BF)], name="copies")(part)
    part, gh_next = lax.optimization_barrier((part, gh_next))
    part = exchanged(part.reshape(size, share, 128), *near).reshape(PACK // 2, 128)
    (grad_volume,) = call(
        volume_kernel, [((16, QD, 16, 128), BF)], [pltpu.VMEM((256, 4 * LANES), BF), pltpu.VMEM((3, 3, 32, LANES), BF)], flops=2 * 256 * 1024 * 4000, name="volume"
    )(ewin, gh_next, cwin, up1, spread, order)
    part, grad_volume = lax.optimization_barrier((part, grad_volume))
    g1, g2, g3, g4 = call(
        functools.partial(finish_kernel, scale, core),
        [((27, 16, 32), F32), ((27, 32, 64), F32), ((27, 32, 64), F32), ((27, 16, 32), F32)],
        [pltpu.VMEM((PACK, 128), F32)],
        name="finish",
    )(part, swapped(part, 0, 1))
    return (
        grad_volume.reshape(volume.shape),
        from_tap(g1, True),
        from_tap(g2, True),
        from_tap(g3, False),
        from_tap(g4, False),
    )


def solution(mesh):
    return jax.shard_map(
        shards,
        mesh=mesh,
        in_specs=(P(None, None, "row", "col"), P(None, None, "row", "col"), P(), P(), P(), P()),
        out_specs=(P(None, None, "row", "col"), P(), P(), P(), P()),
        check_vma=False,
    )
```

```python
import functools
import math

import jax
import jax.numpy as jnp
from jax import lax
from jax.experimental import pallas as pl
from jax.experimental.pallas import tpu as pltpu
from jax.sharding import PartitionSpec as P

BF = jnp.bfloat16
F32 = jnp.float32

QD, QC, HALO = 8, 32, 2
SPAN = QC + 2 * HALO
LANES = 384
PACK = 1280
LIMIT = 24 * 1024 * 1024


def lane_of(d, c):
    return SPAN * d + c + HALO


def iota(shape, dim):
    return lax.broadcasted_iota(jnp.int32, shape, dim)


def ones_where(condition):
    return jnp.where(condition, 1.0, 0.0).astype(BF)


def lane_tables(spread_ref, place_ref):
    w, lane = iota((128, 256), 0), iota((128, 256), 1)
    for phase in range(4):
        apart = jnp.where((w & 3) == phase, lane - (w >> 2), -LANES)
        for d in range(QD):
            block = ones_where(apart == lane_of(d, 0) - (0 if d < 6 else 128))
            spread_ref[d * 128 : (d + 1) * 128, phase * 256 : (phase + 1) * 256] = block
    place_ref[...] = jnp.zeros(place_ref.shape, BF)
    slot, lane = iota((16, LANES), 0), iota((16, LANES), 1)
    for side in range(2):
        block = ones_where(lane == SPAN * (slot >> 1) + HALO + (slot & 1) + (QC if side else -2))
        for array in range(2):
            for phase in range(4):
                row = side * 128 + array * 64 + phase * 16
                place_ref[array, row : row + 16, phase * LANES : (phase + 1) * LANES] = block


def row_tables(rims_ref, order_ref):
    slot, row = iota((QD * 128, 128), 1), iota((QD * 128, 128), 0)
    column = (slot & 1) + jnp.where(slot >= 64, QC - 2, 0)
    rims_ref[...] = ones_where(row == ((slot >> 1) & 7) * 128 + 4 * column + ((slot >> 4) & 3))
    row, column = iota((256, 256), 0), iota((256, 256), 1)
    order_ref[...] = ones_where(column == (row & 15) * 16 + ((row >> 4) & 3) * 4 + (row >> 6))


def dot(a, b):
    return lax.dot_general(a, b, (((1,), (0,)), ((), ())), preferred_element_type=F32)


def dot_nt(a, b):
    return lax.dot_general(a, b, (((1,), (1,)), ((), ())), preferred_element_type=F32)


def sigmoid(t):
    return 1.0 / (1.0 + jnp.exp(-t))


def slope(t):
    s = sigmoid(t)
    return s * (1.0 + t * (1.0 - s))


def by_rows(x_ref, order_ref):
    wide = jnp.concatenate([x_ref[:, d].reshape(256, 128) for d in range(QD)], axis=1)
    return dot(order_ref[...], wide).astype(BF)


def to_lanes(rows, spread_ref):
    early = dot(rows[:, :768], spread_ref[0:768])
    late = dot(rows[:, 768:], spread_ref[768:1024])
    pieces = []
    for pc in range(4):
        low, high = pc * 256, pc * 256 + 128
        pieces += [early[:, low:high], early[:, high : low + 256] + late[:, low:high], late[:, high : low + 256]]
    return jnp.concatenate(pieces, axis=1)


def fetch(pairs, sems):
    copies = [pltpu.make_async_copy(source, target, sems.at[i]) for i, (source, target) in enumerate(pairs)]
    for copy in copies:
        copy.start()
    return copies


def edge_kernel(vol_ref, cot_ref, order_ref, vol_rows_ref, cot_rows_ref, main_ref, first_ref, last_ref, first_low_ref, last_low_ref, vol_here, cot_here, rims_ref, sems):
    copies = fetch(((vol_ref, vol_here), (cot_ref, cot_here)), sems)
    row_tables(rims_ref, order_ref)
    edges = []
    for i, (here, rows_ref) in enumerate(((vol_here, vol_rows_ref), (cot_here, cot_rows_ref))):
        copies[i].wait()
        rows = by_rows(here, order_ref)
        rows_ref[...] = rows
        main_ref[i * 64 : i * 64 + 64] = rows[192:256]
        edges.append(dot(rows, rims_ref[...]))
    first_ref[...] = jnp.concatenate([edge[:, :64] for edge in edges], axis=1).astype(BF)
    last_ref[...] = jnp.concatenate([edge[:, 64:] for edge in edges], axis=1).astype(BF)
    first_low_ref[...] = first_ref[192:256]
    last_low_ref[...] = last_ref[192:256]


def own_kernel(vol_rows_ref, cot_rows_ref, yv_ref, yc_ref, spread_ref, place_ref):
    lane_tables(spread_ref, place_ref)
    yv_ref[...] = to_lanes(vol_rows_ref[...], spread_ref).astype(BF)
    yc_ref[...] = to_lanes(cot_rows_ref[...], spread_ref).astype(BF)


def flag(condition):
    return jnp.where(condition, 1.0, 0.0).astype(F32)


def rims_of(left_ref, right_ref):
    left = left_ref[...].astype(F32) * flag(lax.axis_index("col") > 0)
    return jnp.concatenate([left.astype(BF), right_ref[...]], axis=1)


UP_TAP = {(0, 0): 1, (1, 0): 0, (1, 1): 2}
PAIRS = [(a, b, c) for a in range(2) for b in range(2) for c in range(2)]


def write_masks(mask_ref):
    lane = lax.broadcasted_iota(jnp.int32, (1, LANES), 1)
    c = lane
    for d in range(1, QD):
        c = jnp.where(lane >= d * SPAN, lane - d * SPAN, c)
    c = c - HALO
    inside = lane < QD * SPAN
    last_col = lax.axis_index("col") == lax.axis_size("col") - 1
    last_row = lax.axis_index("row") == lax.axis_size("row") - 1
    bound = jnp.where(last_col, QC, LANES)
    seen = jnp.where(inside & (c < bound), 1.0, 0.0).astype(F32)
    mask_ref[...] = jnp.zeros(mask_ref.shape, F32)
    mask_ref[0:1] = seen
    mask_ref[1:2] = seen * jnp.where(last_row, 0.0, 1.0)
    mask_ref[2:3] = jnp.where(inside & (c >= 0) & (c < QC), 1.0, 0.0).astype(F32)


def as_conv(ref, out_ref, back):
    small, large = ref.shape[1], ref.shape[2]
    if back:
        flat = jnp.concatenate([ref[26 - k] for k in range(27)], axis=0)
    else:
        flat = ref[...].reshape(27 * small, large)
    unit = ones_where(iota((large, large), 0) == iota((large, large), 1))
    out_ref[...] = dot_nt(unit, flat).astype(BF)


def as_up(ref, out_ref, back):
    small, large = ref.shape[1], ref.shape[2]
    out_ref[...] = jnp.zeros(out_ref.shape, BF)
    for p, (pr, pd, pc) in enumerate(PAIRS):
        for n, (nr, nd, nc) in enumerate(PAIRS):
            taps = [UP_TAP.get(key) for key in ((pd, nd), (pr, nr), (pc, nc))]
            if None in taps:
                continue
            j = taps[0] * 9 + taps[1] * 3 + taps[2]
            out_ref[p * small : (p + 1) * small, n * large : (n + 1) * large] = ref[26 - j if back else j]


def first_weights_kernel(wh_far, wbf_far, w1_ref, w4_ref, mask_ref, wh_ref, wbf_ref, sems):
    copies = fetch(((wh_far, wh_ref), (wbf_far, wbf_ref)), sems)
    write_masks(mask_ref)
    for copy in copies:
        copy.wait()
    as_conv(wh_ref, w1_ref, False)
    as_conv(wbf_ref, w4_ref, True)


def other_weights_kernel(wh_far, wq_far, wbh_far, after_ref, w2_ref, w3_ref, up1_ref, up2_ref, up3_ref, wh_ref, wq_ref, wbh_ref, sems):
    copies = fetch(((wh_far, wh_ref), (wq_far, wq_ref), (wbh_far, wbh_ref)), sems)
    for copy in copies:
        copy.wait()
    as_conv(wq_ref, w2_ref, False)
    as_conv(wbh_ref, w3_ref, True)
    as_up(wh_ref, up1_ref, True)
    as_up(wq_ref, up2_ref, True)
    as_up(wbh_ref, up3_ref, False)


def roll_up(x, steps):
    return pltpu.roll(x, steps % LANES, x.ndim - 1)


def fill_full(win_ref, y, base, count):
    pieces = [y[:, pc * LANES : (pc + 1) * LANES] for pc in range(4)]
    pieces = [roll_up(pieces[3], 1)] + pieces
    for c in range(5):
        piece = pieces[c].reshape(count, 4, 16, LANES)
        for pd in range(4):
            win_ref[1 + pd, base : base + count, c] = piece[:, pd].astype(BF)
        last = piece[:, 3].reshape(count * 16, LANES)
        win_ref[0, base : base + count, c] = roll_up(last, SPAN).reshape(count, 16, LANES).astype(BF)


def put_half(win_ref, row, pd, pc, value):
    win_ref[1 + pd, row, 1 + pc] = value.astype(BF)
    if pc == 1:
        left = roll_up(value, 1)
        win_ref[1 + pd, row, 0] = left.astype(BF)
    if pd == 1:
        above = roll_up(value, SPAN)
        win_ref[0, row, 1 + pc] = above.astype(BF)
        if pc == 1:
            win_ref[0, row, 0] = roll_up(left, SPAN).astype(BF)


def packed(values):
    tails = [pltpu.roll(value[:, 256:], 32 * i, 1) if i else value[:, 256:] for i, value in enumerate(values)]
    tail = (tails[0] + tails[1]) + (tails[2] + tails[3])
    return jnp.concatenate([value[:, :256] for value in values] + [tail], axis=1).astype(BF)


def unpacked(value, i):
    tail = value[:, 1024:]
    tail = pltpu.roll(tail, 128 - 32 * i, 1) if i else tail
    tail = jnp.where(iota(tail.shape, 1) < 32, tail, 0.0)
    return jnp.concatenate([value[:, 256 * i : 256 * i + 256], tail], axis=1)


def rounded(value):
    return value.astype(BF).astype(F32)


def neighbours(low, high):
    parts = []
    for value in (low, high):
        for nd in range(2):
            moved = roll_up(value, -SPAN) if nd else value
            parts.append(moved.astype(BF))
            parts.append(roll_up(moved, -1).astype(BF))
    return jnp.concatenate(parts, axis=0)


def half_kernel(main_ref, yv_ref, left_ref, right_ref, low_left_ref, low_right_ref, mask_ref, spread_ref, place_ref, w1_ref, vwin_ref, preh_ref, h_ref, h_all_ref, h_last_ref):
    seen = mask_ref[0:1]
    to_vol = place_ref[0]
    y = to_lanes(main_ref[0:64], spread_ref) + dot(rims_of(low_left_ref, low_right_ref), to_vol)
    fill_full(vwin_ref, y * flag(lax.axis_index("row") > 0), 0, 1)
    fill_full(vwin_ref, yv_ref[...].astype(F32) + dot(rims_of(left_ref, right_ref), to_vol), 1, 4)
    w1 = w1_ref[...]
    for pr, pd, pc in PAIRS:
        col = vwin_ref[2 * pd : 2 * pd + 3, 2 * pr : 2 * pr + 3, 2 * pc : 2 * pc + 3].reshape(432, LANES)
        pre = dot(w1, col)
        preh_ref[pr, pd, pc] = pre
        h_ref[pr, pd, pc] = (pre * sigmoid(pre) * seen).astype(BF)
    for pr in range(2):
        h_all_ref[pr] = packed([h_ref[pr, pd, pc].astype(F32) for pd in range(2) for pc in range(2)])
    h_last_ref[...] = h_all_ref[1]


def cotangent_kernel(main_ref, yc_ref, left_ref, right_ref, low_left_ref, low_right_ref, spread_ref, place_ref, w4_ref, cwin_ref, pull_ref):
    to_cot = place_ref[1]
    y = to_lanes(main_ref[64:128], spread_ref) + dot(rims_of(low_left_ref, low_right_ref), to_cot)
    fill_full(cwin_ref, y * flag(lax.axis_index("row") > 0), 0, 1)
    fill_full(cwin_ref, yc_ref[...].astype(F32) + dot(rims_of(left_ref, right_ref), to_cot), 1, 4)
    w4 = w4_ref[...]
    for p, (pr, pd, pc) in enumerate(PAIRS):
        col = cwin_ref[2 * pd : 2 * pd + 3, 2 * pr : 2 * pr + 3, 2 * pc : 2 * pc + 3].reshape(432, LANES)
        pull_ref[p] = dot(w4, col)


def middle_kernel(h_ref, hlo_ref, hhi_ref, pull_ref, mask_ref, w2_ref, up3_ref, hwin_ref, preq_ref, q_ref, m_ref, gm_ref, gm_all_ref, gm_last_ref):
    seen = mask_ref[0:1]
    seen_next = mask_ref[1:2]
    own = mask_ref[2:3]
    inner = flag(lax.axis_index("row") > 0)
    for pd in range(2):
        for pc in range(2):
            phase = 2 * pd + pc
            put_half(hwin_ref, 0, pd, pc, unpacked(hlo_ref[...].astype(F32), phase) * inner)
            for pr in range(2):
                put_half(hwin_ref, 1 + pr, pd, pc, h_ref[pr, pd, pc].astype(F32))
                put_half(hwin_ref, 3 + pr, pd, pc, unpacked(hhi_ref[pr].astype(F32), phase) * seen_next)
    quarters = []
    for qr in range(2):
        col = hwin_ref[:, 2 * qr : 2 * qr + 3].reshape(864, LANES)
        pre = dot(w2_ref[...], col)
        preq_ref[qr] = pre
        quarters.append(rounded(pre * sigmoid(pre)) * (seen_next if qr else seen))
    q_ref[...] = (quarters[0] * own).astype(BF)
    up = dot(up3_ref[...], neighbours(quarters[0], quarters[1]))
    for p, (pr, pd, pc) in enumerate(PAIRS):
        pre = up[p * 32 : p * 32 + 32] + h_ref[pr, pd, pc].astype(F32)
        m_ref[p] = (rounded(pre * sigmoid(pre)) * own).astype(BF)
        gm = rounded(pull_ref[p] * slope(pre)) * seen
        gm_ref[pr, pd, pc] = gm.astype(BF)
    for pr in range(2):
        gm_all_ref[pr] = packed([gm_ref[pr, pd, pc].astype(F32) for pd in range(2) for pc in range(2)])
    gm_last_ref[...] = gm_all_ref[1]


def full_grad_kernel(cwin_ref, m_ref, out_ref):
    total = None
    for p, (pr, pd, pc) in enumerate(PAIRS):
        col = cwin_ref[2 * pd : 2 * pd + 3, 2 * pr : 2 * pr + 3, 2 * pc : 2 * pc + 3].reshape(432, LANES)
        part = dot_nt(col, m_ref[p])
        total = part if total is None else total + part
    store_groups(out_ref, total, 0, 112, 32)


def store_groups(out_ref, total, base, rows, width):
    size = total.shape[0]
    for group in range(128 // width):
        low, high = group * rows, min((group + 1) * rows, size)
        out_ref[base : base + high - low, group * width : (group + 1) * width] = total[low:high]
        if high - low < rows:
            out_ref[base + high - low : base + rows, group * width : (group + 1) * width] = jnp.zeros((rows - high + low, width), F32)


def put_upper(win_ref, pd, pc, value):
    win_ref[pd, pc] = value.astype(BF)
    if pc == 0:
        right = roll_up(value, -1)
        win_ref[pd, 2] = right.astype(BF)
    if pd == 0:
        win_ref[2, pc] = roll_up(value, -SPAN).astype(BF)
        if pc == 0:
            win_ref[2, 2] = roll_up(right, -SPAN).astype(BF)


def backward_kernel(stage, gm_ref, gmlo_ref, gmhi_ref, vwin_ref, hwin_ref, preh_ref, preq_ref, q_ref, g4_ref, mask_ref, w3_ref, up2_ref, ewin_ref, gh_first_ref, pack_ref, send_ref, mwin_ref):
    seen = mask_ref[0:1]
    seen_next = mask_ref[1:2]
    own = mask_ref[2:3]
    inner = flag(lax.axis_index("row") > 0)
    for pd in range(2):
        for pc in range(2):
            phase = 2 * pd + pc
            put_half(mwin_ref, 0, pd, pc, unpacked(gmlo_ref[...].astype(F32), phase) * inner)
            for pr in range(2):
                put_half(mwin_ref, 1 + pr, pd, pc, gm_ref[pr, pd, pc].astype(F32))
                put_half(mwin_ref, 3 + pr, pd, pc, unpacked(gmhi_ref[pr].astype(F32), phase))
    quarters = []
    for qr in range(2):
        col = mwin_ref[:, 2 * qr : 2 * qr + 3].reshape(864, LANES)
        gq = rounded(dot(w3_ref[...], col) * slope(preq_ref[qr])) * (seen_next if qr else seen)
        quarters.append(gq)
        if qr == 0:
            store_groups(pack_ref, dot_nt(col, q_ref[...]), 672, 448, 64)
    up = dot(up2_ref[...], neighbours(quarters[0], quarters[1]))
    total = None
    first_row = []
    for p, (pr, pd, pc) in enumerate(PAIRS):
        conv = up[p * 32 : p * 32 + 32]
        gm = mwin_ref[1 + pd, 1 + pr, 1 + pc].astype(F32)
        gh = rounded((conv + gm) * slope(preh_ref[pr, pd, pc])) * seen
        put_upper(ewin_ref.at[:, pr], pd, pc, gh)
        if pr == 0:
            first_row.append(gh)
        col = vwin_ref[2 * pd : 2 * pd + 3, 2 * pr : 2 * pr + 3, 2 * pc : 2 * pc + 3].reshape(432, LANES)
        part = dot_nt(col, (gh * own).astype(BF))
        total = part if total is None else total + part
    gh_first_ref[...] = packed(first_row)
    store_groups(pack_ref, total, 0, 112, 32)
    pack_ref[112:224] = g4_ref[...]
    col = hwin_ref[:, 0:3].reshape(864, LANES)
    store_groups(pack_ref, dot_nt(col, (quarters[0] * own).astype(BF)), 224, 448, 64)
    pack_ref[1120:PACK] = jnp.zeros((PACK - 1120, 128), F32)
    send_ref[...] = half(pack_ref, stage, False)[...].astype(BF)


def volume_kernel(ewin_ref, next_ref, cwin_ref, up1_ref, spread_ref, order_ref, out_ref, z_ref, ext_ref):
    below = flag(lax.axis_index("row") < lax.axis_size("row") - 1)
    for pd in range(2):
        for pc in range(2):
            put_upper(ext_ref, pd, pc, unpacked(next_ref[...].astype(F32), 2 * pd + pc) * below)
    up1 = up1_ref[...]
    for pr, pd, pc in PAIRS:
        near = jnp.concatenate(
            [
                ewin_ref[pd + nd, pr + nr, pc + nc] if pr + nr < 2 else ext_ref[pd + nd, pc + nc]
                for nr, nd, nc in PAIRS
            ],
            axis=0,
        )
        up = dot(up1, near)
        for f, (fr, fd, fc) in enumerate(PAIRS):
            r, d, c = 2 * pr + fr, 2 * pd + fd, 2 * pc + fc
            value = up[f * 16 : f * 16 + 16] + cwin_ref[1 + d, 1 + r, 1 + c].astype(F32)
            z_ref[r * 64 + d * 16 : r * 64 + d * 16 + 16, c * LANES : (c + 1) * LANES] = value.astype(BF)
    early = jnp.concatenate([z_ref[:, c * LANES : c * LANES + 256] for c in range(4)], axis=1)
    late = jnp.concatenate([z_ref[:, c * LANES + 128 : (c + 1) * LANES] for c in range(4)], axis=1)
    wide = jnp.concatenate([dot_nt(early, spread_ref[0:768]), dot_nt(late, spread_ref[768:1024])], axis=1).astype(BF)
    wide = lax.dot_general(order_ref[...], wide, (((0,), (0,)), ((), ())), preferred_element_type=F32).astype(BF)
    for d in range(QD):
        out_ref[:, d] = wide[:, d * 128 : (d + 1) * 128].reshape(16, 16, 128)


def side_of(axis, step):
    return jnp.where((lax.axis_index(axis) & step) != 0, 1, 0)


def half(ref, stage, mine):
    count = ref.shape[0] // 2
    side = side_of(*stage)
    return ref.at[pl.ds(pl.multiple_of((side if mine else 1 - side) * count, 16), count)]


def fold_kernel(stage, kept_ref, got_ref, out_ref):
    out_ref[...] = (half(kept_ref, stage, True)[...] + got_ref[...].astype(F32)).astype(BF)


def sum_kernel(terms, copies, x_ref, out_ref):
    size = x_ref.shape[0] // terms
    total = jnp.sum(x_ref[...].astype(F32).reshape(terms, size, 128), axis=0, keepdims=True)
    out_ref[...] = jnp.broadcast_to(total, (copies, size, 128)).reshape(copies * size, 128).astype(BF)


def finish_kernel(scale, stage, own_ref, got_ref, g1_ref, g2_ref, g3_ref, g4_ref, full_ref):
    half(full_ref, stage, True)[...] = own_ref[...].astype(F32)
    half(full_ref, stage, False)[...] = got_ref[...].astype(F32)
    for ref, base, rows, width in ((g1_ref, 0, 112, 32), (g4_ref, 112, 112, 32), (g2_ref, 224, 448, 64), (g3_ref, 672, 448, 64)):
        small = ref.shape[1]
        taps = rows // small
        back = ref is g3_ref or ref is g4_ref
        for group in range(128 // width):
            count = min(taps, 27 - group * taps)
            block = full_ref[base : base + count * small, group * width : (group + 1) * width] * scale
            block = block.reshape(count, small, width)
            if back:
                for t in range(count):
                    ref[26 - group * taps - t] = block[t]
            else:
                ref[group * taps : group * taps + count] = block


def call(kernel, outs, scratch=(), flops=0, far=None, name=None):
    shapes = [jax.ShapeDtypeStruct(shape, dtype) for shape, dtype in outs]
    specs = {}
    if far:
        specs["in_specs"] = [pl.BlockSpec(memory_space=pltpu.HBM)] * far[0] + [pl.BlockSpec(memory_space=pltpu.VMEM)] * far[1]
    return pl.pallas_call(
        kernel,
        out_shape=shapes,
        scratch_shapes=list(scratch),
        **specs,
        compiler_params=pltpu.CompilerParams(vmem_limit_bytes=LIMIT),
        cost_estimate=pl.CostEstimate(flops=flops, bytes_accessed=4000000, transcendentals=0),
        name=name,
    )


def swapped(value, row_step, col_step):
    rows, cols = lax.axis_size("row"), lax.axis_size("col")
    pairs = [(r * cols + c, (r ^ row_step) * cols + (c ^ col_step)) for r in range(rows) for c in range(cols)]
    return lax.ppermute(value, ("row", "col"), pairs)


def shifted(value, axis, steps):
    count = lax.axis_size(axis)
    return lax.ppermute(value, axis, [(i, (i + steps) % count) for i in range(count)])


def diagonal(value, row_step, col_step):
    rows, cols = lax.axis_size("row"), lax.axis_size("col")
    pairs = [(r * cols + c, (r + row_step) % rows * cols + (c + col_step) % cols) for r in range(rows) for c in range(cols)]
    return lax.ppermute(value, ("row", "col"), pairs)


def exchanged(value, row_bits, col_bits):
    rows, cols = lax.axis_size("row"), lax.axis_size("col")
    if not row_bits and not col_bits:
        return value
    groups = {}
    for r in range(rows):
        for c in range(cols):
            groups.setdefault((r & ~row_bits, c & ~col_bits), []).append(r * cols + c)
    return lax.all_to_all(value, ("row", "col"), 0, 0, axis_index_groups=list(groups.values()), tiled=True)


def held(value):
    return pltpu.with_memory_space_constraint(value, pltpu.HBM)


def by_tap(weight, swap):
    order = (2, 3, 4, 1, 0) if swap else (2, 3, 4, 0, 1)
    moved = weight.transpose(order)
    return moved.reshape((27,) + moved.shape[3:])


def from_tap(grad, swap):
    cube = grad.reshape((3, 3, 3) + grad.shape[1:])
    return cube.transpose((4, 3, 0, 1, 2) if swap else (3, 4, 0, 1, 2))


def shards(volume, cotangent, w_half, w_quarter, w_back_half, w_back_full):
    rows, cols = lax.axis_size("row"), lax.axis_size("col")
    cells = volume.size // volume.shape[0] * rows * cols
    scale = 1.0 / math.sqrt(cells)
    vol = volume.reshape(16, QD, 16, 128)
    cot = cotangent.reshape(16, QD, 16, 128)
    order, vol_rows, cot_rows, main, first, last, first_low, last_low = call(
        edge_kernel,
        [((256, 256), BF), ((256, 1024), BF), ((256, 1024), BF), ((128, 1024), BF), ((256, 128), BF), ((256, 128), BF), ((64, 128), BF), ((64, 128), BF)],
        [pltpu.VMEM(vol.shape, BF), pltpu.VMEM(cot.shape, BF), pltpu.VMEM((QD * 128, 128), BF), pltpu.SemaphoreType.DMA((2,))],
        far=(2, 0),
        name="edge",
    )(held(vol), held(cot))
    main_lo = shifted(main, "row", 1)
    edges = [shifted(last, "col", 1), shifted(first, "col", -1), diagonal(last_low, 1, 1), diagonal(first_low, 1, -1)]
    yv, yc, spread, place = call(
        own_kernel,
        [((256, 4 * LANES), BF), ((256, 4 * LANES), BF), ((QD * 128, 1024), BF), ((2, 256, 4 * LANES), BF)],
        flops=2 * 256 * 1024 * 4000,
        name="own",
    )(vol_rows, cot_rows)
    wh, wq = held(by_tap(w_half, True)), held(by_tap(w_quarter, True))
    wbh, wbf = held(by_tap(w_back_half, False)), held(by_tap(w_back_full, False))
    w1, w4, mask = call(
        first_weights_kernel,
        [((32, 432), BF), ((32, 432), BF), ((8, LANES), F32)],
        [pltpu.VMEM(wh.shape, BF), pltpu.VMEM(wbf.shape, BF), pltpu.SemaphoreType.DMA((2,))],
        far=(2, 0),
        name="first_weights",
    )(wh, wbf)
    full_window, half_rows = (5, 5, 5, 16, LANES), (2, 2, 2, 32, LANES)
    vwin, preh, half_act, half_all, half_last = call(
        half_kernel,
        [(full_window, BF), (half_rows, F32), (half_rows, BF), ((2, 32, 1152), BF), ((32, 1152), BF)],
        name="half",
    )(main_lo, yv, *edges, mask, spread, place, w1)
    half_lo, half_hi = shifted(half_last, "row", 1), shifted(half_all, "row", -1)
    cwin, pull = call(
        cotangent_kernel, [(full_window, BF), ((8, 32, LANES), F32)], flops=2 * 432 * 32 * LANES * 64, name="cotangent"
    )(main_lo, yc, *edges, spread, place, w4)
    w2, w3, up1, up2, up3 = call(
        other_weights_kernel,
        [((64, 864), BF), ((64, 864), BF), ((128, 256), BF), ((256, 512), BF), ((256, 512), BF)],
        [pltpu.VMEM(weight.shape, BF) for weight in (wh, wq, wbh)] + [pltpu.SemaphoreType.DMA((3,))],
        far=(3, 1),
        name="other_weights",
    )(wh, wq, wbh, half_last)
    hwin, preq, quarter, mixed, gm, gm_all, gm_last = call(
        middle_kernel,
        [((3, 5, 3, 32, LANES), BF), ((2, 64, LANES), F32), ((64, LANES), BF), ((8, 32, LANES), BF), (half_rows, BF), ((2, 32, 1152), BF), ((32, 1152), BF)],
        name="middle",
    )(half_act, half_lo, half_hi, pull, mask, w2, up3)
    gm_lo, gm_hi = shifted(gm_last, "row", 1), shifted(gm_all, "row", -1)
    (g4,) = call(full_grad_kernel, [((112, 128), F32)], flops=2 * 432 * 32 * LANES * 64, name="full_grad")(cwin, mixed)
    core = ("col", 1)
    ewin, gh_first, kept, send = call(
        functools.partial(backward_kernel, core),
        [((3, 2, 3, 32, LANES), BF), ((32, 1152), BF), ((PACK, 128), F32), ((PACK // 2, 128), BF)],
        [pltpu.VMEM((3, 5, 3, 32, LANES), BF)],
        name="backward",
    )(gm, gm_lo, gm_hi, vwin, hwin, preh, preq, quarter, g4, mask, w3, up2)
    (part,) = call(functools.partial(fold_kernel, core), [((PACK // 2, 128), BF)], name="fold")(kept, swapped(send, 0, 1))
    gh_next = shifted(gh_first, "row", -1)
    along = [(7 & (rows - 1), 2 & (cols - 1)), (0, 28 & (cols - 1))]
    sizes = [2 ** (r.bit_count() + c.bit_count()) for r, c in along]
    share = PACK // 2 // sizes[0]
    for bits, size, later in zip(along, sizes, sizes[::-1]):
        part = exchanged(part.reshape(size, share, 128), *bits).reshape(size * share, 128)
        (part,) = call(functools.partial(sum_kernel, size, later), [((later * share, 128), BF)], name="sum")(part)
    part, gh_next = lax.optimization_barrier((part, gh_next))
    part = exchanged(part.reshape(sizes[0], share, 128), *along[0]).reshape(PACK // 2, 128)
    (grad_volume,) = call(
        volume_kernel, [((16, QD, 16, 128), BF)], [pltpu.VMEM((256, 4 * LANES), BF), pltpu.VMEM((3, 3, 32, LANES), BF)], flops=2 * 256 * 1024 * 4000, name="volume"
    )(ewin, gh_next, cwin, up1, spread, order)
    part, grad_volume = lax.optimization_barrier((part, grad_volume))
    g1, g2, g3, g4 = call(
        functools.partial(finish_kernel, scale, core),
        [((27, 16, 32), F32), ((27, 32, 64), F32), ((27, 32, 64), F32), ((27, 16, 32), F32)],
        [pltpu.VMEM((PACK, 128), F32)],
        name="finish",
    )(part, swapped(part, 0, 1))
    return (
        grad_volume.reshape(volume.shape),
        from_tap(g1, True),
        from_tap(g2, True),
        from_tap(g3, False),
        from_tap(g4, False),
    )


def solution(mesh):
    return jax.shard_map(
        shards,
        mesh=mesh,
        in_specs=(P(None, None, "row", "col"), P(None, None, "row", "col"), P(), P(), P(), P()),
        out_specs=(P(None, None, "row", "col"), P(), P(), P(), P()),
        check_vma=False,
    )
```
